512 devices in a mesh: section: 8 (over z_hi, core), dp: 64 (over y, x, z_lo).
Axes of the slice: x: 4, y: 4, z: 16 (z_hi: 4, z_lo: 4; z = z_hi * 4 + z_lo), core: 2. Of those that a mesh axis runs over, the one named last changes fastest.
Arguments:
- encoder_embed: bfloat16 [128, 64, 2048], P('dp'), may hold values from -6 to 6
- decoder_embed: bfloat16 [128, 64, 2048], P('dp'), may hold values from -6 to 6
- section_weights: bfloat16 [8, 2, 2048, 1024], P('section', None, 'dp'), may hold values from -2 to 2
- norm_gains: float32 [5, 2048], replicated, may hold values from 0.1 to 1.9
- input_lengths: int32 [128], P('dp'), may hold values from 16 to 64
- target_lengths: int32 [128], P('dp'), may hold values from 16 to 64
Outputs:
- section_out: bfloat16 [8, 128, 64, 2048], P('section', 'dp')
The draws below stay inside these ranges and needn't reach their ends.
All inputs are finite; a program needn't handle non-finite values.
Results may differ from the reference program's by a relative error of at most 0.039.
Values may be sent and summed in bfloat16 or wider, within the bound.
No kernel may reach another device: no remote copies, remote signals or barrier semaphores. Data moves between devices by JAX's collectives and lax.ppermute only.
A program may use at most 64 MiB of HBM per device.

```python
import jax
import jax.numpy as jnp
from jax import lax

D = 2048
HEADS = 8
HEAD_DIM = 128
LEN = 64
DOCS = 128
ENC_LAYERS = 2
SUBLAYERS = 4
BLOCKS = 8
N_SECTION = 8


def draw_section_weights(key, part):
    key = jax.random.fold_in(key, 11)
    inner_width = HEADS * HEAD_DIM
    base = jnp.clip(jax.random.normal(key, (BLOCKS, 2, D, inner_width), jnp.float32), -4.5, 4.5)
    block_ids = jnp.arange(BLOCKS)[:, None, None, None]
    slot_ids = jnp.arange(2)[None, :, None, None]
    is_front = block_ids % 2 == 0
    front_scale = 1.4 * D ** (-0.5)
    value_scale = D ** (-0.5)
    out_scale = 2.0 * inner_width ** (-0.5)
    scale = jnp.where(is_front, front_scale, jnp.where(slot_ids == 0, value_scale, out_scale))
    weights = base * scale
    return weights.astype(jnp.bfloat16)


def plant(array, stream_key, least, high):
    longest = array.shape.index(max(array.shape))
    spots = []
    for shift in (0, 1):
        where = [jax.random.randint(jax.random.fold_in(stream_key, axis), (), 0, length) for axis, length in enumerate(array.shape)]
        where[longest] = (where[longest] + shift) % array.shape[longest]
        spots.append(tuple(where))
    return array.at[spots[0]].set(least).at[spots[1]].set(high)


def block_scale(stream_key, extent, pieces, low, high):
    def one(axis_at, blocks):
        draws = jax.random.uniform(jax.random.fold_in(jax.random.fold_in(stream_key, 6), axis_at), (blocks,), jnp.float32, low / len(pieces), high / len(pieces))
        return jnp.repeat(jnp.exp(draws), extent[axis_at] // blocks).reshape((-1,) + (1,) * (len(extent) - axis_at - 1))

    level = one(*pieces[0])
    for cut in pieces[1:]:
        level = level * one(*cut)
    return level


def normal_values(key, shape, width, most, pieces=(), held_as=jnp.bfloat16):
    entries = width * jax.random.normal(key, shape, jnp.float32)
    if pieces:
        entries = entries * block_scale(key, shape, pieces, -0.22, 0.18)
    return jnp.clip(entries, -most, most).astype(held_as)


def setup_inputs(seed: int = 0) -> dict:
    arg_keys = jax.random.split(jax.random.key(seed), 7)
    return {
        "encoder_embed": normal_values(arg_keys[0], (DOCS, LEN, D), 1.0, 6.0, ((0, 64),)),
        "decoder_embed": normal_values(arg_keys[1], (DOCS, LEN, D), 1.0, 6.0, ((0, 64),)),
        "section_weights": draw_section_weights(jax.random.fold_in(arg_keys[6], 71), 0),
        "norm_gains": jnp.clip(1.0 + 0.18 * jax.random.normal(arg_keys[3], (SUBLAYERS + 1, D), jnp.float32), 0.1, 1.9),
        "input_lengths": plant(jax.random.randint(arg_keys[4], (DOCS,), LEN // 4, LEN + 1), jax.random.fold_in(arg_keys[4], 1), LEN // 4, LEN).astype(jnp.int32),
        "target_lengths": plant(jax.random.randint(arg_keys[5], (DOCS,), LEN // 4, LEN + 1), jax.random.fold_in(arg_keys[5], 1), LEN // 4, LEN).astype(jnp.int32),
    }


def rms_scale(values, norm_gain):
    widened = values.astype(jnp.float32)
    mean_square = lax.optimization_barrier(jnp.mean(widened * widened, axis=-1, keepdims=True))
    return (widened * lax.rsqrt(mean_square + 1e-06) * norm_gain).astype(jnp.bfloat16)

def project(source, weight):
    doc_count, row_count, model_width = source.shape
    flat_rows = source.reshape(doc_count * row_count, model_width)
    result = jnp.dot(flat_rows, weight, preferred_element_type=jnp.float32).astype(jnp.bfloat16)
    return result.reshape(doc_count, row_count, weight.shape[1])

def soft_attention(query_rows, key_rows, key_lengths, causal):
    doc_count, row_count, inner_width = query_rows.shape
    head_count = inner_width // HEAD_DIM
    query_heads = query_rows.reshape(doc_count, row_count, head_count, HEAD_DIM).astype(jnp.float32)
    key_heads = key_rows.reshape(doc_count, row_count, head_count, HEAD_DIM).astype(jnp.float32)
    scores = jnp.einsum('bqhe,bkhe->bhqk', query_heads, key_heads) * HEAD_DIM ** (-0.5)
    positions = jnp.arange(row_count, dtype=jnp.int32)
    key_live = (positions[None, :] < key_lengths[:, None])[:, None, None, :]
    if causal:
        key_live = key_live & (positions[None, None, None, :] <= positions[None, None, :, None])
    scores = jnp.where(key_live, scores, -1e+30)
    largest = lax.optimization_barrier(jnp.max(scores, axis=-1, keepdims=True))
    raised = jnp.exp(scores - largest)
    return (raised / lax.optimization_barrier(jnp.sum(raised, axis=-1, keepdims=True))).astype(jnp.bfloat16)

def mix_out(soft_weights, value_rows, out_weight):
    doc_count, row_count, inner_width = value_rows.shape
    head_count = inner_width // HEAD_DIM
    value_heads = value_rows.reshape(doc_count, row_count, head_count, HEAD_DIM).astype(jnp.float32)
    mixed_rows = jnp.einsum('bhqk,bkhe->bqhe', soft_weights.astype(jnp.float32), value_heads).astype(jnp.bfloat16)
    mixed_rows = mixed_rows.reshape(doc_count * row_count, inner_width)
    head_term = lax.dot_general(mixed_rows, out_weight, (((1,), (1,)), ((), ())), preferred_element_type=jnp.float32)
    return head_term.reshape(doc_count, row_count, out_weight.shape[0])

def layer_kind(sublayer, enc_layers):
    if sublayer < enc_layers:
        return 'encoder'
    if (sublayer - enc_layers) % 2 == 0:
        return 'self'
    return 'cross'

def reference(encoder_embed, decoder_embed, section_weights, norm_gains, input_lengths, target_lengths):
    per_section = BLOCKS // N_SECTION
    row_count = encoder_embed.shape[1]
    positions = jnp.arange(row_count, dtype=jnp.int32)
    stream = encoder_embed
    memory = encoder_embed
    soft_weights = None
    section_rows = []
    for block_index in range(BLOCKS):
        sublayer = block_index // 2
        layer_type = layer_kind(sublayer, ENC_LAYERS)
        weight_pair = section_weights[block_index]
        norm_gain = norm_gains[sublayer]
        if block_index % 2 == 0:
            if sublayer == ENC_LAYERS:
                stream = decoder_embed
            source = rms_scale(stream, norm_gain)
            key_source = memory if layer_type == 'cross' else source
            key_lengths = target_lengths if layer_type == 'self' else input_lengths
            soft_weights = soft_attention(project(source, weight_pair[0]), project(key_source, weight_pair[1]), key_lengths, layer_type == 'self')
        else:
            value_source = memory if layer_type == 'cross' else rms_scale(stream, norm_gain)
            head_term = mix_out(soft_weights, project(value_source, weight_pair[0]), weight_pair[1])
            row_lengths = input_lengths if layer_type == 'encoder' else target_lengths
            row_live = (positions[None, :] < row_lengths[:, None])[:, :, None]
            head_term = jnp.where(row_live, head_term, 0.0)
            stream = (stream.astype(jnp.float32) + head_term).astype(jnp.bfloat16)
            if sublayer == ENC_LAYERS - 1:
                memory = rms_scale(stream, norm_gains[SUBLAYERS])
        if block_index % per_section == per_section - 1:
            section_rows.append(stream)
    return jnp.stack(section_rows)
```

```python
import jax
import jax.numpy as jnp
from jax import lax
from jax.experimental import pallas as pl
from jax.experimental.pallas import tpu as pltpu
from jax.sharding import Mesh, PartitionSpec as P

HEAD_DIM = 128
SIDE = 4
TURNS = (0, -1, 1, 2)
AXES = ("zh", "core", "y", "x", "zl")
DP = ("y", "x", "zl")
SECTION = ("zh", "core")
F32 = jnp.float32
BF16 = jnp.bfloat16


def shift(array, axis, by):
    return lax.ppermute(array, axis, [(i, (i + by) % SIDE) for i in range(SIDE)])


def dot(a, b):
    return jnp.dot(a, b, preferred_element_type=F32)


def dot_t(a, b):
    return lax.dot_general(a, b, (((1,), (1,)), ((), ())), preferred_element_type=F32)


def rms(values, gain):
    mean_square = jnp.mean(values * values, axis=-1, keepdims=True)
    return (values * lax.rsqrt(mean_square + 1e-06) * gain).astype(BF16)


def sublayer_kernel(cross, last, *refs):
    refs = list(refs)
    scal = refs.pop(0)
    gains, mine, other = refs[:3]
    refs = refs[3:]
    if cross:
        mem_mine, mem_other = refs[:2]
        refs = refs[2:]
    a_refs, b_refs = refs[:5], refs[5:10]
    refs = refs[10:]
    out_mine, out_other = refs[:2]
    h3, m3, t3 = refs[2:]
    rows = mine.shape[0]
    x, y, sub, causal, len_mine, len_other = (scal[i] for i in range(6))
    gain = gains[pl.ds(sub, 1), :]
    for part, ref in enumerate((mine, other)):
        h = rms(ref[...].astype(F32), gain)
        for i in range(16):
            h3[i, part * rows:(part + 1) * rows, :] = h[:, i * 128:(i + 1) * 128]
    kv3 = h3
    if cross:
        kv3 = m3
        for part, ref in enumerate((mem_mine, mem_other)):
            for i in range(16):
                m3[i, part * rows:(part + 1) * rows, :] = ref[:, i * 128:(i + 1) * 128]

    def blk(dy, dx):
        return lax.rem(y + dy + SIDE, SIDE) * SIDE + lax.rem(x + dx + SIDE, SIDE)

    def piece(group, turn, which):
        own, plus, minus, far0, far1 = group
        if turn == 2:
            return (far0, far1)[which][0]
        return {0: own, -1: plus, 1: minus}[turn][which]

    q = k = v = None
    for turn in TURNS:
        cols = [blk(turn, d) for d in TURNS]
        hq = jnp.concatenate([h3[c] for c in cols], axis=1)
        hk = jnp.concatenate([kv3[c] for c in cols], axis=1) if cross else hq
        dq, dk = dot(hq, piece(a_refs, turn, 0)), dot(hk, piece(a_refs, turn, 1))
        cols = [blk(d, turn) for d in TURNS]
        dv = dot(jnp.concatenate([kv3[c] for c in cols], axis=1), piece(b_refs, turn, 0))
        q, k, v = (dq, dk, dv) if q is None else (q + dq, k + dk, v + dv)
    q, k, v = q.astype(BF16), k.astype(BF16), v.astype(BF16)
    r = lax.broadcasted_iota(jnp.int32, (2 * rows, 2 * rows), 0)
    c = lax.broadcasted_iota(jnp.int32, (2 * rows, 2 * rows), 1)
    first = c < rows
    live = (r < rows) == first
    key_at = jnp.where(first, c, c - rows)
    live = live & (key_at < jnp.where(first, len_mine, len_other))
    live = live & ((c <= r) | (causal == 0))
    mixed = []
    for head in range(4):
        at = slice(head * HEAD_DIM, (head + 1) * HEAD_DIM)
        s = dot_t(q[:, at], k[:, at]) * HEAD_DIM ** (-0.5)
        s = jnp.where(live, s, -1e30)
        e = jnp.exp(s - jnp.max(s, axis=-1, keepdims=True))
        p = (e / jnp.sum(e, axis=-1, keepdims=True)).astype(BF16)
        mixed.append(dot(p, v[:, at]).astype(BF16))
    mixed = jnp.concatenate(mixed, axis=1)
    for turn in TURNS:
        t = dot_t(mixed, piece(b_refs, turn, 1))
        for j, d in enumerate(TURNS):
            t3[blk(d, turn)] = t[:, j * 128:(j + 1) * 128]
    for i in range(16):
        at = slice(i * 128, (i + 1) * 128)
        out_mine[:, at] = t3[i, :rows, :].astype(out_mine.dtype)
        out_other[:, at] = t3[i, rows:, :].astype(out_other.dtype)


def sublayer(cross, last, scal, gains, streams, mem, a_parts, b_parts):
    import functools
    rows, width = streams[0].shape
    vmem = pl.BlockSpec(memory_space=pltpu.VMEM)
    operands = [gains, *streams, *mem, *a_parts, *b_parts]
    return pl.pallas_call(
        functools.partial(sublayer_kernel, cross, last),
        out_shape=(
            jax.ShapeDtypeStruct((rows, width), F32),
            jax.ShapeDtypeStruct((rows, width), BF16),
        ),
        in_specs=[pl.BlockSpec(memory_space=pltpu.SMEM)] + [vmem] * len(operands),
        out_specs=(vmem, vmem),
        scratch_shapes=[
            pltpu.VMEM((16, 2 * rows, 128), BF16),
            pltpu.VMEM((16, 2 * rows, 128) if cross else (1, 16, 128), BF16),
            pltpu.VMEM((16, 2 * rows, 128), F32),
        ],
        compiler_params=pltpu.CompilerParams(vmem_limit_bytes=40 * 1024 * 1024),
        cost_estimate=pl.CostEstimate(
            flops=2 * 128 * 2048 * 512 * 4, bytes_accessed=9 * 2**20, transcendentals=65536
        ),
    )(scal, *operands)


def ring(array, axis):
    parts = [array] + [shift(array, axis, -turn) for turn in TURNS[1:]]
    return jnp.concatenate(parts, axis=1)


def ring_parts(array, axis):
    plus, minus = shift(array, axis, 1), shift(array, axis, -1)
    return plus, minus


def far_parts(plus, minus, axis):
    return shift(plus[:1], axis, 1), shift(minus[1:], axis, -1)


def gather(weights):
    pair, depth, width = weights.shape[1:]
    halves = weights[0].reshape(pair, depth, 2, width // 2).transpose(2, 0, 1, 3)
    sent = jnp.broadcast_to(halves[:, None], (2, SIDE) + halves.shape[1:])
    sent = sent.reshape((2 * SIDE,) + halves.shape[1:])
    got = lax.all_to_all(sent, ("core", "zl"), 0, 0, tiled=True)
    got = got.reshape(2, SIDE, pair, depth, width // 2).transpose(0, 2, 1, 3, 4)
    got = got.reshape(2, pair, SIDE * depth, width // 2)
    a, b = ring(got[0], "x"), ring(got[1], "y")
    a, b = lax.optimization_barrier((a, b))
    ap, am = ring_parts(a, "y")
    bp, bm = ring_parts(b, "x")
    af0, af1 = far_parts(ap, am, "y")
    bf0, bf1 = far_parts(bp, bm, "x")
    return (a, ap, am, af0, af1), (b, bp, bm, bf0, bf1)


def on_device(encoder_embed, decoder_embed, section_weights, norm_gains, input_lengths, target_lengths):
    zh, core = lax.axis_index("zh"), lax.axis_index("core")
    y, x = lax.axis_index("y"), lax.axis_index("x")
    rows = encoder_embed.shape[1]
    encoder = zh < 2
    causal = zh == 2
    key_lengths = jnp.where(causal, target_lengths, input_lengths)
    row_lengths = jnp.where(encoder, input_lengths, target_lengths)
    scal = jnp.stack(
        [x, y, zh, causal.astype(jnp.int32), key_lengths[core], key_lengths[1 - core]]
    ).astype(jnp.int32)
    live = (jnp.arange(rows, dtype=jnp.int32) < row_lengths[core])[:, None]
    live_other = (jnp.arange(rows, dtype=jnp.int32) < row_lengths[1 - core])[:, None]

    a_parts, b_parts = gather(section_weights)
    source = jnp.where(encoder, encoder_embed, decoder_embed)
    mine, other = source[core], source[1 - core]

    def added(stream, term, alive):
        return stream.astype(F32) + jnp.where(alive, term, 0.0)

    def swapped(array):
        return lax.ppermute(array, "core", [(0, 1), (1, 0)])

    kept, sent = sublayer(False, False, scal, norm_gains, (mine, other), (), a_parts, b_parts)
    first = added(mine, kept + swapped(sent).astype(F32), live).astype(BF16)
    mine2 = lax.ppermute(first, "zh", [(0, 1), (2, 3)])
    other2 = swapped(mine2)
    kept, sent = sublayer(False, False, scal, norm_gains, (mine2, other2), (), a_parts, b_parts)
    second = added(mine2, kept + swapped(sent).astype(F32), live).astype(BF16)
    memory = rms(second.astype(F32), norm_gains[4:5])
    mem = lax.ppermute(memory, "zh", [(1, 3)])
    mem_other = swapped(mem)
    early = jnp.where(zh == 1, second, first)
    early_other = lax.ppermute(early, "core", [(0, 1)])
    kept, sent = sublayer(
        True, True, scal, norm_gains, (mine2, other2), (mem, mem_other), a_parts, b_parts
    )
    kept_mine, kept_other = lax.ppermute((sent, kept.astype(BF16)), SECTION, [(6, 7)])
    third = added(mine2, kept + kept_mine.astype(F32), live).astype(BF16)
    third_other = added(other2, sent.astype(F32) + kept_other.astype(F32), live_other).astype(BF16)

    back = core == 1
    final = zh == 3
    even = (zh == 0) | (zh == 2)
    front_mine = jnp.where(even, mine, mine2)
    front_other = jnp.where(even, other, other2)
    back_mine = jnp.where(final, third, early)
    back_other = jnp.where(final, third_other, early_other)
    doc0 = jnp.where(back, back_other, front_mine)
    doc1 = jnp.where(back, back_mine, front_other)
    return jnp.stack([doc0, doc1])[None]


def solution(mesh):
    fine = Mesh(mesh.devices.reshape(SIDE, 2, SIDE, SIDE, SIDE), AXES)
    in_specs = (
        P(DP, None, None),
        P(DP, None, None),
        P(SECTION, None, DP, None),
        P(),
        P(DP),
        P(DP),
    )
    out_specs = P(SECTION, DP, None, None)
    return jax.shard_map(
        on_device, mesh=fine, in_specs=in_specs, out_specs=out_specs, check_vma=False
    )
```

```python
import functools

import jax
import jax.numpy as jnp
from jax import lax
from jax.experimental import pallas as pl
from jax.experimental.pallas import tpu as pltpu
from jax.sharding import Mesh, PartitionSpec as P

HEAD_DIM = 128
SIDE = 4
TURNS = (0, 1, 3, 2)
AXES = ("zh", "core", "y", "x", "zl")
DP = ("y", "x", "zl")
SECTION = ("zh", "core")
F32 = jnp.float32
BF16 = jnp.bfloat16


def exchange(array, axis, by):
    return lax.ppermute(array, axis, [(i, i ^ by) for i in range(SIDE)])


def dot(a, b):
    return jnp.dot(a, b, preferred_element_type=F32)


def dot_t(a, b):
    return lax.dot_general(a, b, (((1,), (1,)), ((), ())), preferred_element_type=F32)


def rms(values, gain):
    mean_square = jnp.mean(values * values, axis=-1, keepdims=True)
    return (values * lax.rsqrt(mean_square + 1e-06) * gain).astype(BF16)


def sublayer_kernel(cross, cube, *refs):
    refs = list(refs)
    scal = refs.pop(0)
    gains, mine, other = refs[:3]
    refs = refs[3:]
    mem = ()
    if cross:
        mem = refs[:2]
        refs = refs[2:]
    a_refs, b_refs = refs[:5], refs[5:10]
    refs = refs[10:]
    if cross:
        rows = mine.shape[0]
        out_mine, out_other = refs[0].at[:rows], refs[0].at[rows:]
        refs = refs[1:]
    else:
        out_mine, out_other = refs[:2]
        refs = refs[2:]
    h3, m3, t3 = refs

    def work():
        sublayer_body(scal, gains, (mine, other), mem, a_refs, b_refs, out_mine, out_other, h3, m3, t3)

    if cube is None:
        work()
    else:
        pl.when(scal[2] == cube)(work)


def sublayer_body(scal, gains, streams, mem, a_refs, b_refs, out_mine, out_other, h3, m3, t3):
    rows = streams[0].shape[0]
    x, y, sub, causal, len_mine, len_other = (scal[i] for i in range(6))
    gain = gains[pl.ds(sub, 1), :]
    for part, ref in enumerate(streams):
        h = rms(ref[...].astype(F32), gain)
        for i in range(16):
            h3[i, part * rows:(part + 1) * rows, :] = h[:, i * 128:(i + 1) * 128]
    kv3 = m3 if mem else h3
    for part, ref in enumerate(mem):
        for i in range(16):
            m3[i, part * rows:(part + 1) * rows, :] = ref[:, i * 128:(i + 1) * 128]

    def blk(dy, dx):
        return lax.bitwise_xor(y, dy) * SIDE + lax.bitwise_xor(x, dx)

    def piece(group, turn, which):
        if turn == 2:
            return group[3 + which][0]
        return group[TURNS.index(turn)][which]

    q = k = v = None
    for turn in TURNS:
        cols = [blk(turn, d) for d in TURNS]
        hq = jnp.concatenate([h3[c] for c in cols], axis=1)
        hk = jnp.concatenate([kv3[c] for c in cols], axis=1) if mem else hq
        dq, dk = dot(hq, piece(a_refs, turn, 0)), dot(hk, piece(a_refs, turn, 1))
        cols = [blk(d, turn) for d in TURNS]
        dv = dot(jnp.concatenate([kv3[c] for c in cols], axis=1), piece(b_refs, turn, 0))
        q, k, v = (dq, dk, dv) if q is None else (q + dq, k + dk, v + dv)
    q, k, v = q.astype(BF16), k.astype(BF16), v.astype(BF16)
    r = lax.broadcasted_iota(jnp.int32, (2 * rows, 2 * rows), 0)
    c = lax.broadcasted_iota(jnp.int32, (2 * rows, 2 * rows), 1)
    first = c < rows
    live = (r < rows) == first
    key_at = jnp.where(first, c, c - rows)
    live = live & (key_at < jnp.where(first, len_mine, len_other))
    live = live & ((c <= r) | (causal == 0))
    mixed = []
    for head in range(4):
        at = slice(head * HEAD_DIM, (head + 1) * HEAD_DIM)
        s = dot_t(q[:, at], k[:, at]) * HEAD_DIM ** (-0.5)
        s = jnp.where(live, s, -1e30)
        e = jnp.exp(s - jnp.max(s, axis=-1, keepdims=True))
        p = (e / jnp.sum(e, axis=-1, keepdims=True)).astype(BF16)
        mixed.append(dot(p, v[:, at]).astype(BF16))
    mixed = jnp.concatenate(mixed, axis=1)
    for turn in TURNS:
        t = dot_t(mixed, piece(b_refs, turn, 1))
        for j, d in enumerate(TURNS):
            t3[blk(d, turn)] = t[:, j * 128:(j + 1) * 128]
    for i in range(16):
        at = slice(i * 128, (i + 1) * 128)
        out_mine[:, at] = t3[i, :rows, :].astype(out_mine.dtype)
        out_other[:, at] = t3[i, rows:, :].astype(out_other.dtype)


VMEM = pl.BlockSpec(memory_space=pltpu.VMEM)
SMEM = pl.BlockSpec(memory_space=pltpu.SMEM)


def sublayer(cross, cube, scal, gains, streams, mem, a_parts, b_parts):
    rows, width = streams[0].shape
    operands = [gains, *streams, *mem, *a_parts, *b_parts]
    halves = tuple(jax.ShapeDtypeStruct((rows, width), kind) for kind in (F32, BF16))
    return pl.pallas_call(
        functools.partial(sublayer_kernel, cross, cube),
        out_shape=jax.ShapeDtypeStruct((2 * rows, width), BF16) if cross else halves,
        in_specs=[SMEM] + [VMEM] * len(operands),
        out_specs=VMEM if cross else (VMEM, VMEM),
        scratch_shapes=[
            pltpu.VMEM((16, 2 * rows, 128), BF16),
            pltpu.VMEM((16, 2 * rows, 128) if cross else (1, 16, 128), BF16),
            pltpu.VMEM((16, 2 * rows, 128), F32),
        ],
        compiler_params=pltpu.CompilerParams(vmem_limit_bytes=20 * 1024 * 1024),
        cost_estimate=pl.CostEstimate(
            flops=2 * 128 * 2048 * 512 * 4, bytes_accessed=9 * 2**20, transcendentals=65536
        ),
    )(scal, *operands)


def finish_kernel(scal, mine, other, in1m, in1o, in3m, in3o, early_m, early_o, own, got, out):
    rows = mine.shape[0]
    cube, core = scal[2], scal[6]
    even = (cube == 0) | (cube == 2)

    def put(doc0, doc1):
        out[0] = doc0[...]
        out[1] = doc1[...]

    @pl.when((core == 0) & even)
    def _():
        put(mine, other)

    @pl.when((core == 0) & (cube == 1))
    def _():
        put(in1m, in1o)

    @pl.when((core == 0) & (cube == 3))
    def _():
        put(in3m, in3o)

    @pl.when((core == 1) & (cube != 3))
    def _():
        put(early_o, early_m)

    @pl.when((core == 1) & (cube == 3))
    def _():
        at = lax.broadcasted_iota(jnp.int32, mine.shape, 0)
        low, high = slice(0, rows), slice(rows, 2 * rows)
        for slot, base, a, b, live in ((1, in3m, low, high, scal[7]), (0, in3o, high, low, scal[8])):
            term = own[a, :].astype(F32) + got[b, :].astype(F32)
            term = jnp.where(at < live, term, 0.0)
            out[slot] = (base[...].astype(F32) + term).astype(BF16)


def finish(scal, *parts):
    return pl.pallas_call(
        finish_kernel,
        out_shape=jax.ShapeDtypeStruct((2,) + parts[0].shape, BF16),
        in_specs=[SMEM] + [VMEM] * len(parts),
        out_specs=VMEM,
        compiler_params=pltpu.CompilerParams(vmem_limit_bytes=20 * 1024 * 1024),
    )(scal, *parts)


def ring(array, axis):
    parts = [array] + [exchange(array, axis, turn) for turn in TURNS[1:]]
    return jnp.concatenate(parts, axis=1)


def ring_parts(array, axis):
    return exchange(array, axis, 1), exchange(array, axis, 3)


def far_parts(by1, by3, axis):
    return exchange(by1[:1], axis, 3), exchange(by3[1:], axis, 1)


def gather(weights):
    pair, depth, width = weights.shape[1:]
    halves = weights[0].reshape(pair, depth, 2, width // 2).transpose(2, 0, 1, 3)
    sent = jnp.broadcast_to(halves[:, None], (2, SIDE) + halves.shape[1:])
    sent = sent.reshape((2 * SIDE,) + halves.shape[1:])
    got = lax.all_to_all(sent, ("core", "zl"), 0, 0, tiled=True)
    got = got.reshape(2, SIDE, pair, depth, width // 2).transpose(0, 2, 1, 3, 4)
    got = got.reshape(2, pair, SIDE * depth, width // 2)
    a, b = ring(got[0], "x"), ring(got[1], "y")
    a, b = lax.optimization_barrier((a, b))
    ap, am = ring_parts(a, "y")
    bp, bm = ring_parts(b, "x")
    af0, af1 = far_parts(ap, am, "y")
    bf0, bf1 = far_parts(bp, bm, "x")
    return (a, ap, am, af0, af1), (b, bp, bm, bf0, bf1)


def on_device(encoder_embed, decoder_embed, section_weights, norm_gains, input_lengths, target_lengths):
    zh, core = lax.axis_index("zh"), lax.axis_index("core")
    y, x = lax.axis_index("y"), lax.axis_index("x")
    rows = encoder_embed.shape[1]
    encoder = zh < 2
    causal = zh == 2
    key_lengths = jnp.where(causal, target_lengths, input_lengths)
    row_lengths = jnp.where(encoder, input_lengths, target_lengths)
    scal = jnp.stack(
        [
            x,
            y,
            zh,
            causal.astype(jnp.int32),
            key_lengths[core],
            key_lengths[1 - core],
            core,
            row_lengths[core],
            row_lengths[1 - core],
        ]
    ).astype(jnp.int32)
    live = (jnp.arange(rows, dtype=jnp.int32) < row_lengths[core])[:, None]

    a_parts, b_parts = gather(section_weights)
    source = jnp.where(encoder, encoder_embed, decoder_embed)
    mine, other = source[core], source[1 - core]

    def added(stream, term, alive):
        return stream.astype(F32) + jnp.where(alive, term, 0.0)

    def swapped(array, cubes=range(SIDE)):
        pairs = [(2 * c + i, 2 * c + 1 - i) for c in cubes for i in range(2)]
        return lax.ppermute(array, SECTION, pairs)

    kept, sent = sublayer(False, None, scal, norm_gains, (mine, other), (), a_parts, b_parts)
    first = added(mine, kept + swapped(sent, (0, 2)).astype(F32), live).astype(BF16)
    in1 = lax.ppermute(first, "zh", [(0, 1)])
    in3 = lax.ppermute(first, "zh", [(2, 3)])
    in1_other = swapped(in1, (1,))
    kept, sent = sublayer(False, 1, scal, norm_gains, (in1, in1_other), (), a_parts, b_parts)
    second = added(in1, kept + swapped(sent, (1,)).astype(F32), live).astype(BF16)
    memory = rms(second.astype(F32), norm_gains[4:5])
    mem = lax.ppermute(memory, "zh", [(1, 3)])
    early = jnp.where(zh == 1, second, first)
    early_other = lax.ppermute(early, SECTION, [(0, 1), (2, 3), (4, 5)])
    in3_other = swapped(in3, (3,))
    mem_other = swapped(mem, (3,))
    own = sublayer(
        True, 3, scal, norm_gains, (in3, in3_other), (mem, mem_other), a_parts, b_parts
    )
    got = lax.ppermute(own, SECTION, [(6, 7)])
    out = finish(
        scal, mine, other, in1, in1_other, in3, in3_other, early, early_other, own, got
    )
    return out[None]


def solution(mesh):
    fine = Mesh(mesh.devices.reshape(SIDE, 2, SIDE, SIDE, SIDE), AXES)
    in_specs = (
        P(DP, None, None),
        P(DP, None, None),
        P(SECTION, None, DP, None),
        P(),
        P(DP),
        P(DP),
    )
    out_specs = P(SECTION, DP, None, None)
    return jax.shard_map(
        on_device, mesh=fine, in_specs=in_specs, out_specs=out_specs, check_vma=False
    )
```

```python
import functools

import jax
import jax.numpy as jnp
from jax import lax
from jax.experimental import pallas as pl
from jax.experimental.pallas import tpu as pltpu
from jax.sharding import Mesh, PartitionSpec as P

HEAD_DIM = 128
SIDE = 4
TURNS = (0, 1, 3, 2)
AXES = ("zh", "core", "y", "x", "zl")
DP = ("y", "x", "zl")
SECTION = ("zh", "core")
F32 = jnp.float32
BF16 = jnp.bfloat16
VMEM = pl.BlockSpec(memory_space=pltpu.VMEM)
SMEM = pl.BlockSpec(memory_space=pltpu.SMEM)
BLOCKS = 16
LANES = 128


def exchange(array, axis, by):
    return lax.ppermute(array, axis, [(i, i ^ by) for i in range(SIDE)])


def dot(a, b):
    return jnp.dot(a, b, preferred_element_type=F32)


def dot_t(a, b):
    return lax.dot_general(a, b, (((1,), (1,)), ((), ())), preferred_element_type=F32)


def rms(values, gain):
    mean_square = jnp.mean(values * values, axis=-1, keepdims=True)
    return (values * lax.rsqrt(mean_square + 1e-06) * gain).astype(BF16)


def lanes(i):
    return slice(i * LANES, (i + 1) * LANES)


def block_at(scal, dy, dx):
    return lax.bitwise_xor(scal[1], dy) * SIDE + lax.bitwise_xor(scal[0], dx)


def alive(scal, shape):
    at = lax.broadcasted_iota(jnp.int32, shape, 0)
    half = shape[0] // 2
    second = at >= half
    return jnp.where(second, at - half, at) < jnp.where(second, scal[8], scal[7])


def attend(scal, h3, m3, gather_a, gather_b):
    acc_q = acc_k = acc_b = None
    for turn, a, b in zip(TURNS, gather_a, gather_b):
        at = [block_at(scal, turn, d) for d in TURNS]
        hq = jnp.concatenate([h3[i] for i in at], axis=1)
        if m3 is h3:
            both = dot(hq, a[...])
            dq, dk = both[:, :512], both[:, 512:]
        else:
            dq = dot(hq, a[:, :512])
            dk = dot(jnp.concatenate([m3[i] for i in at], axis=1), a[:, 512:])
        at = [block_at(scal, d, turn) for d in TURNS]
        db = dot(jnp.concatenate([m3[i] for i in at], axis=1), b[...])
        if acc_q is None:
            acc_q, acc_k, acc_b = dq, dk, db
        else:
            acc_q, acc_k, acc_b = acc_q + dq, acc_k + dk, acc_b + db
    q = acc_q.astype(BF16)
    k = jnp.concatenate([acc_k, acc_b[:, :256]], axis=1).astype(BF16)
    v = acc_b[:, 256:].astype(BF16)
    count = q.shape[0]
    rows = count // 2
    r = lax.broadcasted_iota(jnp.int32, (count, count), 0)
    c = lax.broadcasted_iota(jnp.int32, (count, count), 1)
    first = c < rows
    live = (r < rows) == first
    live = live & (jnp.where(first, c, c - rows) < jnp.where(first, scal[4], scal[5]))
    live = live & ((c <= r) | (scal[3] == 0))
    mixed = []
    for head in range(4):
        at = lanes(head)
        s = dot_t(q[:, at], k[:, at]) * HEAD_DIM ** (-0.5)
        s = jnp.where(live, s, -1e30)
        e = jnp.exp(s - jnp.max(s, axis=-1, keepdims=True))
        p = (e / jnp.sum(e, axis=-1, keepdims=True)).astype(BF16)
        mixed.append(dot(p, v[:, at]).astype(BF16))
    return jnp.concatenate(mixed, axis=1)


def put_blocks(h3, h):
    for i in range(BLOCKS):
        h3[i] = h[:, lanes(i)]


def project_out(scal, mixed, gather_o, t3):
    for turn, o in zip(TURNS, gather_o):
        t = dot_t(mixed, o[...])
        for j, d in enumerate(TURNS):
            t3[block_at(scal, turn, d)] = t[:, lanes(j)]


def first_kernel(scal, gains, stream, *refs):
    gather_a, gather_b, (mixed, h3) = refs[:4], refs[4:8], refs[8:]

    @pl.when(lax.rem(scal[2], 2) == 0)
    def _():
        put_blocks(h3, rms(stream[...].astype(F32), gains[pl.ds(scal[2], 1), :]))
        mixed[...] = attend(scal, h3, h3, gather_a, gather_b)


def received_kernel(scal, mixed, out_weight, part):
    @pl.when(lax.rem(scal[2], 2) == 1)
    def _():
        for i in range(SIDE):
            at = slice(i * 512, (i + 1) * 512)
            part[:, at] = dot_t(mixed[...], out_weight[at, :]).astype(BF16)


def second_kernel(scal, gains, base, own, got, mixed_in, *refs):
    gather_a, gather_b, gather_o = refs[:4], refs[4:8], refs[8:12]
    stream, mine, other, h3, mixed, t3 = refs[12:]
    cube = scal[2]

    @pl.when(lax.rem(cube, 2) == 1)
    def _():
        term = own[...].astype(F32) + got[...].astype(F32)
        term = jnp.where(alive(scal, base.shape), term, 0.0)
        stream[...] = (base[...].astype(F32) + term).astype(BF16)

    @pl.when(cube == 1)
    def _():
        put_blocks(h3, rms(stream[...].astype(F32), gains[pl.ds(cube, 1), :]))
        mixed[...] = attend(scal, h3, h3, gather_a, gather_b)

    @pl.when(lax.rem(cube, 2) == 0)
    def _():
        mixed[...] = mixed_in[...]

    @pl.when(cube != 3)
    def _():
        project_out(scal, mixed[...], gather_o, t3)
        rows = mine.shape[0]
        here = pl.ds(pl.multiple_of(scal[6] * rows, rows), rows)
        there = pl.ds(pl.multiple_of((1 - scal[6]) * rows, rows), rows)
        for i in range(BLOCKS):
            mine[:, lanes(i)] = t3[i, here, :]
            other[:, lanes(i)] = t3[i, there, :].astype(BF16)


def joined_kernel(scal, gains, base, stream, mine, got, out, memory):
    rows = mine.shape[0]
    here = pl.ds(pl.multiple_of(scal[6] * rows, rows), rows)
    cube = scal[2]

    def join(source):
        at = lax.broadcasted_iota(jnp.int32, mine.shape, 0)
        term = mine[...] + got[...].astype(F32)
        term = jnp.where(at < jnp.where(scal[6] == 0, scal[7], scal[8]), term, 0.0)
        out[...] = (source[here, :].astype(F32) + term).astype(BF16)

    @pl.when(lax.rem(cube, 2) == 0)
    def _():
        join(base)

    @pl.when(cube == 1)
    def _():
        join(stream)
        last = gains.shape[0] - 1
        memory[...] = rms(out[...].astype(F32), gains[last:, :])


def third_kernel(scal, gains, stream, mem_mine, mem_other, *refs):
    gather_a, gather_b, gather_o = refs[:4], refs[4:8], refs[8:12]
    part, h3, m3, t3 = refs[12:]
    cube = scal[2]

    @pl.when(cube == 3)
    def _():
        rows = mem_mine.shape[0]
        here = pl.ds(pl.multiple_of(scal[6] * rows, rows), rows)
        there = pl.ds(pl.multiple_of((1 - scal[6]) * rows, rows), rows)
        put_blocks(h3, rms(stream[...].astype(F32), gains[pl.ds(cube, 1), :]))
        for i in range(BLOCKS):
            m3[i, here, :] = mem_mine[:, lanes(i)]
            m3[i, there, :] = mem_other[:, lanes(i)]
        project_out(scal, attend(scal, h3, m3, gather_a, gather_b), gather_o, t3)
        for i in range(BLOCKS):
            part[:, lanes(i)] = t3[i].astype(BF16)


def finish_kernel(scal, base, stream, early, early_other, own, got, out):
    rows = early.shape[0]
    cube, core = scal[2], scal[6]
    odd = lax.rem(cube, 2) == 1

    @pl.when((core == 0) & jnp.logical_not(odd))
    def _():
        out[...] = base[...]

    @pl.when((core == 0) & odd)
    def _():
        out[...] = stream[...]

    @pl.when((core == 1) & (cube != 3))
    def _():
        out[:rows, :] = early_other[...]
        out[rows:, :] = early[...]

    @pl.when((core == 1) & (cube == 3))
    def _():
        term = own[...].astype(F32) + got[...].astype(F32)
        term = jnp.where(alive(scal, base.shape), term, 0.0)
        out[...] = (stream[...].astype(F32) + term).astype(BF16)


def call(kernel, scal, operands, outs, scratch=(), flops=0):
    size = sum(a.size * a.dtype.itemsize for a in operands)
    return pl.pallas_call(
        kernel,
        out_shape=outs,
        in_specs=[SMEM] + [VMEM] * len(operands),
        out_specs=jax.tree.map(lambda _: VMEM, outs),
        scratch_shapes=[pltpu.VMEM(shape, kind) for shape, kind in scratch],
        compiler_params=pltpu.CompilerParams(vmem_limit_bytes=12 * 1024 * 1024),
        cost_estimate=pl.CostEstimate(flops=flops, bytes_accessed=size, transcendentals=0),
    )(scal, *operands)


def rings(array, axis):
    return [array] + [exchange(array, axis, turn) for turn in TURNS[1:]]


def on_device(encoder_embed, decoder_embed, section_weights, norm_gains, input_lengths, target_lengths):
    zh, core = lax.axis_index("zh"), lax.axis_index("core")
    y, x = lax.axis_index("y"), lax.axis_index("x")
    docs, rows, width = encoder_embed.shape
    count = docs * rows
    encoder = zh < 2
    causal = zh == 2
    key_lengths = jnp.where(causal, target_lengths, input_lengths)
    row_lengths = jnp.where(encoder, input_lengths, target_lengths)
    scal = jnp.stack(
        [x, y, zh, causal.astype(jnp.int32), key_lengths[0], key_lengths[1], core]
        + [row_lengths[0], row_lengths[1]]
    ).astype(jnp.int32)
    base = jnp.where(encoder, encoder_embed, decoder_embed).reshape(count, width)

    pair, depth, inner = section_weights.shape[1:]
    half = inner // 2
    sent = section_weights[0].reshape(pair, depth, 2, half).transpose(2, 0, 1, 3)
    sent = jnp.broadcast_to(sent[:, None], (2, SIDE, pair, depth, half))
    sent = sent.reshape(2 * SIDE, pair, depth, half)
    mats = lax.all_to_all(sent, ("core", "zl"), 0, 0, tiled=True)
    mats = mats.reshape(2, SIDE, pair, depth, half).transpose(0, 2, 1, 3, 4)
    mats = mats.reshape(2 * pair, SIDE * depth, half)
    a = jnp.concatenate([mats[0], mats[1][:, : half // 2]], axis=1)
    b = jnp.concatenate([mats[1][:, half // 2:], mats[2]], axis=1)
    own_o = mats[3]
    prev_o = lax.ppermute(own_o, "zh", [(0, 1), (2, 3)])

    a = jnp.concatenate(rings(a, "x"), axis=0)
    b = jnp.concatenate(rings(b, "y"), axis=0)
    prev_o = lax.all_gather(prev_o, ("y", "x"), axis=0, tiled=True)
    a, b = lax.optimization_barrier((a, b))
    gather_a, gather_b = rings(a, "y"), rings(b, "x")
    own_o, gather_a[1] = lax.optimization_barrier((own_o, gather_a[1]))
    own_o = jnp.concatenate(rings(own_o, "x"), axis=0)

    blocks = ((BLOCKS, count, LANES), BF16)
    totals = ((BLOCKS, count, LANES), F32)
    narrow = jax.ShapeDtypeStruct((count, half), BF16)
    wide = jax.ShapeDtypeStruct((count, width), BF16)
    doc = jax.ShapeDtypeStruct((rows, width), BF16)
    doc32 = jax.ShapeDtypeStruct((rows, width), F32)
    work = 2 * count * width * half
    mixed = call(
        first_kernel, scal, [norm_gains, base, *gather_a, *gather_b], narrow, [blocks], 3 * work
    )
    mixed_in = lax.ppermute(mixed, "zh", [(0, 1), (2, 3)])
    own_o, mixed = lax.optimization_barrier((own_o, mixed))
    gather_o = rings(own_o, "y")

    def swapped(array, cubes):
        pairs = [(2 * c + i, 2 * c + 1 - i) for c in cubes for i in range(2)]
        return lax.ppermute(array, SECTION, pairs)

    part = call(received_kernel, scal, [mixed_in, prev_o], wide, (), work)
    part_got = swapped(part, (1, 3))
    stream, mine, other = call(
        second_kernel,
        scal,
        [norm_gains, base, part, part_got, mixed, *gather_a, *gather_b, *gather_o],
        (wide, doc32, doc),
        [blocks, ((count, half), BF16), totals],
        4 * work,
    )
    other = swapped(other, (0, 1, 2))
    early, memory = call(
        joined_kernel, scal, [norm_gains, base, stream, mine, other], (doc, doc)
    )
    mem = lax.ppermute(memory, "zh", [(1, 3)])
    early_other = lax.ppermute(early, SECTION, [(0, 1), (2, 3), (4, 5)])
    mem_other = swapped(mem, (3,))
    own = call(
        third_kernel,
        scal,
        [norm_gains, stream, mem, mem_other, *gather_a, *gather_b, *gather_o],
        wide,
        [blocks, blocks, totals],
        4 * work,
    )
    got = lax.ppermute(own, SECTION, [(6, 7)])
    out = call(finish_kernel, scal, [base, stream, early, early_other, own, got], wide)
    return out.reshape(1, docs, rows, width)


def solution(mesh):
    fine = Mesh(mesh.devices.reshape(SIDE, 2, SIDE, SIDE, SIDE), AXES)
    in_specs = (
        P(DP, None, None),
        P(DP, None, None),
        P(SECTION, None, DP, None),
        P(),
        P(DP),
        P(DP),
    )
    out_specs = P(SECTION, DP, None, None)
    return jax.shard_map(
        on_device, mesh=fine, in_specs=in_specs, out_specs=out_specs, check_vma=False
    )
```

```python
import functools
import itertools

import jax
import jax.numpy as jnp
from jax import lax
from jax.experimental import pallas as pl
from jax.experimental.pallas import tpu as pltpu
from jax.sharding import Mesh, PartitionSpec as P

HEAD_DIM = 128
SIDE = 4
TURNS = (0, 1, 3, 2)
AXES = ("zh", "core", "y", "x", "zl")
DP = ("y", "x", "zl")
SECTION = ("zh", "core")
F32 = jnp.float32
BF16 = jnp.bfloat16


def place(zh, core, y, x, zl):
    return (((zh * 2 + core) * SIDE + y) * SIDE + x) * SIDE + zl


def exchange(array, outer, by):
    pairs = []
    for zh, core, y, x, zl in itertools.product(*map(range, (SIDE, 2, SIDE, SIDE, SIDE))):
        along_y = outer == (core == 0)
        to = (y ^ by, x) if along_y else (y, x ^ by)
        pairs.append((place(zh, core, y, x, zl), place(zh, core, *to, zl)))
    return lax.ppermute(array, AXES, pairs)


def dot(a, b):
    return jnp.dot(a, b, preferred_element_type=F32)


def dot_t(a, b):
    return lax.dot_general(a, b, (((1,), (1,)), ((), ())), preferred_element_type=F32)


def rms(values, gain):
    mean_square = jnp.mean(values * values, axis=-1, keepdims=True)
    return (values * lax.rsqrt(mean_square + 1e-06) * gain).astype(BF16)


def sublayer_kernel(cross, cube, *refs):
    refs = list(refs)
    scal = refs.pop(0)
    gains, mine, other = refs[:3]
    refs = refs[3:]
    mem = ()
    if cross:
        mem = refs[:2]
        refs = refs[2:]
    pieces = refs[:SIDE]
    refs = refs[SIDE:]
    if cross:
        rows = mine.shape[0]
        out_mine, out_other = refs[0].at[:rows], refs[0].at[rows:]
        refs = refs[1:]
    else:
        out_mine, out_other = refs[:2]
        refs = refs[2:]
    h3, m3, t3 = refs

    def work():
        sublayer_body(scal, gains, (mine, other), mem, pieces, out_mine, out_other, h3, m3, t3)

    if cube is None:
        work()
    else:
        pl.when(scal[2] == cube)(work)


def sublayer_body(scal, gains, streams, mem, pieces, out_mine, out_other, h3, m3, t3):
    rows = streams[0].shape[0]
    x, y, sub, causal, len_mine, len_other = (scal[i] for i in range(6))
    gain = gains[pl.ds(sub, 1), :]
    for part, ref in enumerate(streams):
        h = rms(ref[...].astype(F32), gain)
        for i in range(16):
            h3[i, part * rows:(part + 1) * rows, :] = h[:, i * 128:(i + 1) * 128]
    kv3 = m3 if mem else h3
    for part, ref in enumerate(mem):
        for i in range(16):
            m3[i, part * rows:(part + 1) * rows, :] = ref[:, i * 128:(i + 1) * 128]

    back = scal[6] == 1

    def blk(outer, inner):
        dy, dx = jnp.where(back, inner, outer), jnp.where(back, outer, inner)
        return lax.bitwise_xor(y, dy) * SIDE + lax.bitwise_xor(x, dx)

    q = k = v = None
    for turn, piece in zip(TURNS, pieces):
        cols = [blk(turn, d) for d in TURNS]
        hq = jnp.concatenate([h3[c] for c in cols], axis=1)
        hk = jnp.concatenate([kv3[c] for c in cols], axis=1) if mem else hq
        dq, dk, dv = dot(hq, piece[0]), dot(hk, piece[1]), dot(hk, piece[2])
        q, k, v = (dq, dk, dv) if q is None else (q + dq, k + dk, v + dv)
    q, k, v = q.astype(BF16), k.astype(BF16), v.astype(BF16)
    r = lax.broadcasted_iota(jnp.int32, (2 * rows, 2 * rows), 0)
    c = lax.broadcasted_iota(jnp.int32, (2 * rows, 2 * rows), 1)
    first = c < rows
    live = (r < rows) == first
    key_at = jnp.where(first, c, c - rows)
    live = live & (key_at < jnp.where(first, len_mine, len_other))
    live = live & ((c <= r) | (causal == 0))
    mixed = []
    for head in range(4):
        at = slice(head * HEAD_DIM, (head + 1) * HEAD_DIM)
        s = dot_t(q[:, at], k[:, at]) * HEAD_DIM ** (-0.5)
        s = jnp.where(live, s, -1e30)
        e = jnp.exp(s - jnp.max(s, axis=-1, keepdims=True))
        p = (e / jnp.sum(e, axis=-1, keepdims=True)).astype(BF16)
        mixed.append(dot(p, v[:, at]).astype(BF16))
    mixed = jnp.concatenate(mixed, axis=1)
    for turn, piece in zip(TURNS, pieces):
        t = dot_t(mixed, piece[3])
        for j, d in enumerate(TURNS):
            t3[blk(turn, d)] = t[:, j * 128:(j + 1) * 128]
    for i in range(16):
        at = slice(i * 128, (i + 1) * 128)
        out_mine[:, at] = t3[i, :rows, :].astype(out_mine.dtype)
        out_other[:, at] = t3[i, rows:, :].astype(out_other.dtype)


VMEM = pl.BlockSpec(memory_space=pltpu.VMEM)
SMEM = pl.BlockSpec(memory_space=pltpu.SMEM)


def sublayer(cross, cube, scal, gains, streams, mem, pieces):
    rows, width = streams[0].shape
    operands = [gains, *streams, *mem, *pieces]
    halves = tuple(jax.ShapeDtypeStruct((rows, width), kind) for kind in (F32, BF16))
    return pl.pallas_call(
        functools.partial(sublayer_kernel, cross, cube),
        out_shape=jax.ShapeDtypeStruct((2 * rows, width), BF16) if cross else halves,
        in_specs=[SMEM] + [VMEM] * len(operands),
        out_specs=VMEM if cross else (VMEM, VMEM),
        scratch_shapes=[
            pltpu.VMEM((16, 2 * rows, 128), BF16),
            pltpu.VMEM((16, 2 * rows, 128) if cross else (1, 16, 128), BF16),
            pltpu.VMEM((16, 2 * rows, 128), F32),
        ],
        compiler_params=pltpu.CompilerParams(vmem_limit_bytes=12 * 1024 * 1024),
        cost_estimate=pl.CostEstimate(
            flops=2 * 128 * 2048 * 512 * 4, bytes_accessed=9 * 2**20, transcendentals=65536
        ),
    )(scal, *operands)


def finish_kernel(scal, mine, other, in1m, in1o, in3m, in3o, early_m, early_o, own, got, out):
    rows = mine.shape[0]
    cube, core = scal[2], scal[6]
    even = (cube == 0) | (cube == 2)

    def put(doc0, doc1):
        out[0] = doc0[...]
        out[1] = doc1[...]

    @pl.when((core == 0) & even)
    def _():
        put(mine, other)

    @pl.when((core == 0) & (cube == 1))
    def _():
        put(in1m, in1o)

    @pl.when((core == 0) & (cube == 3))
    def _():
        put(in3m, in3o)

    @pl.when((core == 1) & (cube != 3))
    def _():
        put(early_o, early_m)

    @pl.when((core == 1) & (cube == 3))
    def _():
        at = lax.broadcasted_iota(jnp.int32, mine.shape, 0)
        low, high = slice(0, rows), slice(rows, 2 * rows)
        for slot, base, a, b, live in ((1, in3m, low, high, scal[7]), (0, in3o, high, low, scal[8])):
            term = own[a, :].astype(F32) + got[b, :].astype(F32)
            term = jnp.where(at < live, term, 0.0)
            out[slot] = (base[...].astype(F32) + term).astype(BF16)


def finish(scal, *parts):
    return pl.pallas_call(
        finish_kernel,
        out_shape=jax.ShapeDtypeStruct((2,) + parts[0].shape, BF16),
        in_specs=[SMEM] + [VMEM] * len(parts),
        out_specs=VMEM,
        compiler_params=pltpu.CompilerParams(vmem_limit_bytes=12 * 1024 * 1024),
    )(scal, *parts)


def turns(array, outer):
    return [array] + [exchange(array, outer, turn) for turn in TURNS[1:]]


def gather(weights):
    pair, depth, width = weights.shape[1:]
    halves = weights[0].reshape(pair, depth, 2, width // 2).transpose(2, 0, 1, 3)
    sent = jnp.broadcast_to(halves[:, None], (2, SIDE) + halves.shape[1:])
    sent = sent.reshape((2 * SIDE,) + halves.shape[1:])
    got = lax.all_to_all(sent, ("core", "zl"), 0, 0, tiled=True)
    got = got.reshape(2, SIDE, pair, depth, width // 2).transpose(0, 2, 1, 3, 4)
    got = got.reshape(2 * pair, SIDE * depth, width // 2)
    return turns(jnp.concatenate(turns(got, False), axis=1), True)


def on_device(encoder_embed, decoder_embed, section_weights, norm_gains, input_lengths, target_lengths):
    zh, core = lax.axis_index("zh"), lax.axis_index("core")
    y, x = lax.axis_index("y"), lax.axis_index("x")
    rows = encoder_embed.shape[1]
    encoder = zh < 2
    causal = zh == 2
    key_lengths = jnp.where(causal, target_lengths, input_lengths)
    row_lengths = jnp.where(encoder, input_lengths, target_lengths)
    scal = jnp.stack(
        [
            x,
            y,
            zh,
            causal.astype(jnp.int32),
            key_lengths[core],
            key_lengths[1 - core],
            core,
            row_lengths[core],
            row_lengths[1 - core],
        ]
    ).astype(jnp.int32)
    live = (jnp.arange(rows, dtype=jnp.int32) < row_lengths[core])[:, None]

    pieces = gather(section_weights)
    source = jnp.where(encoder, encoder_embed, decoder_embed)
    mine, other = source[core], source[1 - core]

    def added(stream, term, alive):
        return stream.astype(F32) + jnp.where(alive, term, 0.0)

    def swapped(array, cubes=range(SIDE)):
        pairs = [(2 * c + i, 2 * c + 1 - i) for c in cubes for i in range(2)]
        return lax.ppermute(array, SECTION, pairs)

    kept, sent = sublayer(False, None, scal, norm_gains, (mine, other), (), pieces)
    first = added(mine, kept + swapped(sent, (0, 2)).astype(F32), live).astype(BF16)
    in1 = lax.ppermute(first, "zh", [(0, 1)])
    in3 = lax.ppermute(first, "zh", [(2, 3)])
    in1_other = swapped(in1, (1,))
    kept, sent = sublayer(False, 1, scal, norm_gains, (in1, in1_other), (), pieces)
    second = added(in1, kept + swapped(sent, (1,)).astype(F32), live).astype(BF16)
    memory = rms(second.astype(F32), norm_gains[4:5])
    mem = lax.ppermute(memory, "zh", [(1, 3)])
    early = jnp.where(zh == 1, second, first)
    early_other = lax.ppermute(early, SECTION, [(0, 1), (2, 3), (4, 5)])
    in3_other = swapped(in3, (3,))
    mem_other = swapped(mem, (3,))
    own = sublayer(
        True, 3, scal, norm_gains, (in3, in3_other), (mem, mem_other), pieces
    )
    got = lax.ppermute(own, SECTION, [(6, 7)])
    out = finish(
        scal, mine, other, in1, in1_other, in3, in3_other, early, early_other, own, got
    )
    return out[None]


def solution(mesh):
    fine = Mesh(mesh.devices.reshape(SIDE, 2, SIDE, SIDE, SIDE), AXES)
    in_specs = (
        P(DP, None, None),
        P(DP, None, None),
        P(SECTION, None, DP, None),
        P(),
        P(DP),
        P(DP),
    )
    out_specs = P(SECTION, DP, None, None)
    return jax.shard_map(
        on_device, mesh=fine, in_specs=in_specs, out_specs=out_specs, check_vma=False
    )
```

```python
import functools
import itertools

import jax
import jax.numpy as jnp
from jax import lax
from jax.experimental import pallas as pl
from jax.experimental.pallas import tpu as pltpu
from jax.sharding import Mesh, PartitionSpec as P

HEAD_DIM = 128
SIDE = 4
TURNS = (0, 1, 3, 2)
FAR = 2
AXES = ("zh", "core", "y", "x", "zl")
DP = ("y", "x", "zl")
SECTION = ("zh", "core")
F32 = jnp.float32
BF16 = jnp.bfloat16


def place(zh, core, y, x, zl):
    return (((zh * 2 + core) * SIDE + y) * SIDE + x) * SIDE + zl


def exchange(array, outer, by):
    pairs = []
    for zh, core, y, x, zl in itertools.product(*map(range, (SIDE, 2, SIDE, SIDE, SIDE))):
        along_y = outer == (core == 0)
        to = (y ^ by, x) if along_y else (y, x ^ by)
        pairs.append((place(zh, core, y, x, zl), place(zh, core, *to, zl)))
    return lax.ppermute(array, AXES, pairs)


def dot(a, b):
    return jnp.dot(a, b, preferred_element_type=F32)


def dot_t(a, b):
    return lax.dot_general(a, b, (((1,), (1,)), ((), ())), preferred_element_type=F32)


def rms(values, gain):
    mean_square = jnp.mean(values * values, axis=-1, keepdims=True)
    return (values * lax.rsqrt(mean_square + 1e-06) * gain).astype(BF16)


def block_at(scal, outer, inner):
    back = scal[6] == 1
    dy, dx = jnp.where(back, inner, outer), jnp.where(back, outer, inner)
    return lax.bitwise_xor(scal[1], dy) * SIDE + lax.bitwise_xor(scal[0], dx)


def weight(pieces, turn, which):
    chunk, place_in = divmod(which, 2)
    if turn == FAR:
        return pieces[6 + which][0]
    return pieces[2 * TURNS.index(turn) + chunk][place_in]


def put_norm(scal, gains, streams, h3):
    rows = streams[0].shape[0]
    gain = gains[pl.ds(scal[2], 1), :]
    for part, ref in enumerate(streams):
        h = rms(ref[...].astype(F32), gain)
        for i in range(16):
            h3[i, part * rows:(part + 1) * rows, :] = h[:, i * 128:(i + 1) * 128]


def put_memory(mem, m3):
    rows = mem[0].shape[0]
    for part, ref in enumerate(mem):
        for i in range(16):
            m3[i, part * rows:(part + 1) * rows, :] = ref[:, i * 128:(i + 1) * 128]


def project(scal, h3, pieces, turns, which, totals=None):
    totals = [None] * len(which) if totals is None else list(totals)
    for turn in turns:
        h = jnp.concatenate([h3[block_at(scal, turn, d)] for d in TURNS], axis=1)
        for i, m in enumerate(which):
            term = dot(h, weight(pieces, turn, m))
            totals[i] = term if totals[i] is None else totals[i] + term
    return totals


def attend(scal, q, k, v):
    q, k, v = q.astype(BF16), k.astype(BF16), v.astype(BF16)
    count = q.shape[0]
    rows = count // 2
    r = lax.broadcasted_iota(jnp.int32, (count, count), 0)
    c = lax.broadcasted_iota(jnp.int32, (count, count), 1)
    first = c < rows
    live = (r < rows) == first
    key_at = jnp.where(first, c, c - rows)
    live = live & (key_at < jnp.where(first, scal[4], scal[5]))
    live = live & ((c <= r) | (scal[3] == 0))
    mixed = []
    for head in range(4):
        at = slice(head * HEAD_DIM, (head + 1) * HEAD_DIM)
        s = dot_t(q[:, at], k[:, at]) * HEAD_DIM ** (-0.5)
        s = jnp.where(live, s, -1e30)
        e = jnp.exp(s - jnp.max(s, axis=-1, keepdims=True))
        p = (e / jnp.sum(e, axis=-1, keepdims=True)).astype(BF16)
        mixed.append(dot(p, v[:, at]).astype(BF16))
    return jnp.concatenate(mixed, axis=1)


def project_out(scal, mixed, pieces, t3, out_mine, out_other):
    rows = out_mine.shape[0]
    for turn in TURNS:
        t = dot_t(mixed, weight(pieces, turn, 3))
        for j, d in enumerate(TURNS):
            t3[block_at(scal, turn, d)] = t[:, j * 128:(j + 1) * 128]
    for i in range(16):
        at = slice(i * 128, (i + 1) * 128)
        out_mine[:, at] = t3[i, :rows, :].astype(out_mine.dtype)
        out_other[:, at] = t3[i, rows:, :].astype(out_other.dtype)


def early_kernel(scal, gains, mine, other, *refs):
    pieces, (h3, q, k, v) = refs[:6], refs[6:]

    @pl.when(lax.rem(scal[2], 2) == 0)
    def _():
        put_norm(scal, gains, (mine, other), h3)
        q[...], k[...], v[...] = project(scal, h3, pieces, TURNS[:3], (0, 1, 2))


def first_kernel(scal, h3, q, k, v, *refs):
    pieces, (out_mine, out_other, t3) = refs[:10], refs[10:]

    @pl.when(lax.rem(scal[2], 2) == 0)
    def _():
        done = (q[...], k[...], v[...])
        done = project(scal, h3, pieces, TURNS[3:], (0, 1, 2), done)
        project_out(scal, attend(scal, *done), pieces, t3, out_mine, out_other)


def second_kernel(scal, gains, mine, other, *refs):
    pieces, (out_mine, out_other, h3, t3) = refs[:10], refs[10:]

    @pl.when(scal[2] == 1)
    def _():
        put_norm(scal, gains, (mine, other), h3)
        done = project(scal, h3, pieces, TURNS, (0, 1, 2))
        project_out(scal, attend(scal, *done), pieces, t3, out_mine, out_other)


def query_kernel(scal, gains, mine, other, *refs):
    pieces, (q, h3) = refs[:10], refs[10:]

    @pl.when(scal[2] == 3)
    def _():
        put_norm(scal, gains, (mine, other), h3)
        q[...] = project(scal, h3, pieces, TURNS, (0,))[0].astype(BF16)


def third_kernel(scal, q, mem_mine, mem_other, *refs):
    pieces, (out, m3, t3) = refs[:10], refs[10:]

    @pl.when(scal[2] == 3)
    def _():
        rows = mem_mine.shape[0]
        put_memory((mem_mine, mem_other), m3)
        k, v = project(scal, m3, pieces, TURNS, (1, 2))
        mixed = attend(scal, q[...], k, v)
        project_out(scal, mixed, pieces, t3, out.at[:rows], out.at[rows:])


VMEM = pl.BlockSpec(memory_space=pltpu.VMEM)
SMEM = pl.BlockSpec(memory_space=pltpu.SMEM)


def call(kernel, scal, operands, outs, scratch=(), flops=0):
    size = sum(a.size * a.dtype.itemsize for a in operands)
    return pl.pallas_call(
        kernel,
        out_shape=outs,
        in_specs=[SMEM] + [VMEM] * len(operands),
        out_specs=jax.tree.map(lambda _: VMEM, outs),
        scratch_shapes=[pltpu.VMEM(shape, kind) for shape, kind in scratch],
        compiler_params=pltpu.CompilerParams(vmem_limit_bytes=12 * 1024 * 1024),
        cost_estimate=pl.CostEstimate(flops=flops, bytes_accessed=size, transcendentals=0),
    )(scal, *operands)


def finish_kernel(scal, mine, other, in1m, in1o, in3m, in3o, early_m, early_o, own, got, out):
    rows = mine.shape[0]
    cube, core = scal[2], scal[6]
    even = (cube == 0) | (cube == 2)

    def put(doc0, doc1):
        out[0] = doc0[...]
        out[1] = doc1[...]

    @pl.when((core == 0) & even)
    def _():
        put(mine, other)

    @pl.when((core == 0) & (cube == 1))
    def _():
        put(in1m, in1o)

    @pl.when((core == 0) & (cube == 3))
    def _():
        put(in3m, in3o)

    @pl.when((core == 1) & (cube != 3))
    def _():
        put(early_o, early_m)

    @pl.when((core == 1) & (cube == 3))
    def _():
        at = lax.broadcasted_iota(jnp.int32, mine.shape, 0)
        low, high = slice(0, rows), slice(rows, 2 * rows)
        for slot, base, a, b, live in ((1, in3m, low, high, scal[7]), (0, in3o, high, low, scal[8])):
            term = own[a, :].astype(F32) + got[b, :].astype(F32)
            term = jnp.where(at < live, term, 0.0)
            out[slot] = (base[...].astype(F32) + term).astype(BF16)


def turns(array, outer):
    return [array] + [exchange(array, outer, turn) for turn in TURNS[1:]]


def gather(weights):
    pair, depth, width = weights.shape[1:]
    halves = weights[0].reshape(pair, depth, 2, width // 2).transpose(2, 0, 1, 3)
    sent = jnp.broadcast_to(halves[:, None], (2, SIDE) + halves.shape[1:])
    sent = sent.reshape((2 * SIDE,) + halves.shape[1:])
    got = lax.all_to_all(sent, ("core", "zl"), 0, 0, tiled=True)
    got = got.reshape(2, SIDE, pair, depth, width // 2).transpose(0, 2, 1, 3, 4)
    got = got.reshape(2 * pair, SIDE * depth, width // 2)
    near = turns(got, False)
    chunks = [jnp.concatenate([a[i:i + pair] for a in near], axis=1) for i in (0, pair)]
    by1 = [exchange(a, True, 1) for a in chunks]
    by3 = [exchange(a, True, 3) for a in chunks]
    far = []
    for a, b in zip(by1, by3):
        far += [exchange(b[:1], True, 1), exchange(a[1:], True, 3)]
    return [*chunks, *by1, *by3], far


def on_device(encoder_embed, decoder_embed, section_weights, norm_gains, input_lengths, target_lengths):
    zh, core = lax.axis_index("zh"), lax.axis_index("core")
    y, x = lax.axis_index("y"), lax.axis_index("x")
    rows = encoder_embed.shape[1]
    encoder = zh < 2
    causal = zh == 2
    key_lengths = jnp.where(causal, target_lengths, input_lengths)
    row_lengths = jnp.where(encoder, input_lengths, target_lengths)
    scal = jnp.stack(
        [
            x,
            y,
            zh,
            causal.astype(jnp.int32),
            key_lengths[core],
            key_lengths[1 - core],
            core,
            row_lengths[core],
            row_lengths[1 - core],
        ]
    ).astype(jnp.int32)
    live = (jnp.arange(rows, dtype=jnp.int32) < row_lengths[core])[:, None]

    near, far = gather(section_weights)
    pieces = near + far
    source = jnp.where(encoder, encoder_embed, decoder_embed)
    mine, other = source[core], source[1 - core]

    def added(stream, term, alive):
        return stream.astype(F32) + jnp.where(alive, term, 0.0)

    def swapped(array, cubes=range(SIDE)):
        pairs = [(2 * c + i, 2 * c + 1 - i) for c in cubes for i in range(2)]
        return lax.ppermute(array, SECTION, pairs)

    count, width = 2 * rows, mine.shape[1]
    half = near[0].shape[-1]
    blocks = (16, count, 128)
    work = 2 * count * width * half
    wide = jax.ShapeDtypeStruct((count, width), BF16)
    halves = tuple(jax.ShapeDtypeStruct((rows, width), kind) for kind in (F32, BF16))
    total = jax.ShapeDtypeStruct((count, half), F32)
    narrow = jax.ShapeDtypeStruct((count, half), BF16)

    started = call(
        early_kernel,
        scal,
        [norm_gains, mine, other, *near],
        (jax.ShapeDtypeStruct(blocks, BF16), total, total, total),
        (),
        3 * work,
    )
    kept, sent = call(
        first_kernel, scal, [*started, *pieces], halves, [(blocks, F32)], 2 * work
    )
    first = added(mine, kept + swapped(sent, (0, 2)).astype(F32), live).astype(BF16)
    in1 = lax.ppermute(first, "zh", [(0, 1)])
    in3 = lax.ppermute(first, "zh", [(2, 3)])
    in1_other = swapped(in1, (1,))
    kept, sent = call(
        second_kernel,
        scal,
        [norm_gains, in1, in1_other, *pieces],
        halves,
        [(blocks, BF16), (blocks, F32)],
        4 * work,
    )
    second = added(in1, kept + swapped(sent, (1,)).astype(F32), live).astype(BF16)
    memory = rms(second.astype(F32), norm_gains[4:5])
    mem = lax.ppermute(memory, "zh", [(1, 3)])
    early = jnp.where(zh == 1, second, first)
    early_other = lax.ppermute(early, SECTION, [(0, 1), (2, 3), (4, 5)])
    in3_other = swapped(in3, (3,))
    query = call(
        query_kernel, scal, [norm_gains, in3, in3_other, *pieces], narrow, [(blocks, BF16)], work
    )
    mem_other = swapped(mem, (3,))
    own = call(
        third_kernel,
        scal,
        [query, mem, mem_other, *pieces],
        wide,
        [(blocks, BF16), (blocks, F32)],
        3 * work,
    )
    got = lax.ppermute(own, SECTION, [(6, 7)])
    parts = [mine, other, in1, in1_other, in3, in3_other, early, early_other, own, got]
    out = call(finish_kernel, scal, parts, jax.ShapeDtypeStruct((2, rows, width), BF16))
    return out[None]


def solution(mesh):
    fine = Mesh(mesh.devices.reshape(SIDE, 2, SIDE, SIDE, SIDE), AXES)
    in_specs = (
        P(DP, None, None),
        P(DP, None, None),
        P(SECTION, None, DP, None),
        P(),
        P(DP),
        P(DP),
    )
    out_specs = P(SECTION, DP, None, None)
    return jax.shard_map(
        on_device, mesh=fine, in_specs=in_specs, out_specs=out_specs, check_vma=False
    )
```

```python
import itertools

import jax
import jax.numpy as jnp
from jax import lax
from jax.experimental import pallas as pl
from jax.experimental.pallas import tpu as pltpu
from jax.sharding import Mesh, PartitionSpec as P

HEAD_DIM = 128
SIDE = 4
TURNS = (0, 1, 3, 2)
FAR = 2
AXES = ("zh", "core", "y", "x", "zl")
DP = ("y", "x", "zl")
SECTION = ("zh", "core")
F32 = jnp.float32
BF16 = jnp.bfloat16
VMEM = pl.BlockSpec(memory_space=pltpu.VMEM)
SMEM = pl.BlockSpec(memory_space=pltpu.SMEM)
BLOCKS = 16
LANES = 128
TILE = 256
ROWS = 32
X, Y, CUBE, CAUSAL, KEYS, CORE, LIVE = 0, 1, 2, 3, 4, 6, 7


def place(zh, core, y, x, zl):
    return (((zh * 2 + core) * SIDE + y) * SIDE + x) * SIDE + zl


def exchange(array, outer, by):
    pairs = []
    for zh, core, y, x, zl in itertools.product(*map(range, (SIDE, 2, SIDE, SIDE, SIDE))):
        along_y = outer == (core == 0)
        to = (y ^ by, x) if along_y else (y, x ^ by)
        pairs.append((place(zh, core, y, x, zl), place(zh, core, *to, zl)))
    return lax.ppermute(array, AXES, pairs)


def turns(array, outer):
    return [array] + [exchange(array, outer, turn) for turn in TURNS[1:]]


def dot(a, b):
    return jnp.dot(a, b, preferred_element_type=F32)


def dot_t(a, b):
    return lax.dot_general(a, b, (((1,), (1,)), ((), ())), preferred_element_type=F32)


def rms(values, gain):
    mean_square = jnp.mean(values * values, axis=-1, keepdims=True)
    return (values * lax.rsqrt(mean_square + 1e-06) * gain).astype(BF16)


def lanes(i):
    return slice(i * LANES, (i + 1) * LANES)


def span(i, size):
    return pl.ds(pl.multiple_of(i * size, size), size)


def loop(count, body):
    lax.fori_loop(0, count, lambda i, carry: (body(i), carry)[1], 0)


def block_at(scal, outer, inner):
    back = scal[CORE] == 1
    dy, dx = jnp.where(back, inner, outer), jnp.where(back, outer, inner)
    return lax.bitwise_xor(scal[Y], dy) * SIDE + lax.bitwise_xor(scal[X], dx)


def inner_turns(half):
    return 3 * half, 1 + half


def weight(pieces, turn, which):
    chunk, at = divmod(which, 2)
    if turn == FAR:
        return pieces[6 + which], 0
    return pieces[2 * TURNS.index(turn) + chunk], at


def put_blocks(h3, rows, h):
    for i in range(BLOCKS):
        h3[i, rows, :] = h[:, lanes(i)]


def project(scal, h3, pieces, spots, which, total):
    def tile(n):
        cols = span(n, TILE)
        sums = [None] * len(which)
        for turn in spots:
            for half in range(2):
                h = jnp.concatenate([h3[block_at(scal, turn, d)] for d in inner_turns(half)], axis=1)
                for i, m in enumerate(which):
                    ref, at = weight(pieces, turn, m)
                    term = dot(h, ref[at, half * TILE:(half + 1) * TILE, cols])
                    sums[i] = term if sums[i] is None else sums[i] + term
        for i, m in enumerate(which):
            total[m, :, cols] = sums[i]

    loop(2, tile)


def attend(scal, q_at, k_at, v_at, mixed):
    count = mixed.shape[0]
    rows = count // 2
    r = lax.broadcasted_iota(jnp.int32, (count, count), 0)
    c = lax.broadcasted_iota(jnp.int32, (count, count), 1)
    first = c < rows
    live = (r < rows) == first
    live = live & (jnp.where(first, c, c - rows) < jnp.where(first, scal[KEYS], scal[KEYS + 1]))
    live = live & ((c <= r) | (scal[CAUSAL] == 0))

    def pair(step):
        for side in range(2):
            at = span(step * 2 + side, LANES)
            s = dot_t(q_at(at), k_at(at)) * HEAD_DIM ** (-0.5)
            s = jnp.where(live, s, -1e30)
            e = jnp.exp(s - jnp.max(s, axis=-1, keepdims=True))
            p = (e / jnp.sum(e, axis=-1, keepdims=True)).astype(BF16)
            mixed[:, at] = dot(p, v_at(at)).astype(BF16)

    loop(2, pair)


def project_out(scal, mixed, spots, t3):
    def tile(half):
        rows = span(half, TILE)
        for turn, (ref, at) in zip(TURNS, spots):
            t = dot_t(mixed[...], ref[at, rows, :])
            for j, d in enumerate(inner_turns(half)):
                t3[block_at(scal, turn, d)] = t[:, lanes(j)]

    loop(2, tile)


def put_out(t3, rows, out):
    def block(i):
        out[:, span(i, LANES)] = t3[i, rows, :].astype(out.dtype)

    loop(BLOCKS, block)


def doc_rows(scal, rows):
    return span(scal[CORE], rows), span(1 - scal[CORE], rows)


def outs_at(pieces):
    return [weight(pieces, turn, 3) for turn in TURNS]


def put_norm(scal, gains, parts, h3):
    gain = gains[pl.ds(scal[CUBE], 1), :]
    for ref, first in parts:

        def chunk(i, ref=ref, first=first):
            h = rms(ref[span(i, ROWS), :].astype(F32), gain)
            to = pl.ds(pl.multiple_of(first + i * ROWS, ROWS), ROWS)
            put_blocks(h3, to, h)

        loop(ref.shape[0] // ROWS, chunk)


def doc_parts(scal, mine, other):
    rows = mine.shape[0]
    return (mine, scal[CORE] * rows), (other, (1 - scal[CORE]) * rows)


def put_halves(scal, t3, mine, other):
    here, there = doc_rows(scal, mine.shape[0])
    put_out(t3, here, mine)
    put_out(t3, there, other)


def early_kernel(scal, gains, base, *refs):
    pieces, (h3, total) = refs[:6], refs[6:]

    @pl.when(lax.rem(scal[CUBE], 2) == 0)
    def _():
        put_norm(scal, gains, [(base, 0)], h3)
        project(scal, h3, pieces, TURNS[:3], (0, 1, 2), total)


def first_kernel(scal, h3, early, *refs):
    pieces, (mine, other, total, mixed, t3) = refs[:10], refs[10:]

    @pl.when(lax.rem(scal[CUBE], 2) == 0)
    def _():
        project(scal, h3, pieces, (FAR,), (0, 1, 2), total)

        def read(m):
            return lambda at: (total[m, :, at] + early[m, :, at]).astype(BF16)

        attend(scal, read(0), read(1), read(2), mixed)
        project_out(scal, mixed, outs_at(pieces), t3)
        put_halves(scal, t3, mine, other)


def second_kernel(scal, gains, in_mine, in_other, *refs):
    pieces, (mine, other, h3, total, mixed, t3) = refs[:10], refs[10:]

    @pl.when(scal[CUBE] == 1)
    def _():
        put_norm(scal, gains, doc_parts(scal, in_mine, in_other), h3)
        project(scal, h3, pieces, TURNS, (0, 1, 2), total)

        def read(m):
            return lambda at: total[m, :, at].astype(BF16)

        attend(scal, read(0), read(1), read(2), mixed)
        project_out(scal, mixed, outs_at(pieces), t3)
        put_halves(scal, t3, mine, other)


def query_kernel(scal, gains, in_mine, in_other, *refs):
    pieces, (query, h3, total) = refs[:10], refs[10:]

    @pl.when(scal[CUBE] == 3)
    def _():
        put_norm(scal, gains, doc_parts(scal, in_mine, in_other), h3)
        project(scal, h3, pieces, TURNS, (0,), total)
        query[...] = total[0].astype(BF16)


def third_kernel(scal, query, mem_mine, mem_other, *refs):
    pieces, (part, m3, total, mixed, t3) = refs[:10], refs[10:]

    @pl.when(scal[CUBE] == 3)
    def _():
        here, there = doc_rows(scal, mem_mine.shape[0])

        def block(i):
            m3[i, here, :] = mem_mine[:, span(i, LANES)]
            m3[i, there, :] = mem_other[:, span(i, LANES)]

        loop(BLOCKS, block)
        project(scal, m3, pieces, TURNS, (1, 2), total)

        def read(m):
            return lambda at: total[m, :, at].astype(BF16)

        attend(scal, lambda at: query[:, at], read(1), read(2), mixed)
        project_out(scal, mixed, outs_at(pieces), t3)
        put_out(t3, slice(None), part)


def finish_kernel(scal, base, in1m, in1o, in3m, in3o, early, early_other, own, got, out):
    rows = early.shape[0]
    cube, core = scal[CUBE], scal[CORE]
    odd = lax.rem(cube, 2) == 1
    low, high = slice(0, rows), slice(rows, 2 * rows)

    @pl.when((core == 0) & jnp.logical_not(odd))
    def _():
        out[...] = base[...]

    for at, one, two in ((1, in1m, in1o), (3, in3m, in3o)):

        @pl.when((core == 0) & (cube == at))
        def _(one=one, two=two):
            out[low, :] = one[...]
            out[high, :] = two[...]

    @pl.when((core == 1) & (cube != 3))
    def _():
        out[low, :] = early_other[...]
        out[high, :] = early[...]

    @pl.when((core == 1) & (cube == 3))
    def _():
        at = lax.broadcasted_iota(jnp.int32, early.shape, 0)
        for doc, here, stream in ((0, low, in3o), (1, high, in3m)):
            term = own[here, :].astype(F32) + got[here, :].astype(F32)
            term = jnp.where(at < scal[LIVE + doc], term, 0.0)
            out[here, :] = (stream[...].astype(F32) + term).astype(BF16)


def call(kernel, scal, operands, outs, scratch=(), flops=0):
    size = sum(a.size * a.dtype.itemsize for a in operands)
    return pl.pallas_call(
        kernel,
        out_shape=outs,
        in_specs=[SMEM] + [VMEM] * len(operands),
        out_specs=jax.tree.map(lambda _: VMEM, outs),
        scratch_shapes=[pltpu.VMEM(shape, kind) for shape, kind in scratch],
        compiler_params=pltpu.CompilerParams(vmem_limit_bytes=12 * 1024 * 1024),
        cost_estimate=pl.CostEstimate(flops=flops, bytes_accessed=size, transcendentals=0),
    )(scal, *operands)


def gather(weights):
    pair, depth, width = weights.shape[1:]
    halves = weights[0].reshape(pair, depth, 2, width // 2).transpose(2, 0, 1, 3)
    sent = jnp.broadcast_to(halves[:, None], (2, SIDE) + halves.shape[1:])
    sent = sent.reshape((2 * SIDE,) + halves.shape[1:])
    got = lax.all_to_all(sent, ("core", "zl"), 0, 0, tiled=True)
    got = got.reshape(2, SIDE, pair, depth, width // 2).transpose(0, 2, 1, 3, 4)
    got = got.reshape(2 * pair, SIDE * depth, width // 2)
    near = turns(got, False)
    chunks = [jnp.concatenate([a[i:i + pair] for a in near], axis=1) for i in (0, pair)]
    by1 = [exchange(a, True, 1) for a in chunks]
    by3 = [exchange(a, True, 3) for a in chunks]
    far = []
    for a, b in zip(by1, by3):
        far += [exchange(b[:1], True, 1), exchange(a[1:], True, 3)]
    return [*chunks, *by1, *by3], far


def on_device(encoder_embed, decoder_embed, section_weights, norm_gains, input_lengths, target_lengths):
    zh, core = lax.axis_index("zh"), lax.axis_index("core")
    y, x = lax.axis_index("y"), lax.axis_index("x")
    docs, rows, width = encoder_embed.shape
    count = docs * rows
    encoder = zh < 2
    causal = zh == 2
    key_lengths = jnp.where(causal, target_lengths, input_lengths)
    row_lengths = jnp.where(encoder, input_lengths, target_lengths)
    scal = jnp.stack(
        [x, y, zh, causal.astype(jnp.int32), key_lengths[0], key_lengths[1], core]
        + [row_lengths[0], row_lengths[1]]
    ).astype(jnp.int32)
    base = jnp.where(encoder, encoder_embed, decoder_embed).reshape(count, width)
    near, far = gather(section_weights)
    pieces = near + far

    def swapped(array, cubes):
        pairs = [(2 * c + i, 2 * c + 1 - i) for c in cubes for i in range(2)]
        return lax.ppermute(array, SECTION, pairs)

    half = near[0].shape[-1]
    blocks = (BLOCKS, count, LANES)
    totals = (3, count, half)
    work = 2 * count * width * half
    wide = jax.ShapeDtypeStruct((count, width), BF16)
    narrow = jax.ShapeDtypeStruct((count, half), BF16)
    halves = tuple(jax.ShapeDtypeStruct((rows, width), kind) for kind in (F32, BF16))
    rest = [(totals, F32), ((count, half), BF16), (blocks, F32)]
    own_doc = lax.dynamic_slice(base, (core * rows, 0), (rows, width))
    live = (jnp.arange(rows, dtype=jnp.int32) < row_lengths[core])[:, None]

    def added(stream, kept, sent, cubes):
        term = kept + swapped(sent, cubes).astype(F32)
        return (stream.astype(F32) + jnp.where(live, term, 0.0)).astype(BF16)

    h3, early = call(
        early_kernel,
        scal,
        [norm_gains, base, *near],
        (jax.ShapeDtypeStruct(blocks, BF16), jax.ShapeDtypeStruct(totals, F32)),
        (),
        3 * work,
    )
    kept, sent = call(first_kernel, scal, [h3, early, *pieces], halves, rest, 2 * work)
    first = added(own_doc, kept, sent, (0, 2))
    in1 = lax.ppermute(first, "zh", [(0, 1)])
    in3 = lax.ppermute(first, "zh", [(2, 3)])
    in1_other = swapped(in1, (1,))
    kept, sent = call(
        second_kernel,
        scal,
        [norm_gains, in1, in1_other, *pieces],
        halves,
        [(blocks, BF16), *rest],
        4 * work,
    )
    second = added(in1, kept, sent, (1,))
    memory = rms(second.astype(F32), norm_gains[4:5])
    mem = lax.ppermute(memory, "zh", [(1, 3)])
    early_doc = jnp.where(zh == 1, second, first)
    early_other = lax.ppermute(early_doc, SECTION, [(0, 1), (2, 3), (4, 5)])
    in3_other = swapped(in3, (3,))
    query = call(
        query_kernel,
        scal,
        [norm_gains, in3, in3_other, *pieces],
        narrow,
        [(blocks, BF16), (totals, F32)],
        work,
    )
    mem_other = swapped(mem, (3,))
    own = call(
        third_kernel, scal, [query, mem, mem_other, *pieces], wide, [(blocks, BF16), *rest], 3 * work
    )
    got = lax.ppermute(own, SECTION, [(6, 7)])
    parts = [base, in1, in1_other, in3, in3_other, early_doc, early_other, own, got]
    out = call(finish_kernel, scal, parts, wide)
    return out.reshape(1, docs, rows, width)


def solution(mesh):
    fine = Mesh(mesh.devices.reshape(SIDE, 2, SIDE, SIDE, SIDE), AXES)
    in_specs = (
        P(DP, None, None),
        P(DP, None, None),
        P(SECTION, None, DP, None),
        P(),
        P(DP),
        P(DP),
    )
    out_specs = P(SECTION, DP, None, None)
    return jax.shard_map(
        on_device, mesh=fine, in_specs=in_specs, out_specs=out_specs, check_vma=False
    )
```

```python
import functools
import itertools

import jax
import jax.numpy as jnp
from jax import lax
from jax.experimental import pallas as pl
from jax.experimental.pallas import tpu as pltpu
from jax.sharding import Mesh, PartitionSpec as P

HEAD_DIM = 128
SIDE = 4
TURNS = (0, 1, 3, 2)
FAR = 2
AXES = ("zh", "core", "y", "x", "zl")
DP = ("y", "x", "zl")
SECTION = ("zh", "core")
F32 = jnp.float32
BF16 = jnp.bfloat16


def place(zh, core, y, x, zl):
    return (((zh * 2 + core) * SIDE + y) * SIDE + x) * SIDE + zl


def exchange(array, outer, by):
    pairs = []
    for zh, core, y, x, zl in itertools.product(*map(range, (SIDE, 2, SIDE, SIDE, SIDE))):
        along_y = outer == (core == 0)
        to = (y ^ by, x) if along_y else (y, x ^ by)
        pairs.append((place(zh, core, y, x, zl), place(zh, core, *to, zl)))
    return lax.ppermute(array, AXES, pairs)


def dot(a, b):
    return jnp.dot(a, b, preferred_element_type=F32)


def dot_t(a, b):
    return lax.dot_general(a, b, (((1,), (1,)), ((), ())), preferred_element_type=F32)


def rms(values, gain):
    mean_square = jnp.mean(values * values, axis=-1, keepdims=True)
    return (values * lax.rsqrt(mean_square + 1e-06) * gain).astype(BF16)


def block_at(scal, outer, inner):
    back = scal[6] == 1
    dy, dx = jnp.where(back, inner, outer), jnp.where(back, outer, inner)
    return lax.bitwise_xor(scal[1], dy) * SIDE + lax.bitwise_xor(scal[0], dx)


def weight(pieces, turn, which):
    chunk, at = divmod(which, 2)
    if turn == FAR:
        return pieces[8].at[at] if chunk else pieces[6 + which].at[0]
    return pieces[2 * TURNS.index(turn) + chunk].at[at]


class Fetched:
    def __init__(self, pieces, wanted, space, sems):
        self.space = space
        self.copies = {}
        self.slots = {}
        for slot, key in enumerate(wanted):
            copy = pltpu.make_async_copy(weight(pieces, *key), space.at[slot], sems.at[slot])
            copy.start()
            self.copies[key], self.slots[key] = copy, slot

    def take(self, turn, which):
        self.copies[turn, which].wait()
        return self.space[self.slots[turn, which]]


def wanted(spots, which, out=True):
    keys = [(turn, m) for turn in spots for m in which]
    return keys + [(turn, 3) for turn in TURNS] * out


def put_norm(scal, gains, streams, h3):
    rows = streams[0].shape[0]
    gain = gains[pl.ds(scal[2], 1), :]
    for part, ref in enumerate(streams):
        h = rms(ref[...].astype(F32), gain)
        for i in range(16):
            h3[i, part * rows:(part + 1) * rows, :] = h[:, i * 128:(i + 1) * 128]


def put_memory(mem, m3):
    rows = mem[0].shape[0]
    for part, ref in enumerate(mem):
        for i in range(16):
            m3[i, part * rows:(part + 1) * rows, :] = ref[:, i * 128:(i + 1) * 128]


def project(scal, h3, fetched, turns, which, totals=None):
    totals = [None] * len(which) if totals is None else list(totals)
    for turn in turns:
        h = jnp.concatenate([h3[block_at(scal, turn, d)] for d in TURNS], axis=1)
        for i, m in enumerate(which):
            term = dot(h, fetched.take(turn, m))
            totals[i] = term if totals[i] is None else totals[i] + term
    return totals


def attend(scal, q, k, v):
    q, k, v = q.astype(BF16), k.astype(BF16), v.astype(BF16)
    count = q.shape[0]
    rows = count // 2
    r = lax.broadcasted_iota(jnp.int32, (count, count), 0)
    c = lax.broadcasted_iota(jnp.int32, (count, count), 1)
    first = c < rows
    live = (r < rows) == first
    key_at = jnp.where(first, c, c - rows)
    live = live & (key_at < jnp.where(first, scal[4], scal[5]))
    live = live & ((c <= r) | (scal[3] == 0))
    mixed = []
    for head in range(4):
        at = slice(head * HEAD_DIM, (head + 1) * HEAD_DIM)
        s = dot_t(q[:, at], k[:, at]) * HEAD_DIM ** (-0.5)
        s = jnp.where(live, s, -1e30)
        e = jnp.exp(s - jnp.max(s, axis=-1, keepdims=True))
        p = (e / jnp.sum(e, axis=-1, keepdims=True)).astype(BF16)
        mixed.append(dot(p, v[:, at]).astype(BF16))
    return jnp.concatenate(mixed, axis=1)


def project_out(scal, mixed, fetched, t3, out_mine, out_other):
    rows = out_mine.shape[0]
    for turn in TURNS:
        t = dot_t(mixed, fetched.take(turn, 3))
        for j, d in enumerate(TURNS):
            t3[block_at(scal, turn, d)] = t[:, j * 128:(j + 1) * 128]
    for i in range(16):
        at = slice(i * 128, (i + 1) * 128)
        out_mine[:, at] = t3[i, :rows, :].astype(out_mine.dtype)
        out_other[:, at] = t3[i, rows:, :].astype(out_other.dtype)


EARLY = wanted(TURNS[:3], (0, 1, 2), False)
FIRST = wanted(TURNS[3:], (0, 1, 2))
SECOND = wanted(TURNS, (0, 1, 2))
QUERY = wanted(TURNS, (0,), False)
THIRD = wanted(TURNS, (1, 2))


def early_kernel(scal, gains, mine, other, *refs):
    pieces, (h3, q, k, v, space, sems) = refs[:6], refs[6:]

    @pl.when(lax.rem(scal[2], 2) == 0)
    def _():
        fetched = Fetched(pieces, EARLY, space, sems)
        put_norm(scal, gains, (mine, other), h3)
        q[...], k[...], v[...] = project(scal, h3, fetched, TURNS[:3], (0, 1, 2))


def first_kernel(scal, h3, q, k, v, *refs):
    pieces, (out_mine, out_other, t3, space, sems) = refs[:9], refs[9:]

    @pl.when(lax.rem(scal[2], 2) == 0)
    def _():
        fetched = Fetched(pieces, FIRST, space, sems)
        done = (q[...], k[...], v[...])
        done = project(scal, h3, fetched, TURNS[3:], (0, 1, 2), done)
        project_out(scal, attend(scal, *done), fetched, t3, out_mine, out_other)


def second_kernel(scal, gains, mine, other, *refs):
    pieces, (out_mine, out_other, h3, t3, space, sems) = refs[:9], refs[9:]

    @pl.when(scal[2] == 1)
    def _():
        fetched = Fetched(pieces, SECOND, space, sems)
        put_norm(scal, gains, (mine, other), h3)
        done = project(scal, h3, fetched, TURNS, (0, 1, 2))
        project_out(scal, attend(scal, *done), fetched, t3, out_mine, out_other)


def query_kernel(scal, gains, mine, other, *refs):
    pieces, (q, h3, space, sems) = refs[:9], refs[9:]

    @pl.when(scal[2] == 3)
    def _():
        fetched = Fetched(pieces, QUERY, space, sems)
        put_norm(scal, gains, (mine, other), h3)
        q[...] = project(scal, h3, fetched, TURNS, (0,))[0].astype(BF16)


def third_kernel(scal, q, mem_mine, mem_other, *refs):
    pieces, (out, m3, t3, space, sems) = refs[:9], refs[9:]

    @pl.when(scal[2] == 3)
    def _():
        rows = mem_mine.shape[0]
        fetched = Fetched(pieces, THIRD, space, sems)
        put_memory((mem_mine, mem_other), m3)
        k, v = project(scal, m3, fetched, TURNS, (1, 2))
        mixed = attend(scal, q[...], k, v)
        project_out(scal, mixed, fetched, t3, out.at[:rows], out.at[rows:])


VMEM = pl.BlockSpec(memory_space=pltpu.VMEM)
SMEM = pl.BlockSpec(memory_space=pltpu.SMEM)
ANY = pl.BlockSpec(memory_space=pl.ANY)


def call(kernel, scal, operands, outs, scratch=(), pieces=(), fetches=0, flops=0):
    size = sum(a.size * a.dtype.itemsize for a in [*operands, *pieces])
    shapes = [pltpu.VMEM(shape, kind) for shape, kind in scratch]
    if fetches:
        shapes.append(pltpu.VMEM((fetches,) + pieces[0].shape[1:], BF16))
        shapes.append(pltpu.SemaphoreType.DMA((fetches,)))
    return pl.pallas_call(
        kernel,
        out_shape=outs,
        in_specs=[SMEM] + [VMEM] * len(operands) + [ANY] * len(pieces),
        out_specs=jax.tree.map(lambda _: VMEM, outs),
        scratch_shapes=shapes,
        compiler_params=pltpu.CompilerParams(vmem_limit_bytes=16 * 1024 * 1024),
        cost_estimate=pl.CostEstimate(flops=flops, bytes_accessed=size, transcendentals=0),
    )(scal, *operands, *pieces)


def finish_kernel(scal, mine, other, in1m, in1o, in3m, in3o, early_m, early_o, own, got, out):
    rows = mine.shape[0]
    cube, core = scal[2], scal[6]
    even = (cube == 0) | (cube == 2)

    def put(doc0, doc1):
        out[0] = doc0[...]
        out[1] = doc1[...]

    @pl.when((core == 0) & even)
    def _():
        put(mine, other)

    @pl.when((core == 0) & (cube == 1))
    def _():
        put(in1m, in1o)

    @pl.when((core == 0) & (cube == 3))
    def _():
        put(in3m, in3o)

    @pl.when((core == 1) & (cube != 3))
    def _():
        put(early_o, early_m)

    @pl.when((core == 1) & (cube == 3))
    def _():
        at = lax.broadcasted_iota(jnp.int32, mine.shape, 0)
        low, high = slice(0, rows), slice(rows, 2 * rows)
        for slot, base, a, b, live in ((1, in3m, low, high, scal[7]), (0, in3o, high, low, scal[8])):
            term = own[a, :].astype(F32) + got[b, :].astype(F32)
            term = jnp.where(at < live, term, 0.0)
            out[slot] = (base[...].astype(F32) + term).astype(BF16)


def turns(array, outer):
    return [array] + [exchange(array, outer, turn) for turn in TURNS[1:]]


def gather(weights):
    pair, depth, width = weights.shape[1:]
    halves = weights[0].reshape(pair, depth, 2, width // 2).transpose(2, 0, 1, 3)
    sent = jnp.broadcast_to(halves[:, None], (2, SIDE) + halves.shape[1:])
    sent = sent.reshape((2 * SIDE,) + halves.shape[1:])
    got = lax.all_to_all(sent, ("core", "zl"), 0, 0, tiled=True)
    got = got.reshape(2, SIDE, pair, depth, width // 2).transpose(0, 2, 1, 3, 4)
    got = got.reshape(2 * pair, SIDE * depth, width // 2)
    near = turns(got, False)
    chunks = [jnp.concatenate([a[i:i + pair] for a in near], axis=1) for i in (0, pair)]
    by1 = [exchange(a, True, 1) for a in chunks]
    by3 = [exchange(a, True, 3) for a in chunks]
    across = exchange(chunks[1], True, FAR)
    far = [exchange(by3[0][:1], True, 1), exchange(by1[0][1:], True, 3), across]
    return [*chunks, *by1, *by3], far


def on_device(encoder_embed, decoder_embed, section_weights, norm_gains, input_lengths, target_lengths):
    zh, core = lax.axis_index("zh"), lax.axis_index("core")
    y, x = lax.axis_index("y"), lax.axis_index("x")
    rows = encoder_embed.shape[1]
    encoder = zh < 2
    causal = zh == 2
    key_lengths = jnp.where(causal, target_lengths, input_lengths)
    row_lengths = jnp.where(encoder, input_lengths, target_lengths)
    scal = jnp.stack(
        [
            x,
            y,
            zh,
            causal.astype(jnp.int32),
            key_lengths[core],
            key_lengths[1 - core],
            core,
            row_lengths[core],
            row_lengths[1 - core],
        ]
    ).astype(jnp.int32)
    live = (jnp.arange(rows, dtype=jnp.int32) < row_lengths[core])[:, None]

    near, far = gather(section_weights)
    pieces = near + far
    source = jnp.where(encoder, encoder_embed, decoder_embed)
    mine, other = source[core], source[1 - core]

    def added(stream, term, alive):
        return stream.astype(F32) + jnp.where(alive, term, 0.0)

    def swapped(array, cubes=range(SIDE)):
        pairs = [(2 * c + i, 2 * c + 1 - i) for c in cubes for i in range(2)]
        return lax.ppermute(array, SECTION, pairs)

    count, width = 2 * rows, mine.shape[1]
    half = near[0].shape[-1]
    blocks = (16, count, 128)
    work = 2 * count * width * half
    wide = jax.ShapeDtypeStruct((count, width), BF16)
    halves = tuple(jax.ShapeDtypeStruct((rows, width), kind) for kind in (F32, BF16))
    total = jax.ShapeDtypeStruct((count, half), F32)
    narrow = jax.ShapeDtypeStruct((count, half), BF16)

    started = call(
        early_kernel,
        scal,
        [norm_gains, mine, other],
        (jax.ShapeDtypeStruct(blocks, BF16), total, total, total),
        (),
        near,
        len(EARLY),
        3 * work,
    )
    kept, sent = call(
        first_kernel,
        scal,
        [*started],
        halves,
        [(blocks, F32)],
        pieces,
        len(FIRST),
        2 * work,
    )
    first = added(mine, kept + swapped(sent, (0, 2)).astype(F32), live).astype(BF16)
    in1 = lax.ppermute(first, "zh", [(0, 1)])
    in3 = lax.ppermute(first, "zh", [(2, 3)])
    in1_other = swapped(in1, (1,))
    kept, sent = call(
        second_kernel,
        scal,
        [norm_gains, in1, in1_other],
        halves,
        [(blocks, BF16), (blocks, F32)],
        pieces,
        len(SECOND),
        4 * work,
    )
    second = added(in1, kept + swapped(sent, (1,)).astype(F32), live).astype(BF16)
    memory = rms(second.astype(F32), norm_gains[4:5])
    mem = lax.ppermute(memory, "zh", [(1, 3)])
    early = jnp.where(zh == 1, second, first)
    early_other = lax.ppermute(early, SECTION, [(0, 1), (2, 3), (4, 5)])
    in3_other = swapped(in3, (3,))
    query = call(
        query_kernel,
        scal,
        [norm_gains, in3, in3_other],
        narrow,
        [(blocks, BF16)],
        pieces,
        len(QUERY),
        work,
    )
    mem_other = swapped(mem, (3,))
    own = call(
        third_kernel,
        scal,
        [query, mem, mem_other],
        wide,
        [(blocks, BF16), (blocks, F32)],
        pieces,
        len(THIRD),
        3 * work,
    )
    got = lax.ppermute(own, SECTION, [(6, 7)])
    parts = [mine, other, in1, in1_other, in3, in3_other, early, early_other, own, got]
    out = call(finish_kernel, scal, parts, jax.ShapeDtypeStruct((2, rows, width), BF16))
    return out[None]


def solution(mesh):
    fine = Mesh(mesh.devices.reshape(SIDE, 2, SIDE, SIDE, SIDE), AXES)
    in_specs = (
        P(DP, None, None),
        P(DP, None, None),
        P(SECTION, None, DP, None),
        P(),
        P(DP),
        P(DP),
    )
    out_specs = P(SECTION, DP, None, None)
    return jax.shard_map(
        on_device, mesh=fine, in_specs=in_specs, out_specs=out_specs, check_vma=False
    )
```

```python
import functools
import itertools

import jax
import jax.numpy as jnp
from jax import lax
from jax.experimental import pallas as pl
from jax.experimental.pallas import tpu as pltpu
from jax.sharding import Mesh, PartitionSpec as P

HEAD_DIM = 128
SIDE = 4
TURNS = (0, 1, 3, 2)
FAR = 2
EVEN = (0, 2)
ODD = (1, 3)
AXES = ("zh", "core", "y", "x", "zl")
DP = ("y", "x", "zl")
SECTION = ("zh", "core")
F32 = jnp.float32
BF16 = jnp.bfloat16


def place(zh, core, y, x, zl):
    return (((zh * 2 + core) * SIDE + y) * SIDE + x) * SIDE + zl


def moved(array, cubes, move):
    pairs = []
    for zh, core, y, x, zl in itertools.product(cubes, *map(range, (2, SIDE, SIDE, SIDE))):
        pairs.append((place(zh, core, y, x, zl), place(zh, core, *move(core, y, x), zl)))
    return lax.ppermute(array, AXES, pairs)


def exchange(array, outer, by, cubes=range(SIDE)):
    return moved(
        array, cubes, lambda core, y, x: (y ^ by, x) if outer == (core == 0) else (y, x ^ by)
    )


def beside(array):
    return moved(array, EVEN, lambda core, y, x: (y, x ^ 1))


def dot(a, b):
    return jnp.dot(a, b, preferred_element_type=F32)


def dot_t(a, b):
    return lax.dot_general(a, b, (((1,), (1,)), ((), ())), preferred_element_type=F32)


def rms(values, gain):
    mean_square = jnp.mean(values * values, axis=-1, keepdims=True)
    return (values * lax.rsqrt(mean_square + 1e-06) * gain).astype(BF16)


def block_at(scal, outer, inner):
    back = scal[6] == 1
    dy, dx = jnp.where(back, inner, outer), jnp.where(back, outer, inner)
    return lax.bitwise_xor(scal[1], dy) * SIDE + lax.bitwise_xor(scal[0], dx)


class Fetched:
    def __init__(self, sources, space, sems):
        self.space = space
        self.copies = []
        for slot, source in enumerate(sources):
            self.copies.append(pltpu.make_async_copy(source, space.at[slot], sems.at[slot]))
            self.copies[-1].start()

    def take(self, slot):
        self.copies[slot].wait()
        return self.space[slot]


def put_norm(scal, gains, streams, h3):
    rows = streams[0].shape[0]
    gain = gains[pl.ds(scal[2], 1), :]
    for part, ref in enumerate(streams):
        h = rms(ref[...].astype(F32), gain)
        for i in range(16):
            h3[i, part * rows:(part + 1) * rows, :] = h[:, i * 128:(i + 1) * 128]


def put_memory(mem, m3):
    rows = mem[0].shape[0]
    for part, ref in enumerate(mem):
        for i in range(16):
            m3[i, part * rows:(part + 1) * rows, :] = ref[:, i * 128:(i + 1) * 128]


def project(scal, h3, pieces, which, space, sems):
    keys = [(i, m, n) for i in range(SIDE) for m in which for n in range(len(pieces))]
    fetched = Fetched([pieces[n][i].at[m] for i, m, n in keys], space, sems)

    def run():
        totals = {}
        for slot, (i, m, n) in enumerate(keys):
            if (m, n) == (which[0], 0):
                h = jnp.concatenate([h3[block_at(scal, TURNS[i], d)] for d in TURNS], axis=1)
            term = dot(h, fetched.take(slot))
            totals[m, n] = totals[m, n] + term if i else term
        sides = range(len(pieces))
        return [jnp.concatenate([totals[m, n] for n in sides], axis=1).astype(BF16) for m in which]

    return run


def mask(scal, first_limit, second_limit, count):
    rows = count // 2
    r = lax.broadcasted_iota(jnp.int32, (count, count), 0)
    c = lax.broadcasted_iota(jnp.int32, (count, count), 1)
    first = c < rows
    live = (r < rows) == first
    key_at = jnp.where(first, c, c - rows).astype(F32)
    live = live & (key_at < jnp.where(first, first_limit, second_limit))
    return live & ((c <= r) | (scal[3] == 0))


def attend(live, q, k, v):
    mixed = []
    for head in range(q.shape[1] // HEAD_DIM):
        at = slice(head * HEAD_DIM, (head + 1) * HEAD_DIM)
        s = dot_t(q[:, at], k[:, at]) * HEAD_DIM ** (-0.5)
        s = jnp.where(live, s, -1e30)
        e = jnp.exp(s - jnp.max(s, axis=-1, keepdims=True))
        p = (e / jnp.sum(e, axis=-1, keepdims=True)).astype(BF16)
        mixed.append(dot(p, v[:, at]).astype(BF16))
    return jnp.concatenate(mixed, axis=1)


def local_mask(scal, count):
    return mask(scal, scal[4].astype(F32), scal[5].astype(F32), count)


def project_out(scal, mixed, fetched, t3):
    for i, turn in enumerate(TURNS):
        t = dot_t(mixed, fetched.take(i))
        for j, d in enumerate(TURNS):
            t3[block_at(scal, turn, d)] = t[:, j * 128:(j + 1) * 128]


def put_out(t3, first, second, out_mine, out_other):
    for i in range(16):
        at = slice(i * 128, (i + 1) * 128)
        out_mine[:, at] = t3[i, first, :].astype(out_mine.dtype)
        out_other[:, at] = t3[i, second, :].astype(out_other.dtype)


def norm_kernel(scal, gains, own, got, h3, limits):
    @pl.when(lax.rem(scal[2], 2) == 0)
    def _():
        gain = gains[pl.ds(scal[2], 1), :]
        count = h3.shape[1] // 2
        for part, ref in enumerate((own, got)):
            for at in range(0, count, 64):
                h = rms(ref[at:at + 64, :].astype(F32), gain)
                to = part * count + at
                for i in range(16):
                    h3[i, to:to + 64, :] = h[:, i * 128:(i + 1) * 128]
            limits[part] = ref[count:, :128].astype(F32)


def first_kernel(scal, h3, limits, *refs):
    pieces, (own, sent, space, sems) = refs[:SIDE], refs[SIDE:]

    @pl.when(lax.rem(scal[2], 2) == 0)
    def _():
        q, k, v = project(scal, h3, [pieces], (0, 1, 2), space, sems)()
        count = own.shape[0]
        for part, out in enumerate((own, sent)):
            at = slice(part * count, (part + 1) * count)
            live = mask(scal, limits[part, 0:1, :], limits[part, 1:2, :], count)
            out[...] = attend(live, q[at], k[at], v[at])


def first_out_kernel(scal, own, got, *refs):
    pieces, (out_mine, out_other, mixed, t3, space, sems) = refs[:SIDE], refs[SIDE:]

    @pl.when(lax.rem(scal[2], 2) == 0)
    def _():
        fetched = Fetched([ref.at[0] for ref in pieces], space, sems)
        half = own.shape[1]
        side = lax.rem(scal[0], 2)
        mixed[:, pl.ds(pl.multiple_of(side * half, half), half)] = own[...]
        mixed[:, pl.ds(pl.multiple_of((1 - side) * half, half), half)] = got[...]
        project_out(scal, mixed[...], fetched, t3)
        rows = out_mine.shape[0]
        here = pl.ds(pl.multiple_of(scal[6] * rows, rows), rows)
        there = pl.ds(pl.multiple_of((1 - scal[6]) * rows, rows), rows)
        put_out(t3, here, there, out_mine, out_other)


def split(refs):
    return [refs[:SIDE], refs[SIDE:2 * SIDE]], refs[2 * SIDE:3 * SIDE], refs[3 * SIDE:]


def second_kernel(scal, gains, mine, other, *refs):
    pieces, outs, rest = split(refs)
    out_mine, out_other, h3, t3, space, sems, out_space, out_sems = rest

    @pl.when(scal[2] == 1)
    def _():
        run = project(scal, h3, pieces, (0, 1, 2), space, sems)
        fetched = Fetched([ref.at[0] for ref in outs], out_space, out_sems)
        put_norm(scal, gains, (mine, other), h3)
        rows = mine.shape[0]
        mixed = attend(local_mask(scal, 2 * rows), *run())
        project_out(scal, mixed, fetched, t3)
        put_out(t3, slice(0, rows), slice(rows, 2 * rows), out_mine, out_other)


def query_kernel(scal, gains, mine, other, *refs):
    pieces, _, (q, h3, space, sems) = split(refs)

    @pl.when(scal[2] == 3)
    def _():
        run = project(scal, h3, pieces, (0,), space, sems)
        put_norm(scal, gains, (mine, other), h3)
        q[...] = run()[0]


def third_kernel(scal, q, mem_mine, mem_other, *refs):
    pieces, outs, (out, m3, t3, space, sems, out_space, out_sems) = split(refs)

    @pl.when(scal[2] == 3)
    def _():
        rows = mem_mine.shape[0]
        run = project(scal, m3, pieces, (1, 2), space, sems)
        fetched = Fetched([ref.at[0] for ref in outs], out_space, out_sems)
        put_memory((mem_mine, mem_other), m3)
        k, v = run()
        mixed = attend(local_mask(scal, 2 * rows), q[...], k, v)
        project_out(scal, mixed, fetched, t3)
        put_out(t3, slice(0, rows), slice(rows, 2 * rows), out.at[:rows], out.at[rows:])


VMEM = pl.BlockSpec(memory_space=pltpu.VMEM)
SMEM = pl.BlockSpec(memory_space=pltpu.SMEM)
ANY = pl.BlockSpec(memory_space=pl.ANY)


def call(kernel, scal, operands, outs, scratch=(), pieces=(), fetches=(), flops=0):
    size = sum(a.size * a.dtype.itemsize for a in [*operands, *pieces])
    shapes = [pltpu.VMEM(shape, kind) for shape, kind in scratch]
    for shape in fetches:
        shapes += [pltpu.VMEM(shape, BF16), pltpu.SemaphoreType.DMA(shape[:1])]
    return pl.pallas_call(
        kernel,
        out_shape=outs,
        in_specs=[SMEM] + [VMEM] * len(operands) + [ANY] * len(pieces),
        out_specs=jax.tree.map(lambda _: VMEM, outs),
        scratch_shapes=shapes,
        compiler_params=pltpu.CompilerParams(vmem_limit_bytes=16 * 1024 * 1024),
        cost_estimate=pl.CostEstimate(flops=flops, bytes_accessed=size, transcendentals=0),
    )(scal, *operands, *pieces)


def finish_kernel(scal, mine, other, in1m, in1o, in3m, in3o, early_m, early_o, own, got, out):
    rows = mine.shape[0]
    cube, core = scal[2], scal[6]
    even = (cube == 0) | (cube == 2)

    def put(doc0, doc1):
        out[0] = doc0[...]
        out[1] = doc1[...]

    @pl.when((core == 0) & even)
    def _():
        put(mine, other)

    @pl.when((core == 0) & (cube == 1))
    def _():
        put(in1m, in1o)

    @pl.when((core == 0) & (cube == 3))
    def _():
        put(in3m, in3o)

    @pl.when((core == 1) & (cube != 3))
    def _():
        put(early_o, early_m)

    @pl.when((core == 1) & (cube == 3))
    def _():
        at = lax.broadcasted_iota(jnp.int32, mine.shape, 0)
        low, high = slice(0, rows), slice(rows, 2 * rows)
        for slot, base, a, b, live in ((1, in3m, low, high, scal[7]), (0, in3o, high, low, scal[8])):
            term = own[a, :].astype(F32) + got[b, :].astype(F32)
            term = jnp.where(at < live, term, 0.0)
            out[slot] = (base[...].astype(F32) + term).astype(BF16)


def turns(array, outer, cubes=range(SIDE)):
    return [array] + [exchange(array, outer, turn, cubes) for turn in TURNS[1:]]


def gather(weights):
    pair, depth, width = weights.shape[1:]
    halves = weights[0].reshape(pair, depth, 2, width // 2).transpose(2, 0, 1, 3)
    sent = jnp.broadcast_to(halves[:, None], (2, SIDE) + halves.shape[1:])
    sent = sent.reshape((2 * SIDE,) + halves.shape[1:])
    got = lax.all_to_all(sent, ("core", "zl"), 0, 0, tiled=True)
    got = got.reshape(2, SIDE, pair, depth, width // 2).transpose(0, 2, 1, 3, 4)
    got = got.reshape(2 * pair, SIDE * depth, width // 2)
    block = jnp.concatenate(turns(got, False), axis=1)
    zh, core, x = (lax.axis_index(name) for name in ("zh", "core", "x"))
    side = jnp.where(zh % 2 == 0, x % 2, 0)
    across = jnp.where((zh % 2 == 0) & (core == 1), 1 - side, side)
    half = width // 4

    def columns(at):
        return lax.dynamic_slice(block, (0, 0, at * half), (3,) + block.shape[1:2] + (half,))

    kept, sent = columns(side), columns(across)
    first = [kept, exchange(sent, True, 1), exchange(sent, True, 3), exchange(kept, True, FAR)]
    outs = turns(block[3:], True)
    second = turns(block[:3, :, half:], True, ODD)
    return first, second, outs


def on_device(encoder_embed, decoder_embed, section_weights, norm_gains, input_lengths, target_lengths):
    zh, core = lax.axis_index("zh"), lax.axis_index("core")
    y, x = lax.axis_index("y"), lax.axis_index("x")
    rows = encoder_embed.shape[1]
    encoder = zh < 2
    causal = zh == 2
    key_lengths = jnp.where(causal, target_lengths, input_lengths)
    row_lengths = jnp.where(encoder, input_lengths, target_lengths)
    scal = jnp.stack(
        [
            x,
            y,
            zh,
            causal.astype(jnp.int32),
            key_lengths[core],
            key_lengths[1 - core],
            core,
            row_lengths[core],
            row_lengths[1 - core],
        ]
    ).astype(jnp.int32)
    live = (jnp.arange(rows, dtype=jnp.int32) < row_lengths[core])[:, None]

    parts_a, parts_b, parts_o = gather(section_weights)
    pieces = [*parts_a, *parts_b, *parts_o]
    source = jnp.where(encoder, encoder_embed, decoder_embed)
    mine, other = source[core], source[1 - core]

    def added(stream, term, alive):
        return stream.astype(F32) + jnp.where(alive, term, 0.0)

    def swapped(array, cubes=range(SIDE)):
        pairs = [(2 * c + i, 2 * c + 1 - i) for c in cubes for i in range(2)]
        return lax.ppermute(array, SECTION, pairs)

    count, width = 2 * rows, mine.shape[1]
    tile = parts_a[0].shape[1:]
    square = parts_o[0].shape[1:]
    half = square[1]
    blocks = (16, count, 128)
    work = 2 * count * width * half
    wide = jax.ShapeDtypeStruct((count, width), BF16)
    halves = tuple(jax.ShapeDtypeStruct((rows, width), kind) for kind in (F32, BF16))
    narrow = jax.ShapeDtypeStruct((count, half), BF16)
    quarter = jax.ShapeDtypeStruct((count, half // 2), BF16)
    out_fetch = (SIDE,) + square

    limits = jnp.broadcast_to(key_lengths.astype(BF16)[:, None], (2, width))
    limits = jnp.concatenate([limits, jnp.zeros((14, width), BF16)], axis=0)
    shared = jnp.concatenate([source.reshape(count, width), limits], axis=0)
    h3, limits = call(
        norm_kernel,
        scal,
        [norm_gains, shared, beside(shared)],
        (
            jax.ShapeDtypeStruct((16, 2 * count, 128), BF16),
            jax.ShapeDtypeStruct((2, 16, 128), F32),
        ),
    )
    mixed, mixed_sent = call(
        first_kernel, scal, [h3, limits], (quarter, quarter), (), parts_a, [(12,) + tile], 3 * work
    )
    kept, sent = call(
        first_out_kernel,
        scal,
        [mixed, beside(mixed_sent)],
        halves,
        [((count, half), BF16), (blocks, F32)],
        parts_o,
        [out_fetch],
        work,
    )
    first = added(mine, kept + swapped(sent, (0, 2)).astype(F32), live).astype(BF16)
    in1 = lax.ppermute(first, "zh", [(0, 1)])
    in3 = lax.ppermute(first, "zh", [(2, 3)])
    in1_other = swapped(in1, (1,))
    kept, sent = call(
        second_kernel,
        scal,
        [norm_gains, in1, in1_other],
        halves,
        [(blocks, BF16), (blocks, F32)],
        pieces,
        [(24,) + tile, out_fetch],
        4 * work,
    )
    second = added(in1, kept + swapped(sent, (1,)).astype(F32), live).astype(BF16)
    memory = rms(second.astype(F32), norm_gains[4:5])
    mem = lax.ppermute(memory, "zh", [(1, 3)])
    early = jnp.where(zh == 1, second, first)
    early_other = lax.ppermute(early, SECTION, [(0, 1), (2, 3), (4, 5)])
    in3_other = swapped(in3, (3,))
    query = call(
        query_kernel,
        scal,
        [norm_gains, in3, in3_other],
        narrow,
        [(blocks, BF16)],
        pieces,
        [(8,) + tile],
        work,
    )
    mem_other = swapped(mem, (3,))
    own = call(
        third_kernel,
        scal,
        [query, mem, mem_other],
        wide,
        [(blocks, BF16), (blocks, F32)],
        pieces,
        [(16,) + tile, out_fetch],
        3 * work,
    )
    got = lax.ppermute(own, SECTION, [(6, 7)])
    parts = [mine, other, in1, in1_other, in3, in3_other, early, early_other, own, got]
    out = call(finish_kernel, scal, parts, jax.ShapeDtypeStruct((2, rows, width), BF16))
    return out[None]


def solution(mesh):
    fine = Mesh(mesh.devices.reshape(SIDE, 2, SIDE, SIDE, SIDE), AXES)
    in_specs = (
        P(DP, None, None),
        P(DP, None, None),
        P(SECTION, None, DP, None),
        P(),
        P(DP),
        P(DP),
    )
    out_specs = P(SECTION, DP, None, None)
    return jax.shard_map(
        on_device, mesh=fine, in_specs=in_specs, out_specs=out_specs, check_vma=False
    )
```

```python
import functools
import itertools

import jax
import jax.numpy as jnp
from jax import lax
from jax.experimental import pallas as pl
from jax.experimental.pallas import tpu as pltpu
from jax.sharding import Mesh, PartitionSpec as P

HEAD_DIM = 128
SIDE = 4
TURNS = (0, 1, 3, 2)
FAR = 2
EVEN = (0, 2)
ODD = (1, 3)
AXES = ("zh", "core", "y", "x", "zl")
DP = ("y", "x", "zl")
SECTION = ("zh", "core")
F32 = jnp.float32
BF16 = jnp.bfloat16


def place(zh, core, y, x, zl):
    return (((zh * 2 + core) * SIDE + y) * SIDE + x) * SIDE + zl


def moved(array, cubes, move):
    pairs = []
    for zh, core, y, x, zl in itertools.product(cubes, *map(range, (2, SIDE, SIDE, SIDE))):
        pairs.append((place(zh, core, y, x, zl), place(zh, core, *move(core, y, x), zl)))
    return lax.ppermute(array, AXES, pairs)


def exchange(array, outer, by, cubes=range(SIDE)):
    return moved(
        array, cubes, lambda core, y, x: (y ^ by, x) if outer == (core == 0) else (y, x ^ by)
    )


def beside(array):
    return moved(array, EVEN, lambda core, y, x: (y, x ^ 1))


def dot(a, b):
    return jnp.dot(a, b, preferred_element_type=F32)


def dot_t(a, b):
    return lax.dot_general(a, b, (((1,), (1,)), ((), ())), preferred_element_type=F32)


def rms(values, gain):
    mean_square = jnp.mean(values * values, axis=-1, keepdims=True)
    return (values * lax.rsqrt(mean_square + 1e-06) * gain).astype(BF16)


def block_at(scal, outer, inner):
    back = scal[6] == 1
    dy, dx = jnp.where(back, inner, outer), jnp.where(back, outer, inner)
    return lax.bitwise_xor(scal[1], dy) * SIDE + lax.bitwise_xor(scal[0], dx)


class Fetched:
    def __init__(self, sources, space, sems):
        self.space = space
        self.copies = []
        for slot, source in enumerate(sources):
            self.copies.append(pltpu.make_async_copy(source, space.at[slot], sems.at[slot]))
            self.copies[-1].start()

    def take(self, slot):
        self.copies[slot].wait()
        return self.space.at[slot]


def put_norm(scal, gains, streams, h3):
    rows = streams[0].shape[0]
    gain = gains[pl.ds(scal[2], 1), :]
    for part, ref in enumerate(streams):
        h = rms(ref[...].astype(F32), gain)
        for i in range(16):
            h3[i, part * rows:(part + 1) * rows, :] = h[:, i * 128:(i + 1) * 128]


def put_memory(mem, m3):
    rows = mem[0].shape[0]
    for part, ref in enumerate(mem):
        for i in range(16):
            m3[i, part * rows:(part + 1) * rows, :] = ref[:, i * 128:(i + 1) * 128]


def project(scal, h3, pieces, which, space, sems):
    keys = [(i, n) for i in range(SIDE) for n in range(len(pieces))]
    low, high = which[0], which[-1] + 1
    fetched = Fetched([pieces[n][i].at[low:high] for i, n in keys], space, sems)

    def run():
        totals = {}
        for slot, (i, n) in enumerate(keys):
            if n == 0:
                h = jnp.concatenate([h3[block_at(scal, TURNS[i], d)] for d in TURNS], axis=1)
            tile = fetched.take(slot)
            for m in which:
                term = dot(h, tile[m - low])
                totals[m, n] = totals[m, n] + term if i else term
        sides = range(len(pieces))
        return [jnp.concatenate([totals[m, n] for n in sides], axis=1).astype(BF16) for m in which]

    return run


def mask(scal, first_limit, second_limit, count):
    rows = count // 2
    r = lax.broadcasted_iota(jnp.int32, (count, count), 0)
    c = lax.broadcasted_iota(jnp.int32, (count, count), 1)
    first = c < rows
    live = (r < rows) == first
    key_at = jnp.where(first, c, c - rows).astype(F32)
    live = live & (key_at < jnp.where(first, first_limit, second_limit))
    return live & ((c <= r) | (scal[3] == 0))


def attend(live, q, k, v):
    mixed = []
    for head in range(q.shape[1] // HEAD_DIM):
        at = slice(head * HEAD_DIM, (head + 1) * HEAD_DIM)
        s = dot_t(q[:, at], k[:, at]) * HEAD_DIM ** (-0.5)
        s = jnp.where(live, s, -1e30)
        e = jnp.exp(s - jnp.max(s, axis=-1, keepdims=True))
        p = (e / jnp.sum(e, axis=-1, keepdims=True)).astype(BF16)
        mixed.append(dot(p, v[:, at]).astype(BF16))
    return jnp.concatenate(mixed, axis=1)


def local_mask(scal, count):
    return mask(scal, scal[4].astype(F32), scal[5].astype(F32), count)


def project_out(scal, mixed, fetched, t3):
    for i, turn in enumerate(TURNS):
        t = dot_t(mixed, fetched.take(i)[...])
        for j, d in enumerate(TURNS):
            t3[block_at(scal, turn, d)] = t[:, j * 128:(j + 1) * 128]


def put_out(t3, first, second, out_mine, out_other):
    for i in range(16):
        at = slice(i * 128, (i + 1) * 128)
        out_mine[:, at] = t3[i, first, :].astype(out_mine.dtype)
        out_other[:, at] = t3[i, second, :].astype(out_other.dtype)


def norm_kernel(scal, gains, own, got, h3, limits):
    @pl.when(lax.rem(scal[2], 2) == 0)
    def _():
        gain = gains[pl.ds(scal[2], 1), :]
        count = h3.shape[1] // 2
        for part, ref in enumerate((own, got)):
            for at in range(0, count, 64):
                h = rms(ref[at:at + 64, :].astype(F32), gain)
                to = part * count + at
                for i in range(16):
                    h3[i, to:to + 64, :] = h[:, i * 128:(i + 1) * 128]
            limits[part] = ref[count:, :128].astype(F32)


def first_kernel(scal, h3, limits, *refs):
    pieces, (own, sent, space, sems) = refs[:SIDE], refs[SIDE:]

    @pl.when(lax.rem(scal[2], 2) == 0)
    def _():
        q, k, v = project(scal, h3, [pieces], (0, 1, 2), space, sems)()
        count = own.shape[0]
        for part, out in enumerate((own, sent)):
            at = slice(part * count, (part + 1) * count)
            live = mask(scal, limits[part, 0:1, :], limits[part, 1:2, :], count)
            out[...] = attend(live, q[at], k[at], v[at])


def first_out_kernel(scal, own, got, *refs):
    pieces, (out_mine, out_other, mixed, t3, space, sems) = refs[:SIDE], refs[SIDE:]

    @pl.when(lax.rem(scal[2], 2) == 0)
    def _():
        fetched = Fetched([ref.at[0] for ref in pieces], space, sems)
        half = own.shape[1]
        side = lax.rem(scal[0], 2)
        mixed[:, pl.ds(pl.multiple_of(side * half, half), half)] = own[...]
        mixed[:, pl.ds(pl.multiple_of((1 - side) * half, half), half)] = got[...]
        project_out(scal, mixed[...], fetched, t3)
        rows = out_mine.shape[0]
        here = pl.ds(pl.multiple_of(scal[6] * rows, rows), rows)
        there = pl.ds(pl.multiple_of((1 - scal[6]) * rows, rows), rows)
        put_out(t3, here, there, out_mine, out_other)


def split(refs):
    return [refs[:SIDE], refs[SIDE:2 * SIDE]], refs[2 * SIDE:3 * SIDE], refs[3 * SIDE:]


def second_kernel(scal, gains, mine, other, *refs):
    pieces, outs, rest = split(refs)
    out_mine, out_other, h3, t3, space, sems, out_space, out_sems = rest

    @pl.when(scal[2] == 1)
    def _():
        run = project(scal, h3, pieces, (0, 1, 2), space, sems)
        fetched = Fetched([ref.at[0] for ref in outs], out_space, out_sems)
        put_norm(scal, gains, (mine, other), h3)
        rows = mine.shape[0]
        mixed = attend(local_mask(scal, 2 * rows), *run())
        project_out(scal, mixed, fetched, t3)
        put_out(t3, slice(0, rows), slice(rows, 2 * rows), out_mine, out_other)


def query_kernel(scal, gains, mine, other, *refs):
    pieces, _, (q, h3, space, sems) = split(refs)

    @pl.when(scal[2] == 3)
    def _():
        run = project(scal, h3, pieces, (0,), space, sems)
        put_norm(scal, gains, (mine, other), h3)
        q[...] = run()[0]


def third_kernel(scal, q, mem_mine, mem_other, *refs):
    pieces, outs, (out, m3, t3, space, sems, out_space, out_sems) = split(refs)

    @pl.when(scal[2] == 3)
    def _():
        rows = mem_mine.shape[0]
        run = project(scal, m3, pieces, (1, 2), space, sems)
        fetched = Fetched([ref.at[0] for ref in outs], out_space, out_sems)
        put_memory((mem_mine, mem_other), m3)
        k, v = run()
        mixed = attend(local_mask(scal, 2 * rows), q[...], k, v)
        project_out(scal, mixed, fetched, t3)
        put_out(t3, slice(0, rows), slice(rows, 2 * rows), out.at[:rows], out.at[rows:])


VMEM = pl.BlockSpec(memory_space=pltpu.VMEM)
SMEM = pl.BlockSpec(memory_space=pltpu.SMEM)
HBM = pl.BlockSpec(memory_space=pltpu.HBM)


def call(kernel, scal, operands, outs, scratch=(), pieces=(), fetches=(), flops=0):
    size = sum(a.size * a.dtype.itemsize for a in [*operands, *pieces])
    shapes = [pltpu.VMEM(shape, kind) for shape, kind in scratch]
    for shape in fetches:
        shapes += [pltpu.VMEM(shape, BF16), pltpu.SemaphoreType.DMA(shape[:1])]
    return pl.pallas_call(
        kernel,
        out_shape=outs,
        in_specs=[SMEM] + [VMEM] * len(operands) + [HBM] * len(pieces),
        out_specs=jax.tree.map(lambda _: VMEM, outs),
        scratch_shapes=shapes,
        compiler_params=pltpu.CompilerParams(vmem_limit_bytes=16 * 1024 * 1024),
        cost_estimate=pl.CostEstimate(flops=flops, bytes_accessed=size, transcendentals=0),
    )(scal, *operands, *pieces)


def finish_kernel(scal, mine, other, in1m, in1o, in3m, in3o, early_m, early_o, own, got, out):
    rows = mine.shape[0]
    cube, core = scal[2], scal[6]
    even = (cube == 0) | (cube == 2)

    def put(doc0, doc1):
        out[0] = doc0[...]
        out[1] = doc1[...]

    @pl.when((core == 0) & even)
    def _():
        put(mine, other)

    @pl.when((core == 0) & (cube == 1))
    def _():
        put(in1m, in1o)

    @pl.when((core == 0) & (cube == 3))
    def _():
        put(in3m, in3o)

    @pl.when((core == 1) & (cube != 3))
    def _():
        put(early_o, early_m)

    @pl.when((core == 1) & (cube == 3))
    def _():
        at = lax.broadcasted_iota(jnp.int32, mine.shape, 0)
        low, high = slice(0, rows), slice(rows, 2 * rows)
        for slot, base, a, b, live in ((1, in3m, low, high, scal[7]), (0, in3o, high, low, scal[8])):
            term = own[a, :].astype(F32) + got[b, :].astype(F32)
            term = jnp.where(at < live, term, 0.0)
            out[slot] = (base[...].astype(F32) + term).astype(BF16)


def turns(array, outer, cubes=range(SIDE)):
    return [array] + [exchange(array, outer, turn, cubes) for turn in TURNS[1:]]


def gather(weights, early, late):
    pair, depth, width = weights.shape[1:]
    halves = weights[0].reshape(pair, depth, 2, width // 2).transpose(2, 0, 1, 3)
    sent = jnp.broadcast_to(halves[:, None], (2, SIDE) + halves.shape[1:])
    sent = sent.reshape((2 * SIDE,) + halves.shape[1:])
    got = lax.all_to_all(sent, ("core", "zl"), 0, 0, tiled=True)
    got = got.reshape(2, SIDE, pair, depth, width // 2).transpose(0, 2, 1, 3, 4)
    got = got.reshape(2 * pair, SIDE * depth, width // 2)
    near = turns(got, False)
    near[1], early = lax.optimization_barrier((near[1], early))
    block = jnp.concatenate(near, axis=1)
    zh, core, x = (lax.axis_index(name) for name in ("zh", "core", "x"))
    side = jnp.where(zh % 2 == 0, x % 2, 0)
    across = jnp.where((zh % 2 == 0) & (core == 1), 1 - side, side)
    half = width // 4

    def columns(at):
        return lax.dynamic_slice(block, (0, 0, at * half), (3,) + block.shape[1:2] + (half,))

    kept, sent = columns(side), columns(across)
    sent, late = lax.optimization_barrier((sent, late))
    first = [kept, exchange(sent, True, 1), exchange(sent, True, 3), exchange(kept, True, FAR)]
    return first, block[:3, :, half:], block[3:], early, late


def on_device(encoder_embed, decoder_embed, section_weights, norm_gains, input_lengths, target_lengths):
    zh, core = lax.axis_index("zh"), lax.axis_index("core")
    y, x = lax.axis_index("y"), lax.axis_index("x")
    rows = encoder_embed.shape[1]
    encoder = zh < 2
    causal = zh == 2
    key_lengths = jnp.where(causal, target_lengths, input_lengths)
    row_lengths = jnp.where(encoder, input_lengths, target_lengths)
    scal = jnp.stack(
        [
            x,
            y,
            zh,
            causal.astype(jnp.int32),
            key_lengths[core],
            key_lengths[1 - core],
            core,
            row_lengths[core],
            row_lengths[1 - core],
        ]
    ).astype(jnp.int32)
    live = (jnp.arange(rows, dtype=jnp.int32) < row_lengths[core])[:, None]

    source = jnp.where(encoder, encoder_embed, decoder_embed)
    mine, other = source[core], source[1 - core]

    def added(stream, term, alive):
        return stream.astype(F32) + jnp.where(alive, term, 0.0)

    def swapped(array, cubes=range(SIDE)):
        pairs = [(2 * c + i, 2 * c + 1 - i) for c in cubes for i in range(2)]
        return lax.ppermute(array, SECTION, pairs)

    count, width = 2 * rows, mine.shape[1]
    limits = jnp.broadcast_to(key_lengths.astype(BF16)[:, None], (2, width))
    limits = jnp.concatenate([limits, jnp.zeros((14, width), BF16)], axis=0)
    shared = jnp.concatenate([source.reshape(count, width), limits], axis=0)
    parts_a, rest_b, rest_o, (scal, shared), shared_got = gather(
        section_weights, (scal, shared), beside(shared)
    )
    tile = parts_a[0].shape[1:]
    square = rest_o.shape[1:]
    half = square[1]
    blocks = (16, count, 128)
    work = 2 * count * width * half
    wide = jax.ShapeDtypeStruct((count, width), BF16)
    halves = tuple(jax.ShapeDtypeStruct((rows, width), kind) for kind in (F32, BF16))
    narrow = jax.ShapeDtypeStruct((count, half), BF16)
    quarter = jax.ShapeDtypeStruct((count, half // 2), BF16)
    out_fetch = (SIDE,) + square

    h3, limits = call(
        norm_kernel,
        scal,
        [norm_gains, shared, shared_got],
        (
            jax.ShapeDtypeStruct((16, 2 * count, 128), BF16),
            jax.ShapeDtypeStruct((2, 16, 128), F32),
        ),
    )
    rest_o, h3 = lax.optimization_barrier((rest_o, h3))
    parts_o = turns(rest_o, True)
    mixed, mixed_sent = call(
        first_kernel, scal, [h3, limits], (quarter, quarter), (), parts_a, [(4, 3) + tile], 3 * work
    )
    rest_b, mixed = lax.optimization_barrier((rest_b, mixed))
    kept, sent = call(
        first_out_kernel,
        scal,
        [mixed, beside(mixed_sent)],
        halves,
        [((count, half), BF16), (blocks, F32)],
        parts_o,
        [out_fetch],
        work,
    )
    first = added(mine, kept + swapped(sent, (0, 2)).astype(F32), live).astype(BF16)
    pieces = [*parts_a, *turns(rest_b, True, ODD), *parts_o]
    in1 = lax.ppermute(first, "zh", [(0, 1)])
    in3 = lax.ppermute(first, "zh", [(2, 3)])
    in1_other = swapped(in1, (1,))
    kept, sent = call(
        second_kernel,
        scal,
        [norm_gains, in1, in1_other],
        halves,
        [(blocks, BF16), (blocks, F32)],
        pieces,
        [(8, 3) + tile, out_fetch],
        4 * work,
    )
    second = added(in1, kept + swapped(sent, (1,)).astype(F32), live).astype(BF16)
    memory = rms(second.astype(F32), norm_gains[4:5])
    mem = lax.ppermute(memory, "zh", [(1, 3)])
    early = jnp.where(zh == 1, second, first)
    early_other = lax.ppermute(early, SECTION, [(0, 1), (2, 3), (4, 5)])
    in3_other = swapped(in3, (3,))
    query = call(
        query_kernel,
        scal,
        [norm_gains, in3, in3_other],
        narrow,
        [(blocks, BF16)],
        pieces,
        [(8, 1) + tile],
        work,
    )
    mem_other = swapped(mem, (3,))
    own = call(
        third_kernel,
        scal,
        [query, mem, mem_other],
        wide,
        [(blocks, BF16), (blocks, F32)],
        pieces,
        [(8, 2) + tile, out_fetch],
        3 * work,
    )
    got = lax.ppermute(own, SECTION, [(6, 7)])
    parts = [mine, other, in1, in1_other, in3, in3_other, early, early_other, own, got]
    out = call(finish_kernel, scal, parts, jax.ShapeDtypeStruct((2, rows, width), BF16))
    return out[None]


def solution(mesh):
    fine = Mesh(mesh.devices.reshape(SIDE, 2, SIDE, SIDE, SIDE), AXES)
    in_specs = (
        P(DP, None, None),
        P(DP, None, None),
        P(SECTION, None, DP, None),
        P(),
        P(DP),
        P(DP),
    )
    out_specs = P(SECTION, DP, None, None)
    return jax.shard_map(
        on_device, mesh=fine, in_specs=in_specs, out_specs=out_specs, check_vma=False
    )
```

```python
import functools
import itertools

import jax
import jax.numpy as jnp
from jax import lax
from jax.experimental import pallas as pl
from jax.experimental.pallas import tpu as pltpu
from jax.sharding import Mesh, PartitionSpec as P

HEAD_DIM = 128
SIDE = 4
TURNS = (0, 1, 3, 2)
FAR = 2
EVEN = (0, 2)
ODD = (1, 3)
AXES = ("zh", "core", "y", "x", "zl")
DP = ("y", "x", "zl")
SECTION = ("zh", "core")
F32 = jnp.float32
BF16 = jnp.bfloat16


def place(zh, core, y, x, zl):
    return (((zh * 2 + core) * SIDE + y) * SIDE + x) * SIDE + zl


def moved(array, cubes, move):
    pairs = []
    for zh, core, y, x, zl in itertools.product(cubes, *map(range, (2, SIDE, SIDE, SIDE))):
        pairs.append((place(zh, core, y, x, zl), place(zh, core, *move(core, y, x), zl)))
    return lax.ppermute(array, AXES, pairs)


def exchange(array, outer, by, cubes=range(SIDE)):
    return moved(
        array, cubes, lambda core, y, x: (y ^ by, x) if outer == (core == 0) else (y, x ^ by)
    )


def beside(array, cubes=EVEN):
    return moved(array, cubes, lambda core, y, x: (y, x ^ 1))


def dot(a, b):
    return jnp.dot(a, b, preferred_element_type=F32)


def dot_t(a, b):
    return lax.dot_general(a, b, (((1,), (1,)), ((), ())), preferred_element_type=F32)


def rms(values, gain):
    mean_square = jnp.mean(values * values, axis=-1, keepdims=True)
    return (values * lax.rsqrt(mean_square + 1e-06) * gain).astype(BF16)


def block_at(scal, outer, inner):
    back = scal[6] == 1
    dy, dx = jnp.where(back, inner, outer), jnp.where(back, outer, inner)
    return lax.bitwise_xor(scal[1], dy) * SIDE + lax.bitwise_xor(scal[0], dx)


class Fetched:
    def __init__(self, sources, space, sems):
        self.space = space
        self.copies = []
        for slot, source in enumerate(sources):
            self.copies.append(pltpu.make_async_copy(source, space.at[slot], sems.at[slot]))
            self.copies[-1].start()

    def take(self, slot):
        self.copies[slot].wait()
        return self.space.at[slot]


def put_norm(scal, gains, streams, h3):
    rows = streams[0].shape[0]
    gain = gains[pl.ds(scal[2], 1), :]
    for part, ref in enumerate(streams):
        h = rms(ref[...].astype(F32), gain)
        for i in range(16):
            h3[i, part * rows:(part + 1) * rows, :] = h[:, i * 128:(i + 1) * 128]


def put_memory(mem, m3):
    rows = mem[0].shape[0]
    for part, ref in enumerate(mem):
        for i in range(16):
            m3[i, part * rows:(part + 1) * rows, :] = ref[:, i * 128:(i + 1) * 128]


def project(scal, h3, pieces, which, space, sems):
    keys = [(i, n) for i in range(SIDE) for n in range(len(pieces))]
    low, high = which[0], which[-1] + 1
    fetched = Fetched([pieces[n][i].at[low:high] for i, n in keys], space, sems)

    def run():
        totals = {}
        for slot, (i, n) in enumerate(keys):
            if n == 0:
                h = jnp.concatenate([h3[block_at(scal, TURNS[i], d)] for d in TURNS], axis=1)
            tile = fetched.take(slot)
            for m in which:
                term = dot(h, tile[m - low])
                totals[m, n] = totals[m, n] + term if i else term
        sides = range(len(pieces))
        return [jnp.concatenate([totals[m, n] for n in sides], axis=1).astype(BF16) for m in which]

    return run


def mask(scal, first_limit, second_limit, count):
    rows = count // 2
    r = lax.broadcasted_iota(jnp.int32, (count, count), 0)
    c = lax.broadcasted_iota(jnp.int32, (count, count), 1)
    first = c < rows
    live = (r < rows) == first
    key_at = jnp.where(first, c, c - rows).astype(F32)
    live = live & (key_at < jnp.where(first, first_limit, second_limit))
    return live & ((c <= r) | (scal[3] == 0))


def attend(live, q, k, v):
    mixed = []
    for head in range(q.shape[1] // HEAD_DIM):
        at = slice(head * HEAD_DIM, (head + 1) * HEAD_DIM)
        s = dot_t(q[:, at], k[:, at]) * HEAD_DIM ** (-0.5)
        s = jnp.where(live, s, -1e30)
        e = jnp.exp(s - jnp.max(s, axis=-1, keepdims=True))
        p = (e / jnp.sum(e, axis=-1, keepdims=True)).astype(BF16)
        mixed.append(dot(p, v[:, at]).astype(BF16))
    return jnp.concatenate(mixed, axis=1)


def local_mask(scal, count):
    return mask(scal, scal[4].astype(F32), scal[5].astype(F32), count)


def project_out(scal, mixed, fetched, t3):
    for i, turn in enumerate(TURNS):
        t = dot_t(mixed, fetched.take(i)[...])
        for j, d in enumerate(TURNS):
            t3[block_at(scal, turn, d)] = t[:, j * 128:(j + 1) * 128]


def put_out(t3, first, second, out_mine, out_other):
    for i in range(16):
        at = slice(i * 128, (i + 1) * 128)
        out_mine[:, at] = t3[i, first, :].astype(out_mine.dtype)
        out_other[:, at] = t3[i, second, :].astype(out_other.dtype)


def norm_kernel(scal, gains, own, got0, got2, h3):
    count = own.shape[0]

    def put(part, ref):
        gain = gains[pl.ds(scal[2], 1), :]
        for at in range(0, count, 64):
            h = rms(ref[at:at + 64, :].astype(F32), gain)
            to = part * count + at
            for i in range(16):
                h3[i, to:to + 64, :] = h[:, i * 128:(i + 1) * 128]

    @pl.when(scal[2] == 0)
    def _():
        put(0, own)
        put(1, got0)

    @pl.when(scal[2] == 2)
    def _():
        put(0, own)
        put(1, got2)


def first_kernel(scal, h3, own_keys, got_keys, *refs):
    pieces, (own, sent, space, sems) = refs[:SIDE], refs[SIDE:]

    @pl.when(lax.rem(scal[2], 2) == 0)
    def _():
        q, k, v = project(scal, h3, [pieces], (0, 1, 2), space, sems)()
        count = own.shape[0]
        for part, (keys, out) in enumerate(((own_keys, own), (got_keys, sent))):
            at = slice(part * count, (part + 1) * count)
            live = mask(scal, keys[0:1, :], keys[1:2, :], count)
            out[...] = attend(live, q[at], k[at], v[at])


def first_out_kernel(scal, own, got, *refs):
    pieces, (out_mine, out_other, mixed, t3, space, sems) = refs[:SIDE], refs[SIDE:]

    @pl.when(lax.rem(scal[2], 2) == 0)
    def _():
        fetched = Fetched([ref.at[0] for ref in pieces], space, sems)
        half = own.shape[1]
        side = lax.rem(scal[0], 2)
        mixed[:, pl.ds(pl.multiple_of(side * half, half), half)] = own[...]
        mixed[:, pl.ds(pl.multiple_of((1 - side) * half, half), half)] = got[...]
        project_out(scal, mixed[...], fetched, t3)
        rows = out_mine.shape[0]
        here = pl.ds(pl.multiple_of(scal[6] * rows, rows), rows)
        there = pl.ds(pl.multiple_of((1 - scal[6]) * rows, rows), rows)
        put_out(t3, here, there, out_mine, out_other)


def split(refs):
    return [refs[:SIDE], refs[SIDE:2 * SIDE]], refs[2 * SIDE:3 * SIDE], refs[3 * SIDE:]


def second_kernel(scal, gains, mine, other, *refs):
    pieces, outs, rest = split(refs)
    out_mine, out_other, h3, t3, space, sems, out_space, out_sems = rest

    @pl.when(scal[2] == 1)
    def _():
        run = project(scal, h3, pieces, (0, 1, 2), space, sems)
        fetched = Fetched([ref.at[0] for ref in outs], out_space, out_sems)
        put_norm(scal, gains, (mine, other), h3)
        rows = mine.shape[0]
        mixed = attend(local_mask(scal, 2 * rows), *run())
        project_out(scal, mixed, fetched, t3)
        put_out(t3, slice(0, rows), slice(rows, 2 * rows), out_mine, out_other)


def query_kernel(scal, gains, mine, other, *refs):
    pieces, _, (q, h3, space, sems) = split(refs)

    @pl.when(scal[2] == 3)
    def _():
        run = project(scal, h3, pieces, (0,), space, sems)
        put_norm(scal, gains, (mine, other), h3)
        q[...] = run()[0]


def third_kernel(scal, q, mem_mine, mem_other, *refs):
    pieces, outs, (out, m3, t3, space, sems, out_space, out_sems) = split(refs)

    @pl.when(scal[2] == 3)
    def _():
        rows = mem_mine.shape[0]
        run = project(scal, m3, pieces, (1, 2), space, sems)
        fetched = Fetched([ref.at[0] for ref in outs], out_space, out_sems)
        put_memory((mem_mine, mem_other), m3)
        k, v = run()
        mixed = attend(local_mask(scal, 2 * rows), q[...], k, v)
        project_out(scal, mixed, fetched, t3)
        put_out(t3, slice(0, rows), slice(rows, 2 * rows), out.at[:rows], out.at[rows:])


VMEM = pl.BlockSpec(memory_space=pltpu.VMEM)
SMEM = pl.BlockSpec(memory_space=pltpu.SMEM)
ANY = pl.BlockSpec(memory_space=pl.ANY)


def call(kernel, scal, operands, outs, scratch=(), pieces=(), fetches=(), flops=0):
    size = sum(a.size * a.dtype.itemsize for a in [*operands, *pieces])
    shapes = [pltpu.VMEM(shape, kind) for shape, kind in scratch]
    for shape in fetches:
        shapes += [pltpu.VMEM(shape, BF16), pltpu.SemaphoreType.DMA(shape[:1])]
    return pl.pallas_call(
        kernel,
        out_shape=outs,
        in_specs=[SMEM] + [VMEM] * len(operands) + [ANY] * len(pieces),
        out_specs=jax.tree.map(lambda _: VMEM, outs),
        scratch_shapes=shapes,
        compiler_params=pltpu.CompilerParams(vmem_limit_bytes=44 * 1024 * 1024),
        cost_estimate=pl.CostEstimate(flops=flops, bytes_accessed=size, transcendentals=0),
    )(scal, *operands, *pieces)


def finish_kernel(scal, mine, other, in1m, in1o, in3m, in3o, early_m, early_o, own, got, out):
    rows = mine.shape[0]
    cube, core = scal[2], scal[6]
    even = (cube == 0) | (cube == 2)

    def put(doc0, doc1):
        out[0] = doc0[...]
        out[1] = doc1[...]

    @pl.when((core == 0) & even)
    def _():
        put(mine, other)

    @pl.when((core == 0) & (cube == 1))
    def _():
        put(in1m, in1o)

    @pl.when((core == 0) & (cube == 3))
    def _():
        put(in3m, in3o)

    @pl.when((core == 1) & (cube != 3))
    def _():
        put(early_o, early_m)

    @pl.when((core == 1) & (cube == 3))
    def _():
        at = lax.broadcasted_iota(jnp.int32, mine.shape, 0)
        low, high = slice(0, rows), slice(rows, 2 * rows)
        for slot, base, a, b, live in ((1, in3m, low, high, scal[7]), (0, in3o, high, low, scal[8])):
            term = own[a, :].astype(F32) + got[b, :].astype(F32)
            term = jnp.where(at < live, term, 0.0)
            out[slot] = (base[...].astype(F32) + term).astype(BF16)


def turns(array, outer, cubes=range(SIDE)):
    return [array] + [exchange(array, outer, turn, cubes) for turn in TURNS[1:]]


def gather(weights, early, late):
    pair, depth, width = weights.shape[1:]
    halves = weights[0].reshape(pair, depth, 2, width // 2).transpose(2, 0, 1, 3)
    sent = jnp.broadcast_to(halves[:, None], (2, SIDE) + halves.shape[1:])
    sent = sent.reshape((2 * SIDE,) + halves.shape[1:])
    got = lax.all_to_all(sent, ("core", "zl"), 0, 0, tiled=True)
    got, late = lax.optimization_barrier((got, late))
    got = got.reshape(2, SIDE, pair, depth, width // 2).transpose(0, 2, 1, 3, 4)
    got = got.reshape(2 * pair, SIDE * depth, width // 2)
    near = turns(got, False)
    near[1], early = lax.optimization_barrier((near[1], early))
    block = jnp.concatenate(near, axis=1)
    zh, core, x = (lax.axis_index(name) for name in ("zh", "core", "x"))
    side = jnp.where(zh % 2 == 0, x % 2, 0)
    across = jnp.where((zh % 2 == 0) & (core == 1), 1 - side, side)
    half = width // 4

    def columns(at):
        return lax.dynamic_slice(block, (0, 0, at * half), (3,) + block.shape[1:2] + (half,))

    kept, sent = columns(side), columns(across)
    first = [kept, exchange(sent, True, 1), exchange(sent, True, 3), exchange(kept, True, FAR)]
    return first, block[:3, :, half:], block[3:], early, late


def on_device(encoder_embed, decoder_embed, section_weights, norm_gains, input_lengths, target_lengths):
    zh, core = lax.axis_index("zh"), lax.axis_index("core")
    y, x = lax.axis_index("y"), lax.axis_index("x")
    rows = encoder_embed.shape[1]
    encoder = zh < 2
    causal = zh == 2
    key_lengths = jnp.where(causal, target_lengths, input_lengths)
    row_lengths = jnp.where(encoder, input_lengths, target_lengths)
    scal = jnp.stack(
        [
            x,
            y,
            zh,
            causal.astype(jnp.int32),
            key_lengths[core],
            key_lengths[1 - core],
            core,
            row_lengths[core],
            row_lengths[1 - core],
        ]
    ).astype(jnp.int32)
    live = (jnp.arange(rows, dtype=jnp.int32) < row_lengths[core])[:, None]

    source = jnp.where(encoder, encoder_embed, decoder_embed)
    mine, other = source[core], source[1 - core]

    def added(stream, term, alive):
        return stream.astype(F32) + jnp.where(alive, term, 0.0)

    def swapped(array, cubes=range(SIDE)):
        pairs = [(2 * c + i, 2 * c + 1 - i) for c in cubes for i in range(2)]
        return lax.ppermute(array, SECTION, pairs)

    count, width = 2 * rows, mine.shape[1]
    keys = jnp.broadcast_to(key_lengths.astype(F32)[:, None], (2, 128))
    keys = jnp.concatenate([keys, jnp.zeros((6, 128), F32)], axis=0)
    streams = (beside(encoder_embed, (0,)), beside(decoder_embed, (2,)))
    parts_a, rest_b, rest_o, (scal, source, keys_got), (got0, got2) = gather(
        section_weights, (scal, source, beside(keys)), streams
    )
    tile = parts_a[0].shape[1:]
    square = rest_o.shape[1:]
    half = square[1]
    blocks = (16, count, 128)
    work = 2 * count * width * half
    wide = jax.ShapeDtypeStruct((count, width), BF16)
    halves = tuple(jax.ShapeDtypeStruct((rows, width), kind) for kind in (F32, BF16))
    narrow = jax.ShapeDtypeStruct((count, half), BF16)
    quarter = jax.ShapeDtypeStruct((count, half // 2), BF16)
    out_fetch = (SIDE,) + square

    h3 = call(
        norm_kernel,
        scal,
        [norm_gains] + [a.reshape(count, width) for a in (source, got0, got2)],
        jax.ShapeDtypeStruct((16, 2 * count, 128), BF16),
    )
    rest_o, h3 = lax.optimization_barrier((rest_o, h3))
    parts_o = turns(rest_o, True)
    mixed, mixed_sent = call(
        first_kernel,
        scal,
        [h3, keys, keys_got],
        (quarter, quarter),
        (),
        parts_a,
        [(4, 3) + tile],
        3 * work,
    )
    rest_b, mixed = lax.optimization_barrier((rest_b, mixed))
    kept, sent = call(
        first_out_kernel,
        scal,
        [mixed, beside(mixed_sent)],
        halves,
        [((count, half), BF16), (blocks, F32)],
        parts_o,
        [out_fetch],
        work,
    )
    first = added(mine, kept + swapped(sent, (0, 2)).astype(F32), live).astype(BF16)
    pieces = [*parts_a, *turns(rest_b, True, ODD), *parts_o]
    in1 = lax.ppermute(first, "zh", [(0, 1)])
    in3 = lax.ppermute(first, "zh", [(2, 3)])
    in1_other = swapped(in1, (1,))
    kept, sent = call(
        second_kernel,
        scal,
        [norm_gains, in1, in1_other],
        halves,
        [(blocks, BF16), (blocks, F32)],
        pieces,
        [(8, 3) + tile, out_fetch],
        4 * work,
    )
    second = added(in1, kept + swapped(sent, (1,)).astype(F32), live).astype(BF16)
    memory = rms(second.astype(F32), norm_gains[4:5])
    mem = lax.ppermute(memory, "zh", [(1, 3)])
    early = jnp.where(zh == 1, second, first)
    early_other = lax.ppermute(early, SECTION, [(0, 1), (2, 3), (4, 5)])
    in3_other = swapped(in3, (3,))
    query = call(
        query_kernel,
        scal,
        [norm_gains, in3, in3_other],
        narrow,
        [(blocks, BF16)],
        pieces,
        [(8, 1) + tile],
        work,
    )
    mem_other = swapped(mem, (3,))
    own = call(
        third_kernel,
        scal,
        [query, mem, mem_other],
        wide,
        [(blocks, BF16), (blocks, F32)],
        pieces,
        [(8, 2) + tile, out_fetch],
        3 * work,
    )
    got = lax.ppermute(own, SECTION, [(6, 7)])
    parts = [mine, other, in1, in1_other, in3, in3_other, early, early_other, own, got]
    out = call(finish_kernel, scal, parts, jax.ShapeDtypeStruct((2, rows, width), BF16))
    return out[None]


def solution(mesh):
    fine = Mesh(mesh.devices.reshape(SIDE, 2, SIDE, SIDE, SIDE), AXES)
    in_specs = (
        P(DP, None, None),
        P(DP, None, None),
        P(SECTION, None, DP, None),
        P(),
        P(DP),
        P(DP),
    )
    out_specs = P(SECTION, DP, None, None)
    return jax.shard_map(
        on_device, mesh=fine, in_specs=in_specs, out_specs=out_specs, check_vma=False
    )
```

```python
import functools
import itertools

import jax
import jax.numpy as jnp
from jax import lax
from jax.experimental import pallas as pl
from jax.experimental.pallas import tpu as pltpu
from jax.sharding import Mesh, PartitionSpec as P

HEAD_DIM = 128
SIDE = 4
TURNS = (0, 1, 3, 2)
FAR = 2
NORM_COST = 5 * 10**9
EVEN = (0, 2)
ODD = (1, 3)
AXES = ("zh", "core", "y", "x", "zl")
DP = ("y", "x", "zl")
SECTION = ("zh", "core")
F32 = jnp.float32
BF16 = jnp.bfloat16


def place(zh, core, y, x, zl):
    return (((zh * 2 + core) * SIDE + y) * SIDE + x) * SIDE + zl


def moved(array, cubes, move):
    pairs = []
    for zh, core, y, x, zl in itertools.product(cubes, *map(range, (2, SIDE, SIDE, SIDE))):
        pairs.append((place(zh, core, y, x, zl), place(zh, core, *move(core, y, x), zl)))
    return lax.ppermute(array, AXES, pairs)


def exchange(array, outer, by, cubes=range(SIDE)):
    return moved(
        array, cubes, lambda core, y, x: (y ^ by, x) if outer == (core == 0) else (y, x ^ by)
    )


def beside(array, cubes=EVEN):
    return moved(array, cubes, lambda core, y, x: (y, x ^ 1))


def dot(a, b):
    return jnp.dot(a, b, preferred_element_type=F32)


def dot_t(a, b):
    return lax.dot_general(a, b, (((1,), (1,)), ((), ())), preferred_element_type=F32)


def rms(values, gain):
    mean_square = jnp.mean(values * values, axis=-1, keepdims=True)
    return (values * lax.rsqrt(mean_square + 1e-06) * gain).astype(BF16)


def block_at(scal, outer, inner):
    back = scal[6] == 1
    dy, dx = jnp.where(back, inner, outer), jnp.where(back, outer, inner)
    return lax.bitwise_xor(scal[1], dy) * SIDE + lax.bitwise_xor(scal[0], dx)


class Fetched:
    def __init__(self, sources, space, sems):
        self.space = space
        self.copies = []
        for slot, source in enumerate(sources):
            self.copies.append(pltpu.make_async_copy(source, space.at[slot], sems.at[slot]))
            self.copies[-1].start()

    def take(self, slot):
        self.copies[slot].wait()
        return self.space.at[slot]


def put_norm(scal, gains, streams, h3):
    rows = streams[0].shape[0]
    gain = gains[pl.ds(scal[2], 1), :]
    for part, ref in enumerate(streams):
        h = rms(ref[...].astype(F32), gain)
        for i in range(16):
            h3[i, part * rows:(part + 1) * rows, :] = h[:, i * 128:(i + 1) * 128]


def put_memory(mem, m3):
    rows = mem[0].shape[0]
    for part, ref in enumerate(mem):
        for i in range(16):
            m3[i, part * rows:(part + 1) * rows, :] = ref[:, i * 128:(i + 1) * 128]


def project(scal, h3, pieces, which, space, sems):
    keys = [(i, n) for i in range(SIDE) for n in range(len(pieces))]
    low, high = which[0], which[-1] + 1
    fetched = Fetched([pieces[n][i].at[low:high] for i, n in keys], space, sems)

    def run():
        totals = {}
        for slot, (i, n) in enumerate(keys):
            if n == 0:
                h = jnp.concatenate([h3[block_at(scal, TURNS[i], d)] for d in TURNS], axis=1)
            tile = fetched.take(slot)
            for m in which:
                term = dot(h, tile[m - low])
                totals[m, n] = totals[m, n] + term if i else term
        sides = range(len(pieces))
        return [jnp.concatenate([totals[m, n] for n in sides], axis=1).astype(BF16) for m in which]

    return run


def mask(scal, first_limit, second_limit, count):
    rows = count // 2
    r = lax.broadcasted_iota(jnp.int32, (count, count), 0)
    c = lax.broadcasted_iota(jnp.int32, (count, count), 1)
    first = c < rows
    live = (r < rows) == first
    key_at = jnp.where(first, c, c - rows).astype(F32)
    live = live & (key_at < jnp.where(first, first_limit, second_limit))
    return live & ((c <= r) | (scal[3] == 0))


def attend(live, q, k, v):
    mixed = []
    for head in range(q.shape[1] // HEAD_DIM):
        at = slice(head * HEAD_DIM, (head + 1) * HEAD_DIM)
        s = dot_t(q[:, at], k[:, at]) * HEAD_DIM ** (-0.5)
        s = jnp.where(live, s, -1e30)
        e = jnp.exp(s - jnp.max(s, axis=-1, keepdims=True))
        p = (e / jnp.sum(e, axis=-1, keepdims=True)).astype(BF16)
        mixed.append(dot(p, v[:, at]).astype(BF16))
    return jnp.concatenate(mixed, axis=1)


def local_mask(scal, count):
    return mask(scal, scal[4].astype(F32), scal[5].astype(F32), count)


def project_out(scal, mixed, fetched, t3):
    for i, turn in enumerate(TURNS):
        t = dot_t(mixed, fetched.take(i)[...])
        for j, d in enumerate(TURNS):
            t3[block_at(scal, turn, d)] = t[:, j * 128:(j + 1) * 128]


def put_out(t3, first, second, out_mine, out_other):
    for i in range(16):
        at = slice(i * 128, (i + 1) * 128)
        out_mine[:, at] = t3[i, first, :].astype(out_mine.dtype)
        out_other[:, at] = t3[i, second, :].astype(out_other.dtype)


def norm_kernel(scal, gains, own, got0, got2, h3):
    count = own.shape[0]

    def put(part, ref):
        gain = gains[pl.ds(scal[2], 1), :]
        for at in range(0, count, 64):
            h = rms(ref[at:at + 64, :].astype(F32), gain)
            to = part * count + at
            for i in range(16):
                h3[i, to:to + 64, :] = h[:, i * 128:(i + 1) * 128]

    @pl.when(scal[2] == 0)
    def _():
        put(0, own)
        put(1, got0)

    @pl.when(scal[2] == 2)
    def _():
        put(0, own)
        put(1, got2)


def first_kernel(scal, h3, own_keys, got_keys, *refs):
    pieces, (own, sent, space, sems) = refs[:SIDE], refs[SIDE:]

    @pl.when(lax.rem(scal[2], 2) == 0)
    def _():
        q, k, v = project(scal, h3, [pieces], (0, 1, 2), space, sems)()
        count = own.shape[0]
        for part, (keys, out) in enumerate(((own_keys, own), (got_keys, sent))):
            at = slice(part * count, (part + 1) * count)
            live = mask(scal, keys[0:1, :], keys[1:2, :], count)
            out[...] = attend(live, q[at], k[at], v[at])


def first_out_kernel(scal, own, got, *refs):
    pieces, (out_mine, out_other, mixed, t3, space, sems) = refs[:SIDE], refs[SIDE:]

    @pl.when(lax.rem(scal[2], 2) == 0)
    def _():
        fetched = Fetched([ref.at[0] for ref in pieces], space, sems)
        half = own.shape[1]
        side = lax.rem(scal[0], 2)
        mixed[:, pl.ds(pl.multiple_of(side * half, half), half)] = own[...]
        mixed[:, pl.ds(pl.multiple_of((1 - side) * half, half), half)] = got[...]
        project_out(scal, mixed[...], fetched, t3)
        rows = out_mine.shape[0]
        here = pl.ds(pl.multiple_of(scal[6] * rows, rows), rows)
        there = pl.ds(pl.multiple_of((1 - scal[6]) * rows, rows), rows)
        put_out(t3, here, there, out_mine, out_other)


def split(refs):
    return [refs[:SIDE], refs[SIDE:2 * SIDE]], refs[2 * SIDE:3 * SIDE], refs[3 * SIDE:]


def received_kernel(scal, gains, mine, other, h3):
    @pl.when(lax.rem(scal[2], 2) == 1)
    def _():
        put_norm(scal, gains, (mine, other), h3)


def second_kernel(scal, h3, *refs):
    pieces, outs, rest = split(refs)
    out_mine, out_other, query, t3, space, sems, out_space, out_sems = rest

    @pl.when(scal[2] == 1)
    def _():
        run = project(scal, h3, pieces, (0, 1, 2), space, sems)
        fetched = Fetched([ref.at[0] for ref in outs], out_space, out_sems)
        rows = out_mine.shape[0]
        mixed = attend(local_mask(scal, 2 * rows), *run())
        project_out(scal, mixed, fetched, t3)
        put_out(t3, slice(0, rows), slice(rows, 2 * rows), out_mine, out_other)

    @pl.when(scal[2] == 3)
    def _():
        query[...] = project(scal, h3, pieces, (0,), space.at[:, :1], sems)()[0]


def third_kernel(scal, q, mem_mine, mem_other, *refs):
    pieces, outs, (out, m3, t3, space, sems, out_space, out_sems) = split(refs)

    @pl.when(scal[2] == 3)
    def _():
        rows = mem_mine.shape[0]
        run = project(scal, m3, pieces, (1, 2), space, sems)
        fetched = Fetched([ref.at[0] for ref in outs], out_space, out_sems)
        put_memory((mem_mine, mem_other), m3)
        k, v = run()
        mixed = attend(local_mask(scal, 2 * rows), q[...], k, v)
        project_out(scal, mixed, fetched, t3)
        put_out(t3, slice(0, rows), slice(rows, 2 * rows), out.at[:rows], out.at[rows:])


VMEM = pl.BlockSpec(memory_space=pltpu.VMEM)
SMEM = pl.BlockSpec(memory_space=pltpu.SMEM)
ANY = pl.BlockSpec(memory_space=pl.ANY)


def call(kernel, scal, operands, outs, scratch=(), pieces=(), fetches=(), flops=0):
    size = sum(a.size * a.dtype.itemsize for a in [*operands, *pieces])
    shapes = [pltpu.VMEM(shape, kind) for shape, kind in scratch]
    for shape in fetches:
        shapes += [pltpu.VMEM(shape, BF16), pltpu.SemaphoreType.DMA(shape[:1])]
    return pl.pallas_call(
        kernel,
        out_shape=outs,
        in_specs=[SMEM] + [VMEM] * len(operands) + [ANY] * len(pieces),
        out_specs=jax.tree.map(lambda _: VMEM, outs),
        scratch_shapes=shapes,
        compiler_params=pltpu.CompilerParams(vmem_limit_bytes=16 * 1024 * 1024),
        cost_estimate=pl.CostEstimate(flops=flops, bytes_accessed=size, transcendentals=0),
    )(scal, *operands, *pieces)


def finish_kernel(scal, mine, other, hop_m, hop_o, early_m, early_o, own, got, out):
    rows = mine.shape[0]
    cube, core = scal[2], scal[6]
    even = (cube == 0) | (cube == 2)

    def put(doc0, doc1):
        out[0] = doc0[...]
        out[1] = doc1[...]

    @pl.when((core == 0) & even)
    def _():
        put(mine, other)

    @pl.when((core == 0) & jnp.logical_not(even))
    def _():
        put(hop_m, hop_o)

    @pl.when((core == 1) & (cube != 3))
    def _():
        put(early_o, early_m)

    @pl.when((core == 1) & (cube == 3))
    def _():
        at = lax.broadcasted_iota(jnp.int32, mine.shape, 0)
        low, high = slice(0, rows), slice(rows, 2 * rows)
        for slot, base, a, b, live in ((1, hop_m, low, high, scal[7]), (0, hop_o, high, low, scal[8])):
            term = own[a, :].astype(F32) + got[b, :].astype(F32)
            term = jnp.where(at < live, term, 0.0)
            out[slot] = (base[...].astype(F32) + term).astype(BF16)


def turns(array, outer, cubes=range(SIDE)):
    return [array] + [exchange(array, outer, turn, cubes) for turn in TURNS[1:]]


def gather(weights, early, late):
    pair, depth, width = weights.shape[1:]
    halves = weights[0].reshape(pair, depth, 2, width // 2).transpose(2, 0, 1, 3)
    sent = jnp.broadcast_to(halves[:, None], (2, SIDE) + halves.shape[1:])
    sent = sent.reshape((2 * SIDE,) + halves.shape[1:])
    got = lax.all_to_all(sent, ("core", "zl"), 0, 0, tiled=True)
    got, late = lax.optimization_barrier((got, late))
    got = got.reshape(2, SIDE, pair, depth, width // 2).transpose(0, 2, 1, 3, 4)
    got = got.reshape(2 * pair, SIDE * depth, width // 2)
    near = turns(got, False)
    near[1], early = lax.optimization_barrier((near[1], early))
    block = jnp.concatenate(near, axis=1)
    zh, core, x = (lax.axis_index(name) for name in ("zh", "core", "x"))
    side = jnp.where(zh % 2 == 0, x % 2, 0)
    across = jnp.where((zh % 2 == 0) & (core == 1), 1 - side, side)
    half = width // 4

    def columns(at):
        return lax.dynamic_slice(block, (0, 0, at * half), (3,) + block.shape[1:2] + (half,))

    kept, sent = columns(side), columns(across)
    first = [kept, exchange(sent, True, 1), exchange(sent, True, 3), exchange(kept, True, FAR)]
    return first, block[:3, :, half:], block[3:], early, late


def on_device(encoder_embed, decoder_embed, section_weights, norm_gains, input_lengths, target_lengths):
    zh, core = lax.axis_index("zh"), lax.axis_index("core")
    y, x = lax.axis_index("y"), lax.axis_index("x")
    rows = encoder_embed.shape[1]
    encoder = zh < 2
    causal = zh == 2
    key_lengths = jnp.where(causal, target_lengths, input_lengths)
    row_lengths = jnp.where(encoder, input_lengths, target_lengths)
    scal = jnp.stack(
        [
            x,
            y,
            zh,
            causal.astype(jnp.int32),
            key_lengths[core],
            key_lengths[1 - core],
            core,
            row_lengths[core],
            row_lengths[1 - core],
        ]
    ).astype(jnp.int32)
    live = (jnp.arange(rows, dtype=jnp.int32) < row_lengths[core])[:, None]

    source = jnp.where(encoder, encoder_embed, decoder_embed)
    mine, other = source[core], source[1 - core]

    def added(stream, term, alive):
        return stream.astype(F32) + jnp.where(alive, term, 0.0)

    def swapped(array, cubes=range(SIDE)):
        pairs = [(2 * c + i, 2 * c + 1 - i) for c in cubes for i in range(2)]
        return lax.ppermute(array, SECTION, pairs)

    count, width = 2 * rows, mine.shape[1]
    keys = jnp.broadcast_to(key_lengths.astype(F32)[:, None], (2, 128))
    keys = jnp.concatenate([keys, jnp.zeros((6, 128), F32)], axis=0)
    streams = (beside(encoder_embed, (0,)), beside(decoder_embed, (2,)))
    parts_a, rest_b, rest_o, (scal, source, keys_got), (got0, got2) = gather(
        section_weights, (scal, source, beside(keys)), streams
    )
    tile = parts_a[0].shape[1:]
    square = rest_o.shape[1:]
    half = square[1]
    blocks = (16, count, 128)
    work = 2 * count * width * half
    wide = jax.ShapeDtypeStruct((count, width), BF16)
    halves = tuple(jax.ShapeDtypeStruct((rows, width), kind) for kind in (F32, BF16))
    narrow = jax.ShapeDtypeStruct((count, half), BF16)
    quarter = jax.ShapeDtypeStruct((count, half // 2), BF16)
    out_fetch = (SIDE,) + square

    h3 = call(
        norm_kernel,
        scal,
        [norm_gains] + [a.reshape(count, width) for a in (source, got0, got2)],
        jax.ShapeDtypeStruct((16, 2 * count, 128), BF16),
    )
    rest_o, h3 = lax.optimization_barrier((rest_o, h3))
    parts_o = turns(rest_o, True)
    mixed, mixed_sent = call(
        first_kernel,
        scal,
        [h3, keys, keys_got],
        (quarter, quarter),
        (),
        parts_a,
        [(4, 3) + tile],
        3 * work,
    )
    rest_b, mixed = lax.optimization_barrier((rest_b, mixed))
    kept, sent = call(
        first_out_kernel,
        scal,
        [mixed, beside(mixed_sent)],
        halves,
        [((count, half), BF16), (blocks, F32)],
        parts_o,
        [out_fetch],
        work,
    )
    first = added(mine, kept + swapped(sent, (0, 2)).astype(F32), live).astype(BF16)
    pieces = [*parts_a, *turns(rest_b, True, ODD), *parts_o]
    hop = lax.ppermute(first, "zh", [(0, 1), (2, 3)])
    hop_other = swapped(hop, ODD)
    h3 = call(
        received_kernel,
        scal,
        [norm_gains, hop, hop_other],
        jax.ShapeDtypeStruct(blocks, BF16),
        flops=NORM_COST,
    )
    kept, sent, query = call(
        second_kernel,
        scal,
        [h3],
        (*halves, narrow),
        [(blocks, F32)],
        pieces,
        [(8, 3) + tile, out_fetch],
        4 * work,
    )
    second = added(hop, kept + swapped(sent, (1,)).astype(F32), live).astype(BF16)
    memory = rms(second.astype(F32), norm_gains[4:5])
    mem = lax.ppermute(memory, "zh", [(1, 3)])
    early = jnp.where(zh == 1, second, first)
    early_other = lax.ppermute(early, SECTION, [(0, 1), (2, 3), (4, 5)])
    mem_other = swapped(mem, (3,))
    own = call(
        third_kernel,
        scal,
        [query, mem, mem_other],
        wide,
        [(blocks, BF16), (blocks, F32)],
        pieces,
        [(8, 2) + tile, out_fetch],
        3 * work,
    )
    got = lax.ppermute(own, SECTION, [(6, 7)])
    parts = [mine, other, hop, hop_other, early, early_other, own, got]
    out = call(finish_kernel, scal, parts, jax.ShapeDtypeStruct((2, rows, width), BF16))
    return out[None]


def solution(mesh):
    fine = Mesh(mesh.devices.reshape(SIDE, 2, SIDE, SIDE, SIDE), AXES)
    in_specs = (
        P(DP, None, None),
        P(DP, None, None),
        P(SECTION, None, DP, None),
        P(),
        P(DP),
        P(DP),
    )
    out_specs = P(SECTION, DP, None, None)
    return jax.shard_map(
        on_device, mesh=fine, in_specs=in_specs, out_specs=out_specs, check_vma=False
    )
```

```python
import functools
import itertools

import jax
import jax.numpy as jnp
from jax import lax
from jax.experimental import pallas as pl
from jax.experimental.pallas import tpu as pltpu
from jax.sharding import Mesh, PartitionSpec as P

HEAD_DIM = 128
SIDE = 4
TURNS = (0, 1, 3, 2)
FAR = 2
AXES = ("zh", "core", "y", "x", "zl")
DP = ("y", "x", "zl")
SECTION = ("zh", "core")
F32 = jnp.float32
BF16 = jnp.bfloat16


def place(zh, core, y, x, zl):
    return (((zh * 2 + core) * SIDE + y) * SIDE + x) * SIDE + zl


def exchange(array, outer, by):
    pairs = []
    for zh, core, y, x, zl in itertools.product(*map(range, (SIDE, 2, SIDE, SIDE, SIDE))):
        along_y = outer == (core == 0)
        to = (y ^ by, x) if along_y else (y, x ^ by)
        pairs.append((place(zh, core, y, x, zl), place(zh, core, *to, zl)))
    return lax.ppermute(array, AXES, pairs)


def dot(a, b):
    return jnp.dot(a, b, preferred_element_type=F32)


def dot_t(a, b):
    return lax.dot_general(a, b, (((1,), (1,)), ((), ())), preferred_element_type=F32)


def rms(values, gain):
    mean_square = jnp.mean(values * values, axis=-1, keepdims=True)
    return (values * lax.rsqrt(mean_square + 1e-06) * gain).astype(BF16)


def block_at(scal, outer, inner):
    back = scal[6] == 1
    dy, dx = jnp.where(back, inner, outer), jnp.where(back, outer, inner)
    return lax.bitwise_xor(scal[1], dy) * SIDE + lax.bitwise_xor(scal[0], dx)


def weight(pieces, turn, which):
    chunk, at = divmod(which, 2)
    if turn == FAR:
        return pieces[8].at[at] if chunk else pieces[6 + which].at[0]
    return pieces[2 * TURNS.index(turn) + chunk].at[at]


class Fetched:
    def __init__(self, pieces, wanted, space, sems):
        self.space = space
        self.copies = {}
        self.slots = {}
        for slot, key in enumerate(wanted):
            copy = pltpu.make_async_copy(weight(pieces, *key), space.at[slot], sems.at[slot])
            copy.start()
            self.copies[key], self.slots[key] = copy, slot

    def take(self, turn, which):
        self.copies[turn, which].wait()
        return self.space[self.slots[turn, which]]


def wanted(spots, which, out=True):
    keys = [(turn, m) for turn in spots for m in which]
    return keys + [(turn, 3) for turn in TURNS] * out


def put_norm(scal, gains, streams, h3):
    rows = streams[0].shape[0]
    gain = gains[pl.ds(scal[2], 1), :]
    for part, ref in enumerate(streams):
        h = rms(ref[...].astype(F32), gain)
        for i in range(16):
            h3[i, part * rows:(part + 1) * rows, :] = h[:, i * 128:(i + 1) * 128]


def put_memory(mem, m3):
    rows = mem[0].shape[0]
    for part, ref in enumerate(mem):
        for i in range(16):
            m3[i, part * rows:(part + 1) * rows, :] = ref[:, i * 128:(i + 1) * 128]


def project(scal, h3, fetched, turns, which, totals=None):
    totals = [None] * len(which) if totals is None else list(totals)
    for turn in turns:
        h = jnp.concatenate([h3[block_at(scal, turn, d)] for d in TURNS], axis=1)
        for i, m in enumerate(which):
            term = dot(h, fetched.take(turn, m))
            totals[i] = term if totals[i] is None else totals[i] + term
    return totals


def attend(scal, q, k, v):
    q, k, v = q.astype(BF16), k.astype(BF16), v.astype(BF16)
    count = q.shape[0]
    rows = count // 2
    r = lax.broadcasted_iota(jnp.int32, (count, count), 0)
    c = lax.broadcasted_iota(jnp.int32, (count, count), 1)
    first = c < rows
    live = (r < rows) == first
    key_at = jnp.where(first, c, c - rows)
    live = live & (key_at < jnp.where(first, scal[4], scal[5]))
    live = live & ((c <= r) | (scal[3] == 0))
    mixed = []
    for head in range(4):
        at = slice(head * HEAD_DIM, (head + 1) * HEAD_DIM)
        s = dot_t(q[:, at], k[:, at]) * HEAD_DIM ** (-0.5)
        s = jnp.where(live, s, -1e30)
        e = jnp.exp(s - jnp.max(s, axis=-1, keepdims=True))
        p = (e / jnp.sum(e, axis=-1, keepdims=True)).astype(BF16)
        mixed.append(dot(p, v[:, at]).astype(BF16))
    return jnp.concatenate(mixed, axis=1)


def project_out(scal, mixed, fetched, t3, out_mine, out_other):
    rows = out_mine.shape[0]
    for turn in TURNS:
        t = dot_t(mixed, fetched.take(turn, 3))
        for j, d in enumerate(TURNS):
            t3[block_at(scal, turn, d)] = t[:, j * 128:(j + 1) * 128]
    for i in range(16):
        at = slice(i * 128, (i + 1) * 128)
        out_mine[:, at] = t3[i, :rows, :].astype(out_mine.dtype)
        out_other[:, at] = t3[i, rows:, :].astype(out_other.dtype)


EARLY = wanted(TURNS[:3], (0, 1, 2), False)
FIRST = wanted(TURNS[3:], (0, 1, 2))
SECOND = wanted(TURNS, (0, 1, 2))
QUERY = wanted(TURNS, (0,), False)
THIRD = wanted(TURNS, (1, 2))


def early_kernel(scal, gains, mine, other, *refs):
    pieces, (h3, q, k, v, space, sems) = refs[:6], refs[6:]

    @pl.when(lax.rem(scal[2], 2) == 0)
    def _():
        fetched = Fetched(pieces, EARLY, space, sems)
        put_norm(scal, gains, (mine, other), h3)
        q[...], k[...], v[...] = project(scal, h3, fetched, TURNS[:3], (0, 1, 2))


def first_kernel(scal, h3, q, k, v, *refs):
    pieces, (out_mine, out_other, t3, space, sems) = refs[:9], refs[9:]

    @pl.when(lax.rem(scal[2], 2) == 0)
    def _():
        fetched = Fetched(pieces, FIRST, space, sems)
        done = (q[...], k[...], v[...])
        done = project(scal, h3, fetched, TURNS[3:], (0, 1, 2), done)
        project_out(scal, attend(scal, *done), fetched, t3, out_mine, out_other)


def second_kernel(scal, gains, mine, other, *refs):
    pieces, (out_mine, out_other, query, h3, t3, space, sems) = refs[:9], refs[9:]

    @pl.when(scal[2] == 1)
    def _():
        fetched = Fetched(pieces, SECOND, space, sems)
        put_norm(scal, gains, (mine, other), h3)
        done = project(scal, h3, fetched, TURNS, (0, 1, 2))
        project_out(scal, attend(scal, *done), fetched, t3, out_mine, out_other)

    @pl.when(scal[2] == 3)
    def _():
        fetched = Fetched(pieces, QUERY, space, sems)
        put_norm(scal, gains, (mine, other), h3)
        query[...] = project(scal, h3, fetched, TURNS, (0,))[0].astype(BF16)


def third_kernel(scal, q, mem_mine, mem_other, *refs):
    pieces, (out, m3, t3, space, sems) = refs[:9], refs[9:]

    @pl.when(scal[2] == 3)
    def _():
        rows = mem_mine.shape[0]
        fetched = Fetched(pieces, THIRD, space, sems)
        put_memory((mem_mine, mem_other), m3)
        k, v = project(scal, m3, fetched, TURNS, (1, 2))
        mixed = attend(scal, q[...], k, v)
        project_out(scal, mixed, fetched, t3, out.at[:rows], out.at[rows:])


VMEM = pl.BlockSpec(memory_space=pltpu.VMEM)
SMEM = pl.BlockSpec(memory_space=pltpu.SMEM)
ANY = pl.BlockSpec(memory_space=pl.ANY)


def call(kernel, scal, operands, outs, scratch=(), pieces=(), fetches=0, flops=0):
    size = sum(a.size * a.dtype.itemsize for a in [*operands, *pieces])
    shapes = [pltpu.VMEM(shape, kind) for shape, kind in scratch]
    if fetches:
        shapes.append(pltpu.VMEM((fetches,) + pieces[0].shape[1:], BF16))
        shapes.append(pltpu.SemaphoreType.DMA((fetches,)))
    return pl.pallas_call(
        kernel,
        out_shape=outs,
        in_specs=[SMEM] + [VMEM] * len(operands) + [ANY] * len(pieces),
        out_specs=jax.tree.map(lambda _: VMEM, outs),
        scratch_shapes=shapes,
        compiler_params=pltpu.CompilerParams(vmem_limit_bytes=16 * 1024 * 1024),
        cost_estimate=pl.CostEstimate(flops=flops, bytes_accessed=size, transcendentals=0),
    )(scal, *operands, *pieces)


def finish_kernel(scal, mine, other, hop_m, hop_o, early_m, early_o, own, got, out):
    rows = mine.shape[0]
    cube, core = scal[2], scal[6]
    even = (cube == 0) | (cube == 2)

    def put(doc0, doc1):
        out[0] = doc0[...]
        out[1] = doc1[...]

    @pl.when((core == 0) & even)
    def _():
        put(mine, other)

    @pl.when((core == 0) & jnp.logical_not(even))
    def _():
        put(hop_m, hop_o)

    @pl.when((core == 1) & (cube != 3))
    def _():
        put(early_o, early_m)

    @pl.when((core == 1) & (cube == 3))
    def _():
        at = lax.broadcasted_iota(jnp.int32, mine.shape, 0)
        low, high = slice(0, rows), slice(rows, 2 * rows)
        for slot, base, a, b, live in ((1, hop_m, low, high, scal[7]), (0, hop_o, high, low, scal[8])):
            term = own[a, :].astype(F32) + got[b, :].astype(F32)
            term = jnp.where(at < live, term, 0.0)
            out[slot] = (base[...].astype(F32) + term).astype(BF16)


def turns(array, outer):
    return [array] + [exchange(array, outer, turn) for turn in TURNS[1:]]


def gather(weights):
    pair, depth, width = weights.shape[1:]
    halves = weights[0].reshape(pair, depth, 2, width // 2).transpose(2, 0, 1, 3)
    sent = jnp.broadcast_to(halves[:, None], (2, SIDE) + halves.shape[1:])
    sent = sent.reshape((2 * SIDE,) + halves.shape[1:])
    got = lax.all_to_all(sent, ("core", "zl"), 0, 0, tiled=True)
    got = got.reshape(2, SIDE, pair, depth, width // 2).transpose(0, 2, 1, 3, 4)
    got = got.reshape(2 * pair, SIDE * depth, width // 2)
    near = turns(got, False)
    chunks = [jnp.concatenate([a[i:i + pair] for a in near], axis=1) for i in (0, pair)]
    by1 = [exchange(a, True, 1) for a in chunks]
    by3 = [exchange(a, True, 3) for a in chunks]
    across = exchange(chunks[1], True, FAR)
    far = [exchange(by3[0][:1], True, 1), exchange(by1[0][1:], True, 3), across]
    return [*chunks, *by1, *by3], far


def on_device(encoder_embed, decoder_embed, section_weights, norm_gains, input_lengths, target_lengths):
    zh, core = lax.axis_index("zh"), lax.axis_index("core")
    y, x = lax.axis_index("y"), lax.axis_index("x")
    rows = encoder_embed.shape[1]
    encoder = zh < 2
    causal = zh == 2
    key_lengths = jnp.where(causal, target_lengths, input_lengths)
    row_lengths = jnp.where(encoder, input_lengths, target_lengths)
    scal = jnp.stack(
        [
            x,
            y,
            zh,
            causal.astype(jnp.int32),
            key_lengths[core],
            key_lengths[1 - core],
            core,
            row_lengths[core],
            row_lengths[1 - core],
        ]
    ).astype(jnp.int32)
    live = (jnp.arange(rows, dtype=jnp.int32) < row_lengths[core])[:, None]

    near, far = gather(section_weights)
    pieces = near + far
    source = jnp.where(encoder, encoder_embed, decoder_embed)
    mine, other = source[core], source[1 - core]

    def added(stream, term, alive):
        return stream.astype(F32) + jnp.where(alive, term, 0.0)

    def swapped(array, cubes=range(SIDE)):
        pairs = [(2 * c + i, 2 * c + 1 - i) for c in cubes for i in range(2)]
        return lax.ppermute(array, SECTION, pairs)

    count, width = 2 * rows, mine.shape[1]
    half = near[0].shape[-1]
    blocks = (16, count, 128)
    work = 2 * count * width * half
    wide = jax.ShapeDtypeStruct((count, width), BF16)
    halves = tuple(jax.ShapeDtypeStruct((rows, width), kind) for kind in (F32, BF16))
    total = jax.ShapeDtypeStruct((count, half), F32)
    narrow = jax.ShapeDtypeStruct((count, half), BF16)

    started = call(
        early_kernel,
        scal,
        [norm_gains, mine, other],
        (jax.ShapeDtypeStruct(blocks, BF16), total, total, total),
        (),
        near,
        len(EARLY),
        3 * work,
    )
    kept, sent = call(
        first_kernel,
        scal,
        [*started],
        halves,
        [(blocks, F32)],
        pieces,
        len(FIRST),
        2 * work,
    )
    first = added(mine, kept + swapped(sent, (0, 2)).astype(F32), live).astype(BF16)
    hop = lax.ppermute(first, "zh", [(0, 1), (2, 3)])
    hop_other = swapped(hop, (1, 3))
    kept, sent, query = call(
        second_kernel,
        scal,
        [norm_gains, hop, hop_other],
        (*halves, narrow),
        [(blocks, BF16), (blocks, F32)],
        pieces,
        len(SECOND),
        4 * work,
    )
    second = added(hop, kept + swapped(sent, (1,)).astype(F32), live).astype(BF16)
    memory = rms(second.astype(F32), norm_gains[4:5])
    mem = lax.ppermute(memory, "zh", [(1, 3)])
    early = jnp.where(zh == 1, second, first)
    early_other = lax.ppermute(early, SECTION, [(0, 1), (2, 3), (4, 5)])
    mem_other = swapped(mem, (3,))
    own = call(
        third_kernel,
        scal,
        [query, mem, mem_other],
        wide,
        [(blocks, BF16), (blocks, F32)],
        pieces,
        len(THIRD),
        3 * work,
    )
    got = lax.ppermute(own, SECTION, [(6, 7)])
    parts = [mine, other, hop, hop_other, early, early_other, own, got]
    out = call(finish_kernel, scal, parts, jax.ShapeDtypeStruct((2, rows, width), BF16))
    return out[None]


def solution(mesh):
    fine = Mesh(mesh.devices.reshape(SIDE, 2, SIDE, SIDE, SIDE), AXES)
    in_specs = (
        P(DP, None, None),
        P(DP, None, None),
        P(SECTION, None, DP, None),
        P(),
        P(DP),
        P(DP),
    )
    out_specs = P(SECTION, DP, None, None)
    return jax.shard_map(
        on_device, mesh=fine, in_specs=in_specs, out_specs=out_specs, check_vma=False
    )
```

```python
import functools
import itertools

import jax
import jax.numpy as jnp
from jax import lax
from jax.experimental import pallas as pl
from jax.experimental.pallas import tpu as pltpu
from jax.sharding import Mesh, PartitionSpec as P

HEAD_DIM = 128
SIDE = 4
TURNS = (0, 1, 3, 2)
FAR = 2
AXES = ("zh", "core", "y", "x", "zl")
DP = ("y", "x", "zl")
SECTION = ("zh", "core")
F32 = jnp.float32
BF16 = jnp.bfloat16


def place(zh, core, y, x, zl):
    return (((zh * 2 + core) * SIDE + y) * SIDE + x) * SIDE + zl


def exchange(array, outer, by):
    pairs = []
    for zh, core, y, x, zl in itertools.product(*map(range, (SIDE, 2, SIDE, SIDE, SIDE))):
        along_y = outer == (core == 0)
        to = (y ^ by, x) if along_y else (y, x ^ by)
        pairs.append((place(zh, core, y, x, zl), place(zh, core, *to, zl)))
    return lax.ppermute(array, AXES, pairs)


def dot(a, b):
    return jnp.dot(a, b, preferred_element_type=F32)


def dot_t(a, b):
    return lax.dot_general(a, b, (((1,), (1,)), ((), ())), preferred_element_type=F32)


def rms(values, gain):
    mean_square = jnp.mean(values * values, axis=-1, keepdims=True)
    return (values * lax.rsqrt(mean_square + 1e-06) * gain).astype(BF16)


def block_at(scal, outer, inner):
    back = scal[6] == 1
    dy, dx = jnp.where(back, inner, outer), jnp.where(back, outer, inner)
    return lax.bitwise_xor(scal[1], dy) * SIDE + lax.bitwise_xor(scal[0], dx)


def weight(pieces, turn, which):
    return pieces[4 * TURNS.index(turn) + which].at[0]


class Fetched:
    def __init__(self, pieces, wanted, space, sems):
        self.space = space
        self.copies = {}
        self.slots = {}
        for slot, key in enumerate(wanted):
            copy = pltpu.make_async_copy(weight(pieces, *key), space.at[slot], sems.at[slot])
            copy.start()
            self.copies[key], self.slots[key] = copy, slot

    def take(self, turn, which):
        self.copies[turn, which].wait()
        return self.space[self.slots[turn, which]]


def wanted(spots, which, out=True):
    keys = [(turn, m) for turn in spots for m in which]
    return keys + [(turn, 3) for turn in TURNS] * out


def put_norm(scal, gains, streams, h3):
    rows = streams[0].shape[0]
    gain = gains[pl.ds(scal[2], 1), :]
    for part, ref in enumerate(streams):
        h = rms(ref[...].astype(F32), gain)
        for i in range(16):
            h3[i, part * rows:(part + 1) * rows, :] = h[:, i * 128:(i + 1) * 128]


def put_memory(mem, m3):
    rows = mem[0].shape[0]
    for part, ref in enumerate(mem):
        for i in range(16):
            m3[i, part * rows:(part + 1) * rows, :] = ref[:, i * 128:(i + 1) * 128]


def project(scal, h3, fetched, turns, which, totals=None):
    totals = [None] * len(which) if totals is None else list(totals)
    for turn in turns:
        h = jnp.concatenate([h3[block_at(scal, turn, d)] for d in TURNS], axis=1)
        for i, m in enumerate(which):
            term = dot(h, fetched.take(turn, m))
            totals[i] = term if totals[i] is None else totals[i] + term
    return totals


def attend(scal, q, k, v):
    q, k, v = q.astype(BF16), k.astype(BF16), v.astype(BF16)
    count = q.shape[0]
    rows = count // 2
    r = lax.broadcasted_iota(jnp.int32, (count, count), 0)
    c = lax.broadcasted_iota(jnp.int32, (count, count), 1)
    first = c < rows
    live = (r < rows) == first
    key_at = jnp.where(first, c, c - rows)
    live = live & (key_at < jnp.where(first, scal[4], scal[5]))
    live = live & ((c <= r) | (scal[3] == 0))
    mixed = []
    for head in range(4):
        at = slice(head * HEAD_DIM, (head + 1) * HEAD_DIM)
        s = dot_t(q[:, at], k[:, at]) * HEAD_DIM ** (-0.5)
        s = jnp.where(live, s, -1e30)
        e = jnp.exp(s - jnp.max(s, axis=-1, keepdims=True))
        p = (e / jnp.sum(e, axis=-1, keepdims=True)).astype(BF16)
        mixed.append(dot(p, v[:, at]).astype(BF16))
    return jnp.concatenate(mixed, axis=1)


def project_out(scal, mixed, fetched, t3, out_mine, out_other):
    rows = out_mine.shape[0]
    for turn in TURNS:
        t = dot_t(mixed, fetched.take(turn, 3))
        for j, d in enumerate(TURNS):
            t3[block_at(scal, turn, d)] = t[:, j * 128:(j + 1) * 128]
    for i in range(16):
        at = slice(i * 128, (i + 1) * 128)
        out_mine[:, at] = t3[i, :rows, :].astype(out_mine.dtype)
        out_other[:, at] = t3[i, rows:, :].astype(out_other.dtype)


EARLY = wanted(TURNS[:3], (0, 1, 2), False)
FIRST = wanted(TURNS[3:], (0, 1, 2), False)
OUT = wanted((), ())
SECOND = wanted(TURNS, (0, 1, 2))
QUERY = wanted(TURNS, (0,), False)
THIRD = wanted(TURNS, (1, 2))


def early_kernel(scal, gains, mine, other, *refs):
    pieces, (h3, q, k, v, space, sems) = refs[:12], refs[12:]

    @pl.when(lax.rem(scal[2], 2) == 0)
    def _():
        fetched = Fetched(pieces, EARLY, space, sems)
        put_norm(scal, gains, (mine, other), h3)
        q[...], k[...], v[...] = project(scal, h3, fetched, TURNS[:3], (0, 1, 2))


def first_kernel(scal, h3, q, k, v, *refs):
    pieces, (mixed, space, sems) = (None,) * 12 + refs[:3], refs[3:]

    @pl.when(lax.rem(scal[2], 2) == 0)
    def _():
        fetched = Fetched(pieces, FIRST, space, sems)
        done = (q[...], k[...], v[...])
        mixed[...] = attend(scal, *project(scal, h3, fetched, TURNS[3:], (0, 1, 2), done))


def first_out_kernel(scal, mixed, *refs):
    pieces, (out_mine, out_other, t3, space, sems) = refs[:4], refs[4:]

    @pl.when(lax.rem(scal[2], 2) == 0)
    def _():
        spread = [ref for piece in pieces for ref in (None, None, None, piece)]
        fetched = Fetched(spread, OUT, space, sems)
        project_out(scal, mixed[...], fetched, t3, out_mine, out_other)


def second_kernel(scal, gains, mine, other, *refs):
    pieces, (out_mine, out_other, h3, t3, space, sems) = refs[:16], refs[16:]

    @pl.when(scal[2] == 1)
    def _():
        fetched = Fetched(pieces, SECOND, space, sems)
        put_norm(scal, gains, (mine, other), h3)
        done = project(scal, h3, fetched, TURNS, (0, 1, 2))
        project_out(scal, attend(scal, *done), fetched, t3, out_mine, out_other)


def query_kernel(scal, gains, mine, other, *refs):
    pieces, (q, h3, space, sems) = refs[:16], refs[16:]

    @pl.when(scal[2] == 3)
    def _():
        fetched = Fetched(pieces, QUERY, space, sems)
        put_norm(scal, gains, (mine, other), h3)
        q[...] = project(scal, h3, fetched, TURNS, (0,))[0].astype(BF16)


def third_kernel(scal, q, mem_mine, mem_other, *refs):
    pieces, (out, m3, t3, space, sems) = refs[:16], refs[16:]

    @pl.when(scal[2] == 3)
    def _():
        rows = mem_mine.shape[0]
        fetched = Fetched(pieces, THIRD, space, sems)
        put_memory((mem_mine, mem_other), m3)
        k, v = project(scal, m3, fetched, TURNS, (1, 2))
        mixed = attend(scal, q[...], k, v)
        project_out(scal, mixed, fetched, t3, out.at[:rows], out.at[rows:])


VMEM = pl.BlockSpec(memory_space=pltpu.VMEM)
SMEM = pl.BlockSpec(memory_space=pltpu.SMEM)
ANY = pl.BlockSpec(memory_space=pl.ANY)


def call(kernel, scal, operands, outs, scratch=(), pieces=(), fetches=0, flops=0):
    size = sum(a.size * a.dtype.itemsize for a in [*operands, *pieces])
    shapes = [pltpu.VMEM(shape, kind) for shape, kind in scratch]
    if fetches:
        shapes.append(pltpu.VMEM((fetches,) + pieces[0].shape[1:], BF16))
        shapes.append(pltpu.SemaphoreType.DMA((fetches,)))
    return pl.pallas_call(
        kernel,
        out_shape=outs,
        in_specs=[SMEM] + [VMEM] * len(operands) + [ANY] * len(pieces),
        out_specs=jax.tree.map(lambda _: VMEM, outs),
        scratch_shapes=shapes,
        compiler_params=pltpu.CompilerParams(vmem_limit_bytes=16 * 1024 * 1024),
        cost_estimate=pl.CostEstimate(flops=flops, bytes_accessed=size, transcendentals=0),
    )(scal, *operands, *pieces)


def finish_kernel(scal, mine, other, in1m, in1o, in3m, in3o, early_m, early_o, own, got, out):
    rows = mine.shape[0]
    cube, core = scal[2], scal[6]
    even = (cube == 0) | (cube == 2)

    def put(doc0, doc1):
        out[0] = doc0[...]
        out[1] = doc1[...]

    @pl.when((core == 0) & even)
    def _():
        put(mine, other)

    @pl.when((core == 0) & (cube == 1))
    def _():
        put(in1m, in1o)

    @pl.when((core == 0) & (cube == 3))
    def _():
        put(in3m, in3o)

    @pl.when((core == 1) & (cube != 3))
    def _():
        put(early_o, early_m)

    @pl.when((core == 1) & (cube == 3))
    def _():
        at = lax.broadcasted_iota(jnp.int32, mine.shape, 0)
        low, high = slice(0, rows), slice(rows, 2 * rows)
        for slot, base, a, b, live in ((1, in3m, low, high, scal[7]), (0, in3o, high, low, scal[8])):
            term = own[a, :].astype(F32) + got[b, :].astype(F32)
            term = jnp.where(at < live, term, 0.0)
            out[slot] = (base[...].astype(F32) + term).astype(BF16)


def turns(array, outer):
    return [array] + [exchange(array, outer, turn) for turn in TURNS[1:]]


def gather(weights):
    pair, depth, width = weights.shape[1:]
    halves = weights[0].reshape(pair, depth, 2, width // 2).transpose(2, 0, 1, 3)
    sent = jnp.broadcast_to(halves[:, None], (2, SIDE) + halves.shape[1:])
    sent = sent.reshape((2 * SIDE,) + halves.shape[1:])
    got = lax.all_to_all(sent, ("core", "zl"), 0, 0, tiled=True)
    got = got.reshape(2, SIDE, pair, depth, width // 2).transpose(0, 2, 1, 3, 4)
    got = got.reshape(2 * pair, SIDE * depth, width // 2)
    near = turns(got, False)
    parts = [jnp.concatenate([a[i:i + 1] for a in near], axis=1) for i in range(2 * pair)]
    by1 = [exchange(a, True, 1) for a in parts]
    by3 = [exchange(a, True, 3) for a in parts]
    far = [exchange((by1, by3)[i % 2][i], True, (3, 1)[i % 2]) for i in range(2 * pair)]
    return [*parts, *by1, *by3], far


def on_device(encoder_embed, decoder_embed, section_weights, norm_gains, input_lengths, target_lengths):
    zh, core = lax.axis_index("zh"), lax.axis_index("core")
    y, x = lax.axis_index("y"), lax.axis_index("x")
    rows = encoder_embed.shape[1]
    encoder = zh < 2
    causal = zh == 2
    key_lengths = jnp.where(causal, target_lengths, input_lengths)
    row_lengths = jnp.where(encoder, input_lengths, target_lengths)
    scal = jnp.stack(
        [
            x,
            y,
            zh,
            causal.astype(jnp.int32),
            key_lengths[core],
            key_lengths[1 - core],
            core,
            row_lengths[core],
            row_lengths[1 - core],
        ]
    ).astype(jnp.int32)
    live = (jnp.arange(rows, dtype=jnp.int32) < row_lengths[core])[:, None]

    near, far = gather(section_weights)
    pieces = near + far
    source = jnp.where(encoder, encoder_embed, decoder_embed)
    mine, other = source[core], source[1 - core]

    def added(stream, term, alive):
        return stream.astype(F32) + jnp.where(alive, term, 0.0)

    def swapped(array, cubes=range(SIDE)):
        pairs = [(2 * c + i, 2 * c + 1 - i) for c in cubes for i in range(2)]
        return lax.ppermute(array, SECTION, pairs)

    count, width = 2 * rows, mine.shape[1]
    half = near[0].shape[-1]
    blocks = (16, count, 128)
    work = 2 * count * width * half
    wide = jax.ShapeDtypeStruct((count, width), BF16)
    halves = tuple(jax.ShapeDtypeStruct((rows, width), kind) for kind in (F32, BF16))
    total = jax.ShapeDtypeStruct((count, half), F32)
    narrow = jax.ShapeDtypeStruct((count, half), BF16)

    started = call(
        early_kernel,
        scal,
        [norm_gains, mine, other],
        (jax.ShapeDtypeStruct(blocks, BF16), total, total, total),
        (),
        near,
        len(EARLY),
        3 * work,
    )
    mixed = call(
        first_kernel, scal, [*started], narrow, (), far[:3], len(FIRST), work
    )
    kept, sent = call(
        first_out_kernel, scal, [mixed], halves, [(blocks, F32)], pieces[3::4], len(OUT), work
    )
    first = added(mine, kept + swapped(sent, (0, 2)).astype(F32), live).astype(BF16)
    in1 = lax.ppermute(first, "zh", [(0, 1)])
    in3 = lax.ppermute(first, "zh", [(2, 3)])
    in1_other = swapped(in1, (1,))
    kept, sent = call(
        second_kernel,
        scal,
        [norm_gains, in1, in1_other],
        halves,
        [(blocks, BF16), (blocks, F32)],
        pieces,
        len(SECOND),
        4 * work,
    )
    second = added(in1, kept + swapped(sent, (1,)).astype(F32), live).astype(BF16)
    memory = rms(second.astype(F32), norm_gains[4:5])
    mem = lax.ppermute(memory, "zh", [(1, 3)])
    early = jnp.where(zh == 1, second, first)
    early_other = lax.ppermute(early, SECTION, [(0, 1), (2, 3), (4, 5)])
    in3_other = swapped(in3, (3,))
    query = call(
        query_kernel,
        scal,
        [norm_gains, in3, in3_other],
        narrow,
        [(blocks, BF16)],
        pieces,
        len(QUERY),
        work,
    )
    mem_other = swapped(mem, (3,))
    own = call(
        third_kernel,
        scal,
        [query, mem, mem_other],
        wide,
        [(blocks, BF16), (blocks, F32)],
        pieces,
        len(THIRD),
        3 * work,
    )
    got = lax.ppermute(own, SECTION, [(6, 7)])
    parts = [mine, other, in1, in1_other, in3, in3_other, early, early_other, own, got]
    out = call(finish_kernel, scal, parts, jax.ShapeDtypeStruct((2, rows, width), BF16))
    return out[None]


def solution(mesh):
    fine = Mesh(mesh.devices.reshape(SIDE, 2, SIDE, SIDE, SIDE), AXES)
    in_specs = (
        P(DP, None, None),
        P(DP, None, None),
        P(SECTION, None, DP, None),
        P(),
        P(DP),
        P(DP),
    )
    out_specs = P(SECTION, DP, None, None)
    return jax.shard_map(
        on_device, mesh=fine, in_specs=in_specs, out_specs=out_specs, check_vma=False
    )
```

```python
import functools
import itertools

import jax
import jax.numpy as jnp
from jax import lax
from jax.experimental import pallas as pl
from jax.experimental.pallas import tpu as pltpu
from jax.sharding import Mesh, PartitionSpec as P

HEAD_DIM = 128
SIDE = 4
TURNS = (0, 1, 3, 2)
FAR = 2
AXES = ("zh", "core", "y", "x", "zl")
DP = ("y", "x", "zl")
SECTION = ("zh", "core")
F32 = jnp.float32
BF16 = jnp.bfloat16


def place(zh, core, y, x, zl):
    return (((zh * 2 + core) * SIDE + y) * SIDE + x) * SIDE + zl


def exchange(array, outer, by):
    pairs = []
    for zh, core, y, x, zl in itertools.product(*map(range, (SIDE, 2, SIDE, SIDE, SIDE))):
        along_y = outer == (core == 0)
        to = (y ^ by, x) if along_y else (y, x ^ by)
        pairs.append((place(zh, core, y, x, zl), place(zh, core, *to, zl)))
    return lax.ppermute(array, AXES, pairs)


def dot(a, b):
    return jnp.dot(a, b, preferred_element_type=F32)


def dot_t(a, b):
    return lax.dot_general(a, b, (((1,), (1,)), ((), ())), preferred_element_type=F32)


def rms(values, gain):
    mean_square = jnp.mean(values * values, axis=-1, keepdims=True)
    return (values * lax.rsqrt(mean_square + 1e-06) * gain).astype(BF16)


def block_at(scal, outer, inner):
    back = scal[6] == 1
    dy, dx = jnp.where(back, inner, outer), jnp.where(back, outer, inner)
    return lax.bitwise_xor(scal[1], dy) * SIDE + lax.bitwise_xor(scal[0], dx)


def weight(pieces, turn, which):
    return pieces[4 * TURNS.index(turn) + which].at[0]


class Fetched:
    def __init__(self, pieces, wanted, space, sems):
        self.space = space
        self.copies = {}
        self.slots = {}
        for slot, key in enumerate(wanted):
            copy = pltpu.make_async_copy(weight(pieces, *key), space.at[slot], sems.at[slot])
            copy.start()
            self.copies[key], self.slots[key] = copy, slot

    def take(self, turn, which):
        self.copies[turn, which].wait()
        return self.space[self.slots[turn, which]]


def wanted(spots, which, out=True):
    keys = [(turn, m) for turn in spots for m in which]
    return keys + [(turn, 3) for turn in TURNS] * out


def put_norm(scal, gains, streams, h3):
    rows = streams[0].shape[0]
    gain = gains[pl.ds(scal[2], 1), :]
    for part, ref in enumerate(streams):
        h = rms(ref[...].astype(F32), gain)
        for i in range(16):
            h3[i, part * rows:(part + 1) * rows, :] = h[:, i * 128:(i + 1) * 128]


def put_memory(mem, m3):
    rows = mem[0].shape[0]
    for part, ref in enumerate(mem):
        for i in range(16):
            m3[i, part * rows:(part + 1) * rows, :] = ref[:, i * 128:(i + 1) * 128]


def project(scal, h3, fetched, turns, which, totals=None):
    totals = [None] * len(which) if totals is None else list(totals)
    for turn in turns:
        h = jnp.concatenate([h3[block_at(scal, turn, d)] for d in TURNS], axis=1)
        for i, m in enumerate(which):
            term = dot(h, fetched.take(turn, m))
            totals[i] = term if totals[i] is None else totals[i] + term
    return totals


def attend(scal, q, k, v):
    q, k, v = q.astype(BF16), k.astype(BF16), v.astype(BF16)
    count = q.shape[0]
    rows = count // 2
    r = lax.broadcasted_iota(jnp.int32, (count, count), 0)
    c = lax.broadcasted_iota(jnp.int32, (count, count), 1)
    first = c < rows
    live = (r < rows) == first
    key_at = jnp.where(first, c, c - rows)
    live = live & (key_at < jnp.where(first, scal[4], scal[5]))
    live = live & ((c <= r) | (scal[3] == 0))
    mixed = []
    for head in range(4):
        at = slice(head * HEAD_DIM, (head + 1) * HEAD_DIM)
        s = dot_t(q[:, at], k[:, at]) * HEAD_DIM ** (-0.5)
        s = jnp.where(live, s, -1e30)
        e = jnp.exp(s - jnp.max(s, axis=-1, keepdims=True))
        p = (e / jnp.sum(e, axis=-1, keepdims=True)).astype(BF16)
        mixed.append(dot(p, v[:, at]).astype(BF16))
    return jnp.concatenate(mixed, axis=1)


def project_out(scal, mixed, fetched, t3, out_mine, out_other):
    rows = out_mine.shape[0]
    for turn in TURNS:
        t = dot_t(mixed, fetched.take(turn, 3))
        for j, d in enumerate(TURNS):
            t3[block_at(scal, turn, d)] = t[:, j * 128:(j + 1) * 128]
    for i in range(16):
        at = slice(i * 128, (i + 1) * 128)
        out_mine[:, at] = t3[i, :rows, :].astype(out_mine.dtype)
        out_other[:, at] = t3[i, rows:, :].astype(out_other.dtype)


EARLY = wanted(TURNS[:3], (0, 1, 2), False)
FIRST = wanted(TURNS[3:], (0, 1, 2), False)
OUT = wanted((), ())
SECOND = wanted(TURNS, (0, 1, 2))
QUERY = wanted(TURNS, (0,), False)
THIRD = wanted(TURNS, (1, 2))


def early_kernel(scal, gains, mine, other, *refs):
    pieces, (h3, q, k, v, space, sems) = refs[:12], refs[12:]

    @pl.when(lax.rem(scal[2], 2) == 0)
    def _():
        fetched = Fetched(pieces, EARLY, space, sems)
        put_norm(scal, gains, (mine, other), h3)
        q[...], k[...], v[...] = project(scal, h3, fetched, TURNS[:3], (0, 1, 2))


def first_kernel(scal, h3, q, k, v, *refs):
    pieces, (mixed, space, sems) = (None,) * 12 + refs[:3], refs[3:]

    @pl.when(lax.rem(scal[2], 2) == 0)
    def _():
        fetched = Fetched(pieces, FIRST, space, sems)
        done = (q[...], k[...], v[...])
        mixed[...] = attend(scal, *project(scal, h3, fetched, TURNS[3:], (0, 1, 2), done))


def first_out_kernel(scal, mixed, *refs):
    pieces, (out_mine, out_other, t3, space, sems) = refs[:4], refs[4:]

    @pl.when(lax.rem(scal[2], 2) == 0)
    def _():
        spread = [ref for piece in pieces for ref in (None, None, None, piece)]
        fetched = Fetched(spread, OUT, space, sems)
        project_out(scal, mixed[...], fetched, t3, out_mine, out_other)


def second_kernel(scal, gains, mine, other, *refs):
    pieces, (out_mine, out_other, h3, t3, space, sems) = refs[:16], refs[16:]

    @pl.when(scal[2] == 1)
    def _():
        fetched = Fetched(pieces, SECOND, space, sems)
        put_norm(scal, gains, (mine, other), h3)
        done = project(scal, h3, fetched, TURNS, (0, 1, 2))
        project_out(scal, attend(scal, *done), fetched, t3, out_mine, out_other)


def query_kernel(scal, gains, mine, other, *refs):
    pieces, (q, h3, space, sems) = refs[:16], refs[16:]

    @pl.when(scal[2] == 3)
    def _():
        fetched = Fetched(pieces, QUERY, space, sems)
        put_norm(scal, gains, (mine, other), h3)
        q[...] = project(scal, h3, fetched, TURNS, (0,))[0].astype(BF16)


def third_kernel(scal, q, mem_mine, mem_other, *refs):
    pieces, (out, m3, t3, space, sems) = refs[:16], refs[16:]

    @pl.when(scal[2] == 3)
    def _():
        rows = mem_mine.shape[0]
        fetched = Fetched(pieces, THIRD, space, sems)
        put_memory((mem_mine, mem_other), m3)
        k, v = project(scal, m3, fetched, TURNS, (1, 2))
        mixed = attend(scal, q[...], k, v)
        project_out(scal, mixed, fetched, t3, out.at[:rows], out.at[rows:])


VMEM = pl.BlockSpec(memory_space=pltpu.VMEM)
SMEM = pl.BlockSpec(memory_space=pltpu.SMEM)
ANY = pl.BlockSpec(memory_space=pl.ANY)


def call(kernel, scal, operands, outs, scratch=(), pieces=(), fetches=0, flops=0):
    size = sum(a.size * a.dtype.itemsize for a in [*operands, *pieces])
    shapes = [pltpu.VMEM(shape, kind) for shape, kind in scratch]
    if fetches:
        shapes.append(pltpu.VMEM((fetches,) + pieces[0].shape[1:], BF16))
        shapes.append(pltpu.SemaphoreType.DMA((fetches,)))
    return pl.pallas_call(
        kernel,
        out_shape=outs,
        in_specs=[SMEM] + [VMEM] * len(operands) + [ANY] * len(pieces),
        out_specs=jax.tree.map(lambda _: VMEM, outs),
        scratch_shapes=shapes,
        compiler_params=pltpu.CompilerParams(vmem_limit_bytes=16 * 1024 * 1024),
        cost_estimate=pl.CostEstimate(flops=flops, bytes_accessed=size, transcendentals=0),
    )(scal, *operands, *pieces)


def finish_kernel(scal, mine, other, in1m, in1o, in3m, in3o, early_m, early_o, own, got, out):
    rows = mine.shape[0]
    cube, core = scal[2], scal[6]
    even = (cube == 0) | (cube == 2)

    def put(doc0, doc1):
        out[0] = doc0[...]
        out[1] = doc1[...]

    @pl.when((core == 0) & even)
    def _():
        put(mine, other)

    @pl.when((core == 0) & (cube == 1))
    def _():
        put(in1m, in1o)

    @pl.when((core == 0) & (cube == 3))
    def _():
        put(in3m, in3o)

    @pl.when((core == 1) & (cube != 3))
    def _():
        put(early_o, early_m)

    @pl.when((core == 1) & (cube == 3))
    def _():
        at = lax.broadcasted_iota(jnp.int32, mine.shape, 0)
        low, high = slice(0, rows), slice(rows, 2 * rows)
        for slot, base, a, b, live in ((1, in3m, low, high, scal[7]), (0, in3o, high, low, scal[8])):
            term = own[a, :].astype(F32) + got[b, :].astype(F32)
            term = jnp.where(at < live, term, 0.0)
            out[slot] = (base[...].astype(F32) + term).astype(BF16)


def turns(array, outer):
    return [array] + [exchange(array, outer, turn) for turn in TURNS[1:]]


def gather(weights, early):
    pair, depth, width = weights.shape[1:]
    halves = weights[0].reshape(pair, depth, 2, width // 2).transpose(2, 0, 1, 3)
    sent = jnp.broadcast_to(halves[:, None], (2, SIDE) + halves.shape[1:])
    sent = sent.reshape((2 * SIDE,) + halves.shape[1:])
    got = lax.all_to_all(sent, ("core", "zl"), 0, 0, tiled=True)
    got = got.reshape(2, SIDE, pair, depth, width // 2).transpose(0, 2, 1, 3, 4)
    got = got.reshape(2 * pair, SIDE * depth, width // 2)
    near = turns(got, False)
    near[1], early = lax.optimization_barrier((near[1], early))
    parts = [jnp.concatenate([a[i:i + 1] for a in near], axis=1) for i in range(2 * pair)]
    by1 = [exchange(a, True, 1) for a in parts]
    by3 = [exchange(a, True, 3) for a in parts]
    far = [exchange((by1, by3)[i % 2][i], True, (3, 1)[i % 2]) for i in range(2 * pair)]
    return [*parts, *by1, *by3], far, early


def on_device(encoder_embed, decoder_embed, section_weights, norm_gains, input_lengths, target_lengths):
    zh, core = lax.axis_index("zh"), lax.axis_index("core")
    y, x = lax.axis_index("y"), lax.axis_index("x")
    rows = encoder_embed.shape[1]
    encoder = zh < 2
    causal = zh == 2
    key_lengths = jnp.where(causal, target_lengths, input_lengths)
    row_lengths = jnp.where(encoder, input_lengths, target_lengths)
    scal = jnp.stack(
        [
            x,
            y,
            zh,
            causal.astype(jnp.int32),
            key_lengths[core],
            key_lengths[1 - core],
            core,
            row_lengths[core],
            row_lengths[1 - core],
        ]
    ).astype(jnp.int32)
    live = (jnp.arange(rows, dtype=jnp.int32) < row_lengths[core])[:, None]

    source = jnp.where(encoder, encoder_embed, decoder_embed)
    early = (scal, source[core], source[1 - core])
    near, far, (scal, mine, other) = gather(section_weights, early)
    pieces = near + far

    def added(stream, term, alive):
        return stream.astype(F32) + jnp.where(alive, term, 0.0)

    def swapped(array, cubes=range(SIDE)):
        pairs = [(2 * c + i, 2 * c + 1 - i) for c in cubes for i in range(2)]
        return lax.ppermute(array, SECTION, pairs)

    count, width = 2 * rows, mine.shape[1]
    half = near[0].shape[-1]
    blocks = (16, count, 128)
    work = 2 * count * width * half
    wide = jax.ShapeDtypeStruct((count, width), BF16)
    halves = tuple(jax.ShapeDtypeStruct((rows, width), kind) for kind in (F32, BF16))
    total = jax.ShapeDtypeStruct((count, half), F32)
    narrow = jax.ShapeDtypeStruct((count, half), BF16)

    started = call(
        early_kernel,
        scal,
        [norm_gains, mine, other],
        (jax.ShapeDtypeStruct(blocks, BF16), total, total, total),
        (),
        near,
        len(EARLY),
        3 * work,
    )
    mixed = call(
        first_kernel, scal, [*started], narrow, (), far[:3], len(FIRST), work
    )
    kept, sent = call(
        first_out_kernel, scal, [mixed], halves, [(blocks, F32)], pieces[3::4], len(OUT), work
    )
    first = added(mine, kept + swapped(sent, (0, 2)).astype(F32), live).astype(BF16)
    in1 = lax.ppermute(first, "zh", [(0, 1)])
    in3 = lax.ppermute(first, "zh", [(2, 3)])
    in1_other = swapped(in1, (1,))
    kept, sent = call(
        second_kernel,
        scal,
        [norm_gains, in1, in1_other],
        halves,
        [(blocks, BF16), (blocks, F32)],
        pieces,
        len(SECOND),
        4 * work,
    )
    second = added(in1, kept + swapped(sent, (1,)).astype(F32), live).astype(BF16)
    memory = rms(second.astype(F32), norm_gains[4:5])
    mem = lax.ppermute(memory, "zh", [(1, 3)])
    early = jnp.where(zh == 1, second, first)
    early_other = lax.ppermute(early, SECTION, [(0, 1), (2, 3), (4, 5)])
    in3_other = swapped(in3, (3,))
    query = call(
        query_kernel,
        scal,
        [norm_gains, in3, in3_other],
        narrow,
        [(blocks, BF16)],
        pieces,
        len(QUERY),
        work,
    )
    mem_other = swapped(mem, (3,))
    own = call(
        third_kernel,
        scal,
        [query, mem, mem_other],
        wide,
        [(blocks, BF16), (blocks, F32)],
        pieces,
        len(THIRD),
        3 * work,
    )
    got = lax.ppermute(own, SECTION, [(6, 7)])
    parts = [mine, other, in1, in1_other, in3, in3_other, early, early_other, own, got]
    out = call(finish_kernel, scal, parts, jax.ShapeDtypeStruct((2, rows, width), BF16))
    return out[None]


def solution(mesh):
    fine = Mesh(mesh.devices.reshape(SIDE, 2, SIDE, SIDE, SIDE), AXES)
    in_specs = (
        P(DP, None, None),
        P(DP, None, None),
        P(SECTION, None, DP, None),
        P(),
        P(DP),
        P(DP),
    )
    out_specs = P(SECTION, DP, None, None)
    return jax.shard_map(
        on_device, mesh=fine, in_specs=in_specs, out_specs=out_specs, check_vma=False
    )
```

```python
import functools
import itertools

import jax
import jax.numpy as jnp
from jax import lax
from jax.experimental import pallas as pl
from jax.experimental.pallas import tpu as pltpu
from jax.sharding import Mesh, PartitionSpec as P

HEAD_DIM = 128
SIDE = 4
TURNS = (0, 1, 3, 2)
FAR = 2
FIRST_HELD = (1, 3, 5, 6, 7, 8, 9)
QUERY_HELD = (0, 2, 4, 6)
AXES = ("zh", "core", "y", "x", "zl")
DP = ("y", "x", "zl")
SECTION = ("zh", "core")
F32 = jnp.float32
BF16 = jnp.bfloat16


def place(zh, core, y, x, zl):
    return (((zh * 2 + core) * SIDE + y) * SIDE + x) * SIDE + zl


def exchange(array, outer, by):
    pairs = []
    for zh, core, y, x, zl in itertools.product(*map(range, (SIDE, 2, SIDE, SIDE, SIDE))):
        along_y = outer == (core == 0)
        to = (y ^ by, x) if along_y else (y, x ^ by)
        pairs.append((place(zh, core, y, x, zl), place(zh, core, *to, zl)))
    return lax.ppermute(array, AXES, pairs)


def dot(a, b):
    return jnp.dot(a, b, preferred_element_type=F32)


def dot_t(a, b):
    return lax.dot_general(a, b, (((1,), (1,)), ((), ())), preferred_element_type=F32)


def rms(values, gain):
    mean_square = jnp.mean(values * values, axis=-1, keepdims=True)
    return (values * lax.rsqrt(mean_square + 1e-06) * gain).astype(BF16)


def block_at(scal, outer, inner):
    back = scal[6] == 1
    dy, dx = jnp.where(back, inner, outer), jnp.where(back, outer, inner)
    return lax.bitwise_xor(scal[1], dy) * SIDE + lax.bitwise_xor(scal[0], dx)


def weight(pieces, turn, which):
    chunk, place_in = divmod(which, 2)
    if turn == FAR:
        return pieces[6 + which][0]
    return pieces[2 * TURNS.index(turn) + chunk][place_in]


def put_norm(scal, gains, streams, h3):
    rows = streams[0].shape[0]
    gain = gains[pl.ds(scal[2], 1), :]
    for part, ref in enumerate(streams):
        h = rms(ref[...].astype(F32), gain)
        for i in range(16):
            h3[i, part * rows:(part + 1) * rows, :] = h[:, i * 128:(i + 1) * 128]


def put_memory(mem, m3):
    rows = mem[0].shape[0]
    for part, ref in enumerate(mem):
        for i in range(16):
            m3[i, part * rows:(part + 1) * rows, :] = ref[:, i * 128:(i + 1) * 128]


def project(scal, h3, pieces, turns, which, totals=None):
    totals = [None] * len(which) if totals is None else list(totals)
    for turn in turns:
        h = jnp.concatenate([h3[block_at(scal, turn, d)] for d in TURNS], axis=1)
        for i, m in enumerate(which):
            term = dot(h, weight(pieces, turn, m))
            totals[i] = term if totals[i] is None else totals[i] + term
    return totals


def attend(scal, q, k, v):
    q, k, v = q.astype(BF16), k.astype(BF16), v.astype(BF16)
    count = q.shape[0]
    rows = count // 2
    r = lax.broadcasted_iota(jnp.int32, (count, count), 0)
    c = lax.broadcasted_iota(jnp.int32, (count, count), 1)
    first = c < rows
    live = (r < rows) == first
    key_at = jnp.where(first, c, c - rows)
    live = live & (key_at < jnp.where(first, scal[4], scal[5]))
    live = live & ((c <= r) | (scal[3] == 0))
    mixed = []
    for head in range(4):
        at = slice(head * HEAD_DIM, (head + 1) * HEAD_DIM)
        s = dot_t(q[:, at], k[:, at]) * HEAD_DIM ** (-0.5)
        s = jnp.where(live, s, -1e30)
        e = jnp.exp(s - jnp.max(s, axis=-1, keepdims=True))
        p = (e / jnp.sum(e, axis=-1, keepdims=True)).astype(BF16)
        mixed.append(dot(p, v[:, at]).astype(BF16))
    return jnp.concatenate(mixed, axis=1)


def project_out(scal, mixed, pieces, t3, out_mine, out_other):
    rows = out_mine.shape[0]
    for turn in TURNS:
        t = dot_t(mixed, weight(pieces, turn, 3))
        for j, d in enumerate(TURNS):
            t3[block_at(scal, turn, d)] = t[:, j * 128:(j + 1) * 128]
    for i in range(16):
        at = slice(i * 128, (i + 1) * 128)
        out_mine[:, at] = t3[i, :rows, :].astype(out_mine.dtype)
        out_other[:, at] = t3[i, rows:, :].astype(out_other.dtype)


def early_kernel(scal, gains, mine, other, *refs):
    pieces, (h3, q, k, v) = refs[:6], refs[6:]

    @pl.when(lax.rem(scal[2], 2) == 0)
    def _():
        put_norm(scal, gains, (mine, other), h3)
        q[...], k[...], v[...] = project(scal, h3, pieces, TURNS[:3], (0, 1, 2))


def spread(refs, held):
    pieces = [None] * 10
    for at, ref in zip(held, refs):
        pieces[at] = ref
    return pieces


def first_kernel(scal, h3, q, k, v, *refs):
    count = len(FIRST_HELD)
    pieces, (out_mine, out_other, t3) = spread(refs, FIRST_HELD), refs[count:]

    @pl.when(lax.rem(scal[2], 2) == 0)
    def _():
        done = (q[...], k[...], v[...])
        done = project(scal, h3, pieces, TURNS[3:], (0, 1, 2), done)
        project_out(scal, attend(scal, *done), pieces, t3, out_mine, out_other)


def second_kernel(scal, gains, mine, other, *refs):
    pieces, (out_mine, out_other, h3, t3) = refs[:10], refs[10:]

    @pl.when(scal[2] == 1)
    def _():
        put_norm(scal, gains, (mine, other), h3)
        done = project(scal, h3, pieces, TURNS, (0, 1, 2))
        project_out(scal, attend(scal, *done), pieces, t3, out_mine, out_other)


def query_kernel(scal, gains, mine, other, *refs):
    count = len(QUERY_HELD)
    pieces, (q, h3) = spread(refs, QUERY_HELD), refs[count:]

    @pl.when(scal[2] == 3)
    def _():
        put_norm(scal, gains, (mine, other), h3)
        q[...] = project(scal, h3, pieces, TURNS, (0,))[0].astype(BF16)


def third_kernel(scal, q, mem_mine, mem_other, *refs):
    pieces, (out, m3, t3) = refs[:10], refs[10:]

    @pl.when(scal[2] == 3)
    def _():
        rows = mem_mine.shape[0]
        put_memory((mem_mine, mem_other), m3)
        k, v = project(scal, m3, pieces, TURNS, (1, 2))
        mixed = attend(scal, q[...], k, v)
        project_out(scal, mixed, pieces, t3, out.at[:rows], out.at[rows:])


VMEM = pl.BlockSpec(memory_space=pltpu.VMEM)
SMEM = pl.BlockSpec(memory_space=pltpu.SMEM)


def call(kernel, scal, operands, outs, scratch=(), flops=0):
    size = sum(a.size * a.dtype.itemsize for a in operands)
    return pl.pallas_call(
        kernel,
        out_shape=outs,
        in_specs=[SMEM] + [VMEM] * len(operands),
        out_specs=jax.tree.map(lambda _: VMEM, outs),
        scratch_shapes=[pltpu.VMEM(shape, kind) for shape, kind in scratch],
        compiler_params=pltpu.CompilerParams(vmem_limit_bytes=12 * 1024 * 1024),
        cost_estimate=pl.CostEstimate(flops=flops, bytes_accessed=size, transcendentals=0),
    )(scal, *operands)


def finish_kernel(scal, mine, other, in1m, in1o, in3m, in3o, early_m, early_o, own, got, out):
    rows = mine.shape[0]
    cube, core = scal[2], scal[6]
    even = (cube == 0) | (cube == 2)

    def put(doc0, doc1):
        out[0] = doc0[...]
        out[1] = doc1[...]

    @pl.when((core == 0) & even)
    def _():
        put(mine, other)

    @pl.when((core == 0) & (cube == 1))
    def _():
        put(in1m, in1o)

    @pl.when((core == 0) & (cube == 3))
    def _():
        put(in3m, in3o)

    @pl.when((core == 1) & (cube != 3))
    def _():
        put(early_o, early_m)

    @pl.when((core == 1) & (cube == 3))
    def _():
        at = lax.broadcasted_iota(jnp.int32, mine.shape, 0)
        low, high = slice(0, rows), slice(rows, 2 * rows)
        for slot, base, a, b, live in ((1, in3m, low, high, scal[7]), (0, in3o, high, low, scal[8])):
            term = own[a, :].astype(F32) + got[b, :].astype(F32)
            term = jnp.where(at < live, term, 0.0)
            out[slot] = (base[...].astype(F32) + term).astype(BF16)


def turns(array, outer):
    return [array] + [exchange(array, outer, turn) for turn in TURNS[1:]]


def gather(weights):
    pair, depth, width = weights.shape[1:]
    halves = weights[0].reshape(pair, depth, 2, width // 2).transpose(2, 0, 1, 3)
    sent = jnp.broadcast_to(halves[:, None], (2, SIDE) + halves.shape[1:])
    sent = sent.reshape((2 * SIDE,) + halves.shape[1:])
    got = lax.all_to_all(sent, ("core", "zl"), 0, 0, tiled=True)
    got = got.reshape(2, SIDE, pair, depth, width // 2).transpose(0, 2, 1, 3, 4)
    got = got.reshape(2 * pair, SIDE * depth, width // 2)
    near = turns(got, False)
    chunks = [jnp.concatenate([a[i:i + pair] for a in near], axis=1) for i in (0, pair)]
    by1 = [exchange(a, True, 1) for a in chunks]
    by3 = [exchange(a, True, 3) for a in chunks]
    far = []
    for a, b in zip(by1, by3):
        far += [exchange(b[:1], True, 1), exchange(a[1:], True, 3)]
    return [*chunks, *by1, *by3], far


def on_device(encoder_embed, decoder_embed, section_weights, norm_gains, input_lengths, target_lengths):
    zh, core = lax.axis_index("zh"), lax.axis_index("core")
    y, x = lax.axis_index("y"), lax.axis_index("x")
    rows = encoder_embed.shape[1]
    encoder = zh < 2
    causal = zh == 2
    key_lengths = jnp.where(causal, target_lengths, input_lengths)
    row_lengths = jnp.where(encoder, input_lengths, target_lengths)
    scal = jnp.stack(
        [
            x,
            y,
            zh,
            causal.astype(jnp.int32),
            key_lengths[core],
            key_lengths[1 - core],
            core,
            row_lengths[core],
            row_lengths[1 - core],
        ]
    ).astype(jnp.int32)
    live = (jnp.arange(rows, dtype=jnp.int32) < row_lengths[core])[:, None]

    near, far = gather(section_weights)
    pieces = near + far
    source = jnp.where(encoder, encoder_embed, decoder_embed)
    mine, other = source[core], source[1 - core]

    def added(stream, term, alive):
        return stream.astype(F32) + jnp.where(alive, term, 0.0)

    def swapped(array, cubes=range(SIDE)):
        pairs = [(2 * c + i, 2 * c + 1 - i) for c in cubes for i in range(2)]
        return lax.ppermute(array, SECTION, pairs)

    count, width = 2 * rows, mine.shape[1]
    half = near[0].shape[-1]
    blocks = (16, count, 128)
    work = 2 * count * width * half
    wide = jax.ShapeDtypeStruct((count, width), BF16)
    halves = tuple(jax.ShapeDtypeStruct((rows, width), kind) for kind in (F32, BF16))
    total = jax.ShapeDtypeStruct((count, half), F32)
    narrow = jax.ShapeDtypeStruct((count, half), BF16)

    started = call(
        early_kernel,
        scal,
        [norm_gains, mine, other, *near],
        (jax.ShapeDtypeStruct(blocks, BF16), total, total, total),
        (),
        3 * work,
    )
    kept, sent = call(
        first_kernel, scal, [*started, *(pieces[i] for i in FIRST_HELD)], halves, [(blocks, F32)], 2 * work
    )
    first = added(mine, kept + swapped(sent, (0, 2)).astype(F32), live).astype(BF16)
    in1 = lax.ppermute(first, "zh", [(0, 1)])
    in3 = lax.ppermute(first, "zh", [(2, 3)])
    in1_other = swapped(in1, (1,))
    kept, sent = call(
        second_kernel,
        scal,
        [norm_gains, in1, in1_other, *pieces],
        halves,
        [(blocks, BF16), (blocks, F32)],
        4 * work,
    )
    second = added(in1, kept + swapped(sent, (1,)).astype(F32), live).astype(BF16)
    memory = rms(second.astype(F32), norm_gains[4:5])
    mem = lax.ppermute(memory, "zh", [(1, 3)])
    early = jnp.where(zh == 1, second, first)
    early_other = lax.ppermute(early, SECTION, [(0, 1), (2, 3), (4, 5)])
    in3_other = swapped(in3, (3,))
    query = call(
        query_kernel,
        scal,
        [norm_gains, in3, in3_other, *(pieces[i] for i in QUERY_HELD)],
        narrow,
        [(blocks, BF16)],
        work,
    )
    mem_other = swapped(mem, (3,))
    own = call(
        third_kernel,
        scal,
        [query, mem, mem_other, *pieces],
        wide,
        [(blocks, BF16), (blocks, F32)],
        3 * work,
    )
    got = lax.ppermute(own, SECTION, [(6, 7)])
    parts = [mine, other, in1, in1_other, in3, in3_other, early, early_other, own, got]
    out = call(finish_kernel, scal, parts, jax.ShapeDtypeStruct((2, rows, width), BF16))
    return out[None]


def solution(mesh):
    fine = Mesh(mesh.devices.reshape(SIDE, 2, SIDE, SIDE, SIDE), AXES)
    in_specs = (
        P(DP, None, None),
        P(DP, None, None),
        P(SECTION, None, DP, None),
        P(),
        P(DP),
        P(DP),
    )
    out_specs = P(SECTION, DP, None, None)
    return jax.shard_map(
        on_device, mesh=fine, in_specs=in_specs, out_specs=out_specs, check_vma=False
    )
```

```python
import functools
import itertools

import jax
import jax.numpy as jnp
from jax import lax
from jax.experimental import pallas as pl
from jax.experimental.pallas import tpu as pltpu
from jax.sharding import Mesh, PartitionSpec as P

HEAD_DIM = 128
SIDE = 4
TURNS = (0, 1, 3, 2)
FAR = 2
FIRST_HELD = (1, 3, 5, 6, 7, 8, 9)
QUERY_HELD = (0, 2, 4, 6)
THIRD_HELD = (0, 1, 2, 3, 4, 5, 7, 8, 9)
AXES = ("zh", "core", "y", "x", "zl")
DP = ("y", "x", "zl")
SECTION = ("zh", "core")
F32 = jnp.float32
BF16 = jnp.bfloat16


def place(zh, core, y, x, zl):
    return (((zh * 2 + core) * SIDE + y) * SIDE + x) * SIDE + zl


def exchange(array, outer, by):
    pairs = []
    for zh, core, y, x, zl in itertools.product(*map(range, (SIDE, 2, SIDE, SIDE, SIDE))):
        along_y = outer == (core == 0)
        to = (y ^ by, x) if along_y else (y, x ^ by)
        pairs.append((place(zh, core, y, x, zl), place(zh, core, *to, zl)))
    return lax.ppermute(array, AXES, pairs)


def dot(a, b):
    return jnp.dot(a, b, preferred_element_type=F32)


def dot_t(a, b):
    return lax.dot_general(a, b, (((1,), (1,)), ((), ())), preferred_element_type=F32)


def rms(values, gain):
    mean_square = jnp.mean(values * values, axis=-1, keepdims=True)
    return (values * lax.rsqrt(mean_square + 1e-06) * gain).astype(BF16)


def block_at(scal, outer, inner):
    back = scal[6] == 1
    dy, dx = jnp.where(back, inner, outer), jnp.where(back, outer, inner)
    return lax.bitwise_xor(scal[1], dy) * SIDE + lax.bitwise_xor(scal[0], dx)


def weight(pieces, turn, which):
    chunk, place_in = divmod(which, 2)
    if turn == FAR:
        return pieces[6 + which][0]
    return pieces[2 * TURNS.index(turn) + chunk][place_in]


def put_norm(scal, gains, streams, h3):
    rows = streams[0].shape[0]
    gain = gains[pl.ds(scal[2], 1), :]
    for part, ref in enumerate(streams):
        h = rms(ref[...].astype(F32), gain)
        for i in range(16):
            h3[i, part * rows:(part + 1) * rows, :] = h[:, i * 128:(i + 1) * 128]


def put_memory(mem, m3):
    rows = mem[0].shape[0]
    for part, ref in enumerate(mem):
        for i in range(16):
            m3[i, part * rows:(part + 1) * rows, :] = ref[:, i * 128:(i + 1) * 128]


def project(scal, h3, pieces, turns, which, totals=None):
    totals = [None] * len(which) if totals is None else list(totals)
    for turn in turns:
        h = jnp.concatenate([h3[block_at(scal, turn, d)] for d in TURNS], axis=1)
        for i, m in enumerate(which):
            term = dot(h, weight(pieces, turn, m))
            totals[i] = term if totals[i] is None else totals[i] + term
    return totals


def attend(scal, q, k, v):
    q, k, v = q.astype(BF16), k.astype(BF16), v.astype(BF16)
    count = q.shape[0]
    rows = count // 2
    r = lax.broadcasted_iota(jnp.int32, (count, count), 0)
    c = lax.broadcasted_iota(jnp.int32, (count, count), 1)
    first = c < rows
    live = (r < rows) == first
    key_at = jnp.where(first, c, c - rows)
    live = live & (key_at < jnp.where(first, scal[4], scal[5]))
    live = live & ((c <= r) | (scal[3] == 0))
    mixed = []
    for head in range(4):
        at = slice(head * HEAD_DIM, (head + 1) * HEAD_DIM)
        s = dot_t(q[:, at], k[:, at]) * HEAD_DIM ** (-0.5)
        s = jnp.where(live, s, -1e30)
        e = jnp.exp(s - jnp.max(s, axis=-1, keepdims=True))
        p = (e / jnp.sum(e, axis=-1, keepdims=True)).astype(BF16)
        mixed.append(dot(p, v[:, at]).astype(BF16))
    return jnp.concatenate(mixed, axis=1)


def project_out(scal, mixed, pieces, t3, out_mine, out_other):
    rows = out_mine.shape[0]
    for turn in TURNS:
        t = dot_t(mixed, weight(pieces, turn, 3))
        for j, d in enumerate(TURNS):
            t3[block_at(scal, turn, d)] = t[:, j * 128:(j + 1) * 128]
    for i in range(16):
        at = slice(i * 128, (i + 1) * 128)
        out_mine[:, at] = t3[i, :rows, :].astype(out_mine.dtype)
        out_other[:, at] = t3[i, rows:, :].astype(out_other.dtype)


def early_kernel(scal, gains, mine, other, *refs):
    pieces, (h3, q, k, v) = refs[:6], refs[6:]

    @pl.when(lax.rem(scal[2], 2) == 0)
    def _():
        put_norm(scal, gains, (mine, other), h3)
        q[...], k[...], v[...] = project(scal, h3, pieces, TURNS[:3], (0, 1, 2))


def spread(refs, held):
    pieces = [None] * 10
    for at, ref in zip(held, refs):
        pieces[at] = ref
    return pieces


def first_kernel(scal, h3, q, k, v, *refs):
    count = len(FIRST_HELD)
    pieces, (out_mine, out_other, t3) = spread(refs, FIRST_HELD), refs[count:]

    @pl.when(lax.rem(scal[2], 2) == 0)
    def _():
        done = (q[...], k[...], v[...])
        done = project(scal, h3, pieces, TURNS[3:], (0, 1, 2), done)
        project_out(scal, attend(scal, *done), pieces, t3, out_mine, out_other)


def second_kernel(scal, gains, mine, other, *refs):
    pieces, (out_mine, out_other, h3, t3) = refs[:10], refs[10:]

    @pl.when(scal[2] == 1)
    def _():
        put_norm(scal, gains, (mine, other), h3)
        done = project(scal, h3, pieces, TURNS, (0, 1, 2))
        project_out(scal, attend(scal, *done), pieces, t3, out_mine, out_other)


def query_kernel(scal, gains, mine, other, *refs):
    count = len(QUERY_HELD)
    pieces, (q, h3) = spread(refs, QUERY_HELD), refs[count:]

    @pl.when(scal[2] == 3)
    def _():
        put_norm(scal, gains, (mine, other), h3)
        q[...] = project(scal, h3, pieces, TURNS, (0,))[0].astype(BF16)


def third_kernel(scal, q, mem_mine, mem_other, *refs):
    count = len(THIRD_HELD)
    pieces, (out, m3, t3) = spread(refs, THIRD_HELD), refs[count:]

    @pl.when(scal[2] == 3)
    def _():
        rows = mem_mine.shape[0]
        put_memory((mem_mine, mem_other), m3)
        k, v = project(scal, m3, pieces, TURNS, (1, 2))
        mixed = attend(scal, q[...], k, v)
        project_out(scal, mixed, pieces, t3, out.at[:rows], out.at[rows:])


VMEM = pl.BlockSpec(memory_space=pltpu.VMEM)
SMEM = pl.BlockSpec(memory_space=pltpu.SMEM)
ANY = pl.BlockSpec(memory_space=pl.ANY)


def call(kernel, scal, operands, outs, scratch=(), flops=0, passed=(), sems=0):
    size = sum(a.size * a.dtype.itemsize for a in operands)
    return pl.pallas_call(
        kernel,
        out_shape=outs,
        in_specs=[SMEM] + [VMEM] * len(operands) + [ANY] * len(passed),
        out_specs=jax.tree.map(lambda _: VMEM, outs),
        scratch_shapes=[pltpu.VMEM(shape, kind) for shape, kind in scratch]
        + [pltpu.SemaphoreType.DMA((sems,))] * (sems > 0),
        compiler_params=pltpu.CompilerParams(vmem_limit_bytes=12 * 1024 * 1024),
        cost_estimate=pl.CostEstimate(flops=flops, bytes_accessed=size, transcendentals=0),
    )(scal, *operands, *passed)


def finish_kernel(scal, in3m, in3o, own, got, mine, other, in1m, in1o, early_m, early_o, out, sems):
    rows = mine.shape[0]
    cube, core = scal[2], scal[6]
    even = (cube == 0) | (cube == 2)

    def put(doc0, doc1):
        copies = [pltpu.make_async_copy(d, out.at[i], sems.at[i]) for i, d in enumerate((doc0, doc1))]
        for copy in copies:
            copy.start()
        for copy in copies:
            copy.wait()

    @pl.when((core == 0) & even)
    def _():
        put(mine, other)

    @pl.when((core == 0) & (cube == 1))
    def _():
        put(in1m, in1o)

    @pl.when((core == 0) & (cube == 3))
    def _():
        out[0] = in3m[...]
        out[1] = in3o[...]

    @pl.when((core == 1) & (cube != 3))
    def _():
        put(early_o, early_m)

    @pl.when((core == 1) & (cube == 3))
    def _():
        at = lax.broadcasted_iota(jnp.int32, mine.shape, 0)
        low, high = slice(0, rows), slice(rows, 2 * rows)
        for slot, base, a, b, live in ((1, in3m, low, high, scal[7]), (0, in3o, high, low, scal[8])):
            term = own[a, :].astype(F32) + got[b, :].astype(F32)
            term = jnp.where(at < live, term, 0.0)
            out[slot] = (base[...].astype(F32) + term).astype(BF16)


def turns(array, outer):
    return [array] + [exchange(array, outer, turn) for turn in TURNS[1:]]


def gather(weights):
    pair, depth, width = weights.shape[1:]
    halves = weights[0].reshape(pair, depth, 2, width // 2).transpose(2, 0, 1, 3)
    sent = jnp.broadcast_to(halves[:, None], (2, SIDE) + halves.shape[1:])
    sent = sent.reshape((2 * SIDE,) + halves.shape[1:])
    got = lax.all_to_all(sent, ("core", "zl"), 0, 0, tiled=True)
    got = got.reshape(2, SIDE, pair, depth, width // 2).transpose(0, 2, 1, 3, 4)
    got = got.reshape(2 * pair, SIDE * depth, width // 2)
    near = turns(got, False)
    chunks = [jnp.concatenate([a[i:i + pair] for a in near], axis=1) for i in (0, pair)]
    by1 = [exchange(a, True, 1) for a in chunks]
    by3 = [exchange(a, True, 3) for a in chunks]
    far = []
    for a, b in zip(by1, by3):
        far += [exchange(b[:1], True, 1), exchange(a[1:], True, 3)]
    return [*chunks, *by1, *by3], far


def on_device(encoder_embed, decoder_embed, section_weights, norm_gains, input_lengths, target_lengths):
    zh, core = lax.axis_index("zh"), lax.axis_index("core")
    y, x = lax.axis_index("y"), lax.axis_index("x")
    rows = encoder_embed.shape[1]
    encoder = zh < 2
    causal = zh == 2
    key_lengths = jnp.where(causal, target_lengths, input_lengths)
    row_lengths = jnp.where(encoder, input_lengths, target_lengths)
    scal = jnp.stack(
        [
            x,
            y,
            zh,
            causal.astype(jnp.int32),
            key_lengths[core],
            key_lengths[1 - core],
            core,
            row_lengths[core],
            row_lengths[1 - core],
        ]
    ).astype(jnp.int32)
    live = (jnp.arange(rows, dtype=jnp.int32) < row_lengths[core])[:, None]

    near, far = gather(section_weights)
    pieces = near + far
    source = jnp.where(encoder, encoder_embed, decoder_embed)
    mine, other = source[core], source[1 - core]

    def added(stream, term, alive):
        return stream.astype(F32) + jnp.where(alive, term, 0.0)

    def swapped(array, cubes=range(SIDE)):
        pairs = [(2 * c + i, 2 * c + 1 - i) for c in cubes for i in range(2)]
        return lax.ppermute(array, SECTION, pairs)

    count, width = 2 * rows, mine.shape[1]
    half = near[0].shape[-1]
    blocks = (16, count, 128)
    work = 2 * count * width * half
    wide = jax.ShapeDtypeStruct((count, width), BF16)
    halves = tuple(jax.ShapeDtypeStruct((rows, width), kind) for kind in (F32, BF16))
    total = jax.ShapeDtypeStruct((count, half), F32)
    narrow = jax.ShapeDtypeStruct((count, half), BF16)

    started = call(
        early_kernel,
        scal,
        [norm_gains, mine, other, *near],
        (jax.ShapeDtypeStruct(blocks, BF16), total, total, total),
        (),
        3 * work,
    )
    kept, sent = call(
        first_kernel, scal, [*started, *(pieces[i] for i in FIRST_HELD)], halves, [(blocks, F32)], 2 * work
    )
    first = added(mine, kept + swapped(sent, (0, 2)).astype(F32), live).astype(BF16)
    in1 = lax.ppermute(first, "zh", [(0, 1)])
    in3 = lax.ppermute(first, "zh", [(2, 3)])
    in1_other = swapped(in1, (1,))
    kept, sent = call(
        second_kernel,
        scal,
        [norm_gains, in1, in1_other, *pieces],
        halves,
        [(blocks, BF16), (blocks, F32)],
        4 * work,
    )
    second = added(in1, kept + swapped(sent, (1,)).astype(F32), live).astype(BF16)
    memory = rms(second.astype(F32), norm_gains[4:5])
    mem = lax.ppermute(memory, "zh", [(1, 3)])
    early = jnp.where(zh == 1, second, first)
    early_other = lax.ppermute(early, SECTION, [(0, 1), (2, 3), (4, 5)])
    in3_other = swapped(in3, (3,))
    query = call(
        query_kernel,
        scal,
        [norm_gains, in3, in3_other, *(pieces[i] for i in QUERY_HELD)],
        narrow,
        [(blocks, BF16)],
        work,
    )
    mem_other = swapped(mem, (3,))
    own = call(
        third_kernel,
        scal,
        [query, mem, mem_other, *(pieces[i] for i in THIRD_HELD)],
        wide,
        [(blocks, BF16), (blocks, F32)],
        3 * work,
    )
    got = lax.ppermute(own, SECTION, [(6, 7)])
    parts = [in3, in3_other, own, got]
    passed = [mine, other, in1, in1_other, early, early_other]
    whole = jax.ShapeDtypeStruct((2, rows, width), BF16)
    out = call(finish_kernel, scal, parts, whole, passed=passed, sems=2)
    return out[None]


def solution(mesh):
    fine = Mesh(mesh.devices.reshape(SIDE, 2, SIDE, SIDE, SIDE), AXES)
    in_specs = (
        P(DP, None, None),
        P(DP, None, None),
        P(SECTION, None, DP, None),
        P(),
        P(DP),
        P(DP),
    )
    out_specs = P(SECTION, DP, None, None)
    return jax.shard_map(
        on_device, mesh=fine, in_specs=in_specs, out_specs=out_specs, check_vma=False
    )
```
